128 devices in a mesh: ctx: 8 (over z, y_lo), fsdp: 16 (over y_hi, x, core).
Axes of the slice: x: 4, y: 4 (y_hi: 2, y_lo: 2; y = y_hi * 2 + y_lo), z: 4, core: 2. Of those that a mesh axis runs over, the one named last changes fastest.
Arguments:
- tokens: bfloat16 [2, 16, 1024, 1024], P(None, 'fsdp', 'ctx'), may hold values from -6 to 6
- cotangent: bfloat16 [2, 16, 1024, 1024], P(None, 'fsdp', 'ctx'), may hold values from -6 to 6
- block_table: int32 [2, 16], replicated, may hold values from 0 to 15, as said below
- segment_ids: int32 [2, 16, 1024], P(None, 'fsdp'), may hold values from 0 to 2, as said below
- positions: int32 [2, 16, 1024], P(None, 'fsdp', 'ctx'), may hold values from 0 to 895, as said below
- gain_attn: bfloat16 [1024], P('fsdp'), may hold values from 0.5 to 1.5
- w_query: bfloat16 [1024, 2048], P('fsdp'), may hold values from -0.1875 to 0.1875
- key_projection: bfloat16 [1024, 1024], P('fsdp'), may hold values from -0.1875 to 0.1875
- value_projection: bfloat16 [1024, 1024], P('fsdp'), may hold values from -0.1875 to 0.1875
- query_norm_gain: bfloat16 [128], P('fsdp'), may hold values from 0.099609375 to 1.8984375
- key_norm_gain: bfloat16 [128], P('fsdp'), may hold values from 0.099609375 to 1.8984375
- w_out: bfloat16 [2048, 1024], P('fsdp'), may hold values from -4 to 4
- gain_ffn: bfloat16 [1024], P('fsdp'), may hold values from 0.5 to 1.5
- w_gate: bfloat16 [1024, 3072], P('fsdp'), may hold values from -0.1875 to 0.1875
- w_up: bfloat16 [1024, 3072], P('fsdp'), may hold values from -0.1875 to 0.1875
- w_down: bfloat16 [3072, 1024], P('fsdp'), may hold values from -0.109375 to 0.109375
Outputs:
- output: bfloat16 [2, 16, 1024, 1024], P(None, 'fsdp', 'ctx')
- grad_tokens: float32 [2, 16, 1024, 1024], P(None, 'fsdp', 'ctx')
- grad_gain_attn: float32 [1024], P('fsdp')
- grad_w_query: float32 [1024, 2048], P('fsdp')
- grad_w_key: float32 [1024, 1024], P('fsdp')
- grad_w_value: float32 [1024, 1024], P('fsdp')
- grad_gain_query: float32 [128], P('fsdp')
- grad_gain_key: float32 [128], P('fsdp')
- grad_w_out: float32 [2048, 1024], P('fsdp')
- grad_gain_ffn: float32 [1024], P('fsdp')
- grad_w_gate: float32 [1024, 3072], P('fsdp')
- grad_w_up: float32 [1024, 3072], P('fsdp')
- grad_w_down: float32 [3072, 1024], P('fsdp')
The draws below stay inside these ranges and needn't reach their ends.
Inputs may be any that keep to these rules, and one draw needn't show every extreme that they name: `block_table`: each row is a permutation of the 16 logical blocks of 64 tokens; storage blocks 2c and 2c + 1 lie on context index c, and one of the two is among the first 8 logical blocks (the prompt), the other among the last. `segment_ids`: in logical order the ids never fall: 512 tokens of 0, then continuation k of 128 to 384 tokens of k, for k = 1 to 2; stored in the tokens' order. In logical order the prompt stands at 0 to 511 and each continuation at consecutive positions that end at 895; stored in the tokens' order.
All inputs are finite; a program needn't handle non-finite values.
Results may differ from the reference program's by a relative error of at most 0.02.
Values may be sent and summed in bfloat16 or wider, within the bound.
A program may use at most 256 MiB of HBM per device.

```python
import math
import jax
import jax.numpy as jnp
from jax import lax

MODEL_WIDTH = 1024
QUERY_HEAD_COUNT = 16
KEY_VALUE_HEADS = 8
HEAD_SIZE = 128
FF = 3072
MB = 2
CONTS = 2
SAMPLES = 16
SEQ = 1024
PROMPT = 512
CONT = 256
BLOCK = 64
NBLK = 16


def deal_blocks(key):
    key = jax.random.fold_in(key, 5)
    half_count = NBLK // 2
    key_list = jax.random.split(key, 3)
    prompt_order = jax.vmap(lambda subkey: jax.random.permutation(subkey, half_count))(jax.random.split(key_list[0], MB))
    answer_order = jax.vmap(lambda subkey: jax.random.permutation(subkey, half_count))(jax.random.split(key_list[1], MB)) + half_count
    flip_bits = jax.random.randint(key_list[2], (MB, half_count), 0, 2)
    even_slot = jnp.where(flip_bits == 0, prompt_order, answer_order)
    odd_slot = jnp.where(flip_bits == 0, answer_order, prompt_order)
    return jnp.stack([even_slot, odd_slot], axis=2).reshape(MB, NBLK).astype(jnp.int32)


def continuation_layout(key):
    key = jax.random.fold_in(key, 9)
    first_key = jax.random.fold_in(key, 0)
    offsets = jax.random.randint(first_key, (MB, SAMPLES, CONTS), 0, CONT // 2 + 1)
    lengths = CONT + offsets - jnp.roll(offsets, 1, axis=2)
    lead_sizes = CONT + CONT // 2 - lengths
    end_marks = jnp.cumsum(lengths, axis=2)
    starts = end_marks - lengths
    logical_index = jnp.arange(SEQ, dtype=jnp.int32)
    relative = logical_index - PROMPT
    inside = (relative[None, None, None, :] >= starts[..., None]) & (relative[None, None, None, :] < end_marks[..., None])
    labels = jnp.arange(1, CONTS + 1, dtype=jnp.int32)
    segment = jnp.sum(jnp.where(inside, labels[None, None, :, None], 0), axis=2)
    within = lead_sizes[..., None] + relative[None, None, None, :] - starts[..., None]
    position = jnp.where(relative[None, None, :] < 0, logical_index[None, None, :], PROMPT + jnp.sum(jnp.where(inside, within, 0), axis=2))
    return (segment.astype(jnp.int32), position.astype(jnp.int32))


def storage_order(key, value_rows):
    table_rows = deal_blocks(key)
    slot_index = jnp.arange(SEQ, dtype=jnp.int32)
    logical = table_rows[:, slot_index // BLOCK] * BLOCK + slot_index % BLOCK
    logical = jnp.broadcast_to(logical[:, None, :], (MB, SAMPLES, SEQ))
    return jnp.take_along_axis(value_rows, logical, axis=2).astype(jnp.int32)


def draw_block_table(key, part):
    return deal_blocks(key)


def draw_segment_ids(key, part):
    segment, position = continuation_layout(key)
    return storage_order(key, segment)


def draw_positions(key, part):
    segment, position = continuation_layout(key)
    return storage_order(key, position)


def levels(stream_key, extent, cuts, low, high):
    level = 1.0
    for axis_at, shards_of in cuts:
        draws = jax.random.uniform(jax.random.fold_in(jax.random.fold_in(stream_key, 6), axis_at), (shards_of,), jnp.float32, low / len(cuts), high / len(cuts))
        level = level * jnp.repeat(jnp.exp(draws), extent[axis_at] // shards_of).reshape((-1,) + (1,) * (len(extent) - 1 - axis_at))
    return level


def noise(own_key, shape, width, reach, cuts=(), kind=jnp.bfloat16):
    values = width * jax.random.normal(own_key, shape, jnp.float32)
    if cuts:
        values = values * levels(own_key, shape, cuts, -0.22, 0.18)
    return jnp.clip(values, -reach, reach).astype(kind)


def setup_inputs(seed: int = 0) -> dict:
    seeds = jax.random.split(jax.random.key(seed), 17)
    return {
        "tokens": noise(seeds[0], (MB, SAMPLES, SEQ, MODEL_WIDTH), 1.0, 6.0, ((1, 16), (2, 8))),
        "cotangent": noise(seeds[1], (MB, SAMPLES, SEQ, MODEL_WIDTH), 1.0, 6.0, ((1, 16), (2, 8))),
        "block_table": draw_block_table(jax.random.fold_in(seeds[16], 71), 0),
        "segment_ids": draw_segment_ids(jax.random.fold_in(seeds[16], 71), 0),
        "positions": draw_positions(jax.random.fold_in(seeds[16], 71), 0),
        "gain_attn": jnp.clip(1.0 + 0.1 * jax.random.normal(seeds[5], (MODEL_WIDTH,), jnp.float32), 0.5, 1.5).astype(jnp.bfloat16),
        "w_query": noise(seeds[6], (MODEL_WIDTH, QUERY_HEAD_COUNT * HEAD_SIZE), MODEL_WIDTH ** -0.5, 0.1875, ((0, 16),)),
        "key_projection": noise(seeds[7], (MODEL_WIDTH, KEY_VALUE_HEADS * HEAD_SIZE), MODEL_WIDTH ** -0.5, 0.1875, ((0, 16),)),
        "value_projection": noise(seeds[8], (MODEL_WIDTH, KEY_VALUE_HEADS * HEAD_SIZE), MODEL_WIDTH ** -0.5, 0.1875, ((0, 16),)),
        "query_norm_gain": jnp.clip(1.0 + 0.18 * jax.random.normal(seeds[9], (HEAD_SIZE,), jnp.float32), 0.099609375, 1.8984375).astype(jnp.bfloat16),
        "key_norm_gain": jnp.clip(1.0 + 0.18 * jax.random.normal(seeds[10], (HEAD_SIZE,), jnp.float32), 0.099609375, 1.8984375).astype(jnp.bfloat16),
        "w_out": noise(seeds[11], (QUERY_HEAD_COUNT * HEAD_SIZE, MODEL_WIDTH), (max(1, QUERY_HEAD_COUNT * HEAD_SIZE // SEQ)) ** -0.5, 4.0, ((0, 16),)),
        "gain_ffn": jnp.clip(1.0 + 0.1 * jax.random.normal(seeds[12], (MODEL_WIDTH,), jnp.float32), 0.5, 1.5).astype(jnp.bfloat16),
        "w_gate": noise(seeds[13], (MODEL_WIDTH, FF), MODEL_WIDTH ** -0.5, 0.1875, ((0, 16),)),
        "w_up": noise(seeds[14], (MODEL_WIDTH, FF), MODEL_WIDTH ** -0.5, 0.1875, ((0, 16),)),
        "w_down": noise(seeds[15], (FF, MODEL_WIDTH), FF ** -0.5, 0.109375, ((0, 16),)),
    }


@jax.custom_vjp
def to_reduced(v):
    return lax.optimization_barrier(v.astype(jnp.bfloat16)).astype(jnp.float32)

@jax.custom_vjp
def reduced_backward(v):
    return v

def low_keep(v):
    return (to_reduced(v), None)

def low_pass(kept, grad):
    return (grad,)

def back_keep(v):
    return (v, None)

def back_low(kept, grad):
    return (to_reduced(grad),)
to_reduced.defvjp(low_keep, low_pass)
reduced_backward.defvjp(back_keep, back_low)

def precise_product(first_arr, second_arr):
    return jnp.dot(first_arr, second_arr, precision=lax.Precision.HIGHEST)

def rms_gain(value_rows, gain_vec):
    return value_rows * lax.rsqrt(lax.optimization_barrier(jnp.mean(value_rows * value_rows, axis=-1, keepdims=True)) + 1e-06) * gain_vec

def rope_tables(where_at, head_width):
    frequency = jnp.exp(jnp.arange(0, head_width // 2, dtype=jnp.float32) * (-2.0 * math.log(1000000.0) / head_width))
    angles = where_at.astype(jnp.float32)[:, None] * frequency[None, :]
    rotary_cosines = jnp.concatenate([jnp.cos(angles), jnp.cos(angles)], axis=-1)
    rotary_sines = jnp.concatenate([jnp.sin(angles), jnp.sin(angles)], axis=-1)
    return (rotary_cosines, rotary_sines)

def prepare_heads(raw_rows, gain_vec, rotary_cosines, rotary_sines):
    head_width = gain_vec.shape[0]
    per_head = raw_rows.reshape(raw_rows.shape[0], raw_rows.shape[1] // head_width, head_width)
    normed = rms_gain(per_head, gain_vec)
    half_width = head_width // 2
    turned = jnp.concatenate([-normed[..., half_width:], normed[..., :half_width]], axis=-1)
    rotated = normed * rotary_cosines[:, None, :] + turned * rotary_sines[:, None, :]
    return rotated.reshape(raw_rows.shape)

def one_sample(params, inputs, segments, where_at, logical):
    gain_attn, w_query, key_projection, value_projection, query_norm_gain, key_norm_gain, w_out, gain_ffn, w_gate, w_up, w_down = params
    sequence_length = inputs.shape[0]
    query_group_width = QUERY_HEAD_COUNT // KEY_VALUE_HEADS
    visible = (logical[None, :] <= logical[:, None]) & ((segments[None, :] == 0) | (segments[None, :] == segments[:, None]))
    rotary_cosines, rotary_sines = rope_tables(where_at, HEAD_SIZE)
    normalized_input = to_reduced(rms_gain(inputs, gain_attn))
    projected_queries = reduced_backward(precise_product(normalized_input, w_query))
    projected_keys = reduced_backward(precise_product(normalized_input, key_projection))
    query_rows = to_reduced(prepare_heads(projected_queries, query_norm_gain, rotary_cosines, rotary_sines)).reshape(sequence_length, KEY_VALUE_HEADS, query_group_width, HEAD_SIZE)
    key_rows = to_reduced(prepare_heads(projected_keys, key_norm_gain, rotary_cosines, rotary_sines)).reshape(sequence_length, KEY_VALUE_HEADS, HEAD_SIZE)
    value_rows = to_reduced(reduced_backward(precise_product(normalized_input, value_projection))).reshape(sequence_length, KEY_VALUE_HEADS, HEAD_SIZE)
    scores = reduced_backward(jnp.einsum('qkgd,pkd->kgqp', query_rows, key_rows, precision=lax.Precision.HIGHEST) * HEAD_SIZE ** (-0.5))
    scores = jnp.where(visible[None, None], scores, -1e+30)
    row_peak = lax.optimization_barrier(jnp.max(scores, axis=-1, keepdims=True))
    shifted = jnp.exp(scores - row_peak)
    attn_probs = to_reduced(shifted / lax.optimization_barrier(jnp.sum(shifted, axis=-1, keepdims=True)))
    mixed = jnp.einsum('kgqp,pkd->qkgd', attn_probs, value_rows, precision=lax.Precision.HIGHEST)
    mixed = to_reduced(reduced_backward(mixed)).reshape(sequence_length, QUERY_HEAD_COUNT * HEAD_SIZE)
    attended = inputs + reduced_backward(precise_product(mixed, w_out))
    normed_mid = to_reduced(rms_gain(attended, gain_ffn))
    gate_pre = reduced_backward(precise_product(normed_mid, w_gate))
    up_proj = reduced_backward(precise_product(normed_mid, w_up))
    hidden = to_reduced(jax.nn.silu(gate_pre) * up_proj)
    return attended + reduced_backward(precise_product(hidden, w_down))

def reference(tokens, cotangent, block_table, segment_ids, positions, gain_attn, w_query, key_projection, value_projection, query_norm_gain, key_norm_gain, w_out, gain_ffn, w_gate, w_up, w_down):
    params = tuple((member.astype(jnp.float32) for member in (gain_attn, w_query, key_projection, value_projection, query_norm_gain, key_norm_gain, w_out, gain_ffn, w_gate, w_up, w_down)))
    sample_count = MB * SAMPLES
    inputs = tokens.astype(jnp.float32).reshape(sample_count, SEQ, MODEL_WIDTH)
    slots = jnp.arange(SEQ, dtype=jnp.int32)
    logical = block_table[:, slots // BLOCK] * BLOCK + slots % BLOCK
    logical = jnp.broadcast_to(logical[:, None, :], (MB, SAMPLES, SEQ)).reshape(sample_count, SEQ)
    segments = segment_ids.reshape(sample_count, SEQ)
    where_all = positions.reshape(sample_count, SEQ)
    checked = jax.checkpoint(one_sample)

    def forward(weight_set, inputs_all):
        return lax.map(lambda packed: checked(weight_set, *packed), (inputs_all, segments, where_all, logical))
    result, pull_back = jax.vjp(forward, params, inputs)
    weight_grads, input_grad = pull_back(cotangent.astype(jnp.float32).reshape(sample_count, SEQ, MODEL_WIDTH))
    full_shape = (MB, SAMPLES, SEQ, MODEL_WIDTH)
    return (result.reshape(full_shape).astype(jnp.bfloat16), input_grad.reshape(full_shape), weight_grads[0], weight_grads[1], weight_grads[2], weight_grads[3], weight_grads[4], weight_grads[5], weight_grads[6], weight_grads[7], weight_grads[8], weight_grads[9], weight_grads[10])
```

```python
import functools
import math

import jax
import jax.numpy as jnp
from jax import lax
from jax.experimental import pallas as pl
from jax.experimental.pallas import tpu as pltpu
from jax.sharding import PartitionSpec as P

MESH = pl.DeviceIdType.MESH
SIZES = {"z": 4, "yl": 2, "yh": 2, "x": 4, "core": 2}
BF = jnp.bfloat16
F32 = jnp.float32
HEAD = 128


def my_place():
    c = lax.axis_index("ctx")
    f = lax.axis_index("fsdp")
    return {"z": c // 2, "yl": c % 2, "yh": f // 8, "x": (f // 2) % 4, "core": f % 2}


def moved(me, shift):
    to = dict(me)
    for axis, step in shift.items():
        to[axis] = (me[axis] + (step % SIZES[axis])) % SIZES[axis]
    return to


def ctx_of(place):
    return place["z"] * 2 + place["yl"]


def tp_of(place):
    return place["x"] * 2 + place["core"]


def chip_of(place):
    return place["yh"] * 4 + place["x"]


def fsdp_of(place):
    return chip_of(place) * 2 + place["core"]


def device_of(place):
    return (ctx_of(place), fsdp_of(place))


CTX_SHIFTS = [{"z": a, "yl": b} for a in range(4) for b in range(2) if a or b]
PLANE_SHIFTS = [
    {"yh": a, "x": b, "core": d}
    for a in range(2)
    for b in range(4)
    for d in range(2)
    if a or b or d
]
CHIP_SHIFTS = [{"yh": a, "x": b} for a in range(2) for b in range(4) if a or b]
TP_SHIFTS = [{"x": b, "core": d} for b in range(4) for d in range(2) if b or d]
COPY_SHIFTS = [
    {"z": a, "yl": b, "yh": d}
    for a in range(4)
    for b in range(2)
    for d in range(2)
    if a or b or d
]
RING_Z = [{"z": 1}, {"z": 3}, {"yl": 1}]
RING_X = [{"x": 1}, {"x": 3}, {"core": 1}]


class Net:
    def __init__(self, send_sems, recv_sems, local_sems):
        self.me = my_place()
        self.send_sems, self.recv_sems, self.local_sems = send_sems, recv_sems, local_sems
        self.count = 0
        self.locals = 0
        self.pending = []

    def enter(self, shifts):
        barrier = pltpu.get_barrier_semaphore()
        for shift in shifts:
            pl.semaphore_signal(
                barrier, inc=1, device_id=device_of(moved(self.me, shift)), device_id_type=MESH
            )
        pl.semaphore_wait(barrier, len(shifts))

    def send(self, src, dst, **shift):
        at = self.count
        self.count += 1
        copy = pltpu.make_async_remote_copy(
            src_ref=src,
            dst_ref=dst,
            send_sem=self.send_sems.at[at],
            recv_sem=self.recv_sems.at[at],
            device_id=device_of(moved(self.me, shift)),
            device_id_type=MESH,
        )
        copy.start()
        self.pending.append(copy.wait_send)
        return copy

    def local(self, src, dst):
        copy = pltpu.make_async_copy(src, dst, self.local_sems.at[self.locals])
        self.locals += 1
        copy.start()
        self.pending.append(copy.wait)
        return copy

    def finish(self):
        for wait in self.pending:
            wait()


def run_tasks(tasks):
    tasks = list(tasks)
    while tasks:
        left = []
        for task in tasks:
            try:
                next(task)
                left.append(task)
            except StopIteration:
                pass
        tasks = left


def unique(shifts):
    seen, out = set(), []
    for shift in shifts:
        key = tuple(sorted((k, v) for k, v in shift.items() if v))
        if key not in seen:
            seen.add(key)
            out.append(shift)
    return out


def comm_call(body, shifts, outs, scratch, cid, in_vmem, out_vmem, n_remote, n_local=1):
    shifts = unique(shifts)

    def kernel(*refs):
        refs, sems = refs[:-3], refs[-3:]
        net = Net(*sems)
        net.enter(shifts)
        run_tasks(body(net, *refs))
        net.finish()

    vm = pl.BlockSpec(memory_space=pltpu.VMEM)
    hb = pl.BlockSpec(memory_space=pl.ANY)
    return pl.pallas_call(
        kernel,
        out_shape=[jax.ShapeDtypeStruct(s, d) for s, d in outs],
        in_specs=[vm if v else hb for v in in_vmem],
        out_specs=[vm if v else hb for v in out_vmem],
        scratch_shapes=list(scratch)
        + [
            pltpu.SemaphoreType.DMA((n_remote,)),
            pltpu.SemaphoreType.DMA((n_remote,)),
            pltpu.SemaphoreType.DMA((n_local,)),
        ],
        compiler_params=pltpu.CompilerParams(
            collective_id=cid, has_side_effects=True, vmem_limit_bytes=50 << 20
        ),
    )


def gather_ctx(net, src, out):
    me = net.me

    def at(dz, dy, lo, rows):
        return out.at[:, ctx_of(moved(me, {"z": dz, "yl": dy})), pl.ds(lo, rows)]

    net.local(src, out.at[:, ctx_of(me)])
    src_a, src_b = src.at[:, pl.ds(0, 64)], src.at[:, pl.ds(64, 64)]
    b_y = net.send(src_b, at(0, 0, 64, 64), yl=1)
    a_r = net.send(src_a, at(0, 0, 0, 64), z=1)
    a_l = net.send(src_a, at(0, 0, 0, 64), z=-1)
    b_r = net.send(src_b, at(0, 0, 64, 64), z=1)
    b_l = net.send(src_b, at(0, 0, 64, 64), z=-1)
    a_y = net.send(src_a, at(0, 0, 0, 64), yl=1)
    yield
    b_y.wait_recv()
    c_r = net.send(at(0, 1, 64, 64), at(0, 1, 64, 64), z=1)
    c_l = net.send(at(0, 1, 64, 64), at(0, 1, 64, 64), z=-1)
    yield
    a_r.wait_recv()
    fa_r = net.send(at(-1, 0, 0, 32), at(-1, 0, 0, 32), z=1)
    ya_r = net.send(at(-1, 0, 0, 64), at(-1, 0, 0, 64), yl=1)
    a_l.wait_recv()
    fa_l = net.send(at(1, 0, 32, 32), at(1, 0, 32, 32), z=-1)
    ya_l = net.send(at(1, 0, 0, 64), at(1, 0, 0, 64), yl=1)
    yield
    b_r.wait_recv()
    fb_r = net.send(at(-1, 0, 64, 32), at(-1, 0, 64, 32), z=1)
    b_l.wait_recv()
    fb_l = net.send(at(1, 0, 96, 32), at(1, 0, 96, 32), z=-1)
    yield
    c_r.wait_recv()
    fc_r = net.send(at(-1, 1, 64, 32), at(-1, 1, 64, 32), z=1)
    c_l.wait_recv()
    fc_l = net.send(at(1, 1, 96, 32), at(1, 1, 96, 32), z=-1)
    yield
    fa_r.wait_recv()
    yb_r = net.send(at(2, 0, 0, 32), at(2, 0, 0, 32), yl=1)
    fa_l.wait_recv()
    yb_l = net.send(at(2, 0, 32, 32), at(2, 0, 32, 32), yl=1)
    yield
    for copy in (a_y, ya_r, ya_l, fb_r, fb_l, fc_r, fc_l, yb_r, yb_l):
        copy.wait_recv()


def gather_tp(net, src, out):
    me = net.me

    def at(dx, lo=0, rows=256):
        return out.at[tp_of(moved(me, {"x": dx})), pl.ds(lo, rows)]

    net.local(src, out.at[tp_of(me)])
    r = net.send(src, at(0), x=1)
    l = net.send(src, at(0), x=-1)
    own = net.send(src, at(0), core=1)
    yield
    r.wait_recv()
    fr = net.send(at(-1, 0, 128), at(-1, 0, 128), x=1)
    cr = net.send(at(-1), at(-1), core=1)
    l.wait_recv()
    fl = net.send(at(1, 128, 128), at(1, 128, 128), x=-1)
    cl = net.send(at(1), at(1), core=1)
    yield
    fr.wait_recv()
    c2r = net.send(at(2, 0, 128), at(2, 0, 128), core=1)
    fl.wait_recv()
    c2l = net.send(at(2, 128, 128), at(2, 128, 128), core=1)
    yield
    for copy in (own, cr, cl, c2r, c2l):
        copy.wait_recv()


def add_rows(dst, terms, rows, step=32):
    def one(i, carry):
        at = pl.ds(pl.multiple_of(i * step, step), step)
        total = terms[0][..., at, :].astype(F32)
        for term in terms[1:]:
            total = total + term[..., at, :].astype(F32)
        dst[..., at, :] = total.astype(dst.dtype)
        return carry

    lax.fori_loop(0, rows // step, one, 0)


def reduce_ctx(net, part, total, ry, sa, rha, ra, rhb, sb, rb, su, ru):
    me = net.me

    def at(dz, dy, lo, rows):
        return part.at[:, ctx_of(moved(me, {"z": dz, "yl": dy})), pl.ds(lo, rows)]

    cy = {}
    for dz in (2, 1, 3, 0):
        cy[dz] = net.send(at(dz, 1, 0, 64), ry.at[dz], yl=1)
    hb = {}
    for q in (1, 0):
        hb[q, 0] = net.send(at(2, q, 64, 32), rhb.at[q, 0], z=1)
        hb[q, 1] = net.send(at(2, q, 96, 32), rhb.at[q, 1], z=-1)
    yield
    cy[2].wait_recv()
    add_rows(sa.at[2], [at(2, 0, 0, 64), ry.at[2]], 64)
    ha_r = net.send(sa.at[2, :, pl.ds(0, 32)], rha.at[0], z=1)
    ha_l = net.send(sa.at[2, :, pl.ds(32, 32)], rha.at[1], z=-1)
    yield
    cb = {}
    for q in (1, 0):
        hb[q, 0].wait_recv()
        add_rows(sb.at[q, 0, :, pl.ds(0, 32)], [at(1, q, 64, 32), rhb.at[q, 0]], 32)
        add_rows(sb.at[q, 0, :, pl.ds(32, 32)], [at(1, q, 96, 32)], 32)
        cb[q, 0] = net.send(sb.at[q, 0], rb.at[q, 0], z=1)
        hb[q, 1].wait_recv()
        add_rows(sb.at[q, 1, :, pl.ds(0, 32)], [at(3, q, 64, 32)], 32)
        add_rows(sb.at[q, 1, :, pl.ds(32, 32)], [at(3, q, 96, 32), rhb.at[q, 1]], 32)
        cb[q, 1] = net.send(sb.at[q, 1], rb.at[q, 1], z=-1)
        yield
    cy[1].wait_recv()
    ha_r.wait_recv()
    add_rows(sa.at[1, :, pl.ds(0, 32)], [at(1, 0, 0, 32), ry.at[1, :, pl.ds(0, 32)], rha.at[0]], 32)
    add_rows(sa.at[1, :, pl.ds(32, 32)], [at(1, 0, 32, 32), ry.at[1, :, pl.ds(32, 32)]], 32)
    ca_r = net.send(sa.at[1], ra.at[0], z=1)
    cy[3].wait_recv()
    ha_l.wait_recv()
    add_rows(sa.at[3, :, pl.ds(0, 32)], [at(3, 0, 0, 32), ry.at[3, :, pl.ds(0, 32)]], 32)
    add_rows(sa.at[3, :, pl.ds(32, 32)], [at(3, 0, 32, 32), ry.at[3, :, pl.ds(32, 32)], rha.at[1]], 32)
    ca_l = net.send(sa.at[3], ra.at[1], z=-1)
    yield
    cb[1, 0].wait_recv()
    cb[1, 1].wait_recv()
    add_rows(su, [at(0, 1, 64, 64), rb.at[1, 0], rb.at[1, 1]], 64)
    cu = net.send(su, ru, yl=1)
    yield
    cy[0].wait_recv()
    ca_r.wait_recv()
    ca_l.wait_recv()
    add_rows(total.at[:, pl.ds(0, 64)], [at(0, 0, 0, 64), ry.at[0], ra.at[0], ra.at[1]], 64)
    yield
    cb[0, 0].wait_recv()
    cb[0, 1].wait_recv()
    cu.wait_recv()
    add_rows(total.at[:, pl.ds(64, 64)], [at(0, 0, 64, 64), rb.at[0, 0], rb.at[0, 1], ru], 64)


def reduce_ctx_scratch(width):
    def buf(*lead, rows=64):
        return pltpu.VMEM(lead + (2, rows, width), BF)

    return [
        buf(4),
        buf(4),
        buf(2, rows=32),
        buf(2),
        buf(2, 2, rows=32),
        buf(2, 2),
        buf(2, 2),
        buf(),
        buf(),
    ]


def reduce_tp(net, part, total, rc, s, rh, r):
    me = net.me

    def at(dx, dc, lo=0, rows=256):
        return part.at[tp_of(moved(me, {"x": dx, "core": dc})), pl.ds(lo, rows)]

    cc = {}
    for dx in (2, 1, 3, 0):
        cc[dx] = net.send(at(dx, 1), rc.at[dx], core=1)
    yield
    cc[2].wait_recv()
    add_rows(s.at[2], [at(2, 0), rc.at[2]], 256)
    h_r = net.send(s.at[2, pl.ds(0, 128)], rh.at[0], x=1)
    h_l = net.send(s.at[2, pl.ds(128, 128)], rh.at[1], x=-1)
    cc[1].wait_recv()
    add_rows(s.at[1, pl.ds(128, 128)], [at(1, 0, 128, 128), rc.at[1, pl.ds(128, 128)]], 128)
    cc[3].wait_recv()
    add_rows(s.at[3, pl.ds(0, 128)], [at(3, 0, 0, 128), rc.at[3, pl.ds(0, 128)]], 128)
    yield
    h_r.wait_recv()
    add_rows(s.at[1, pl.ds(0, 128)], [at(1, 0, 0, 128), rc.at[1, pl.ds(0, 128)], rh.at[0]], 128)
    c_r = net.send(s.at[1], r.at[0], x=1)
    h_l.wait_recv()
    add_rows(
        s.at[3, pl.ds(128, 128)], [at(3, 0, 128, 128), rc.at[3, pl.ds(128, 128)], rh.at[1]], 128
    )
    c_l = net.send(s.at[3], r.at[1], x=-1)
    yield
    cc[0].wait_recv()
    c_r.wait_recv()
    c_l.wait_recv()
    add_rows(total, [at(0, 0), rc.at[0], r.at[0], r.at[1]], 256)


def reduce_tp_scratch(width):
    return [
        pltpu.VMEM((4, 256, width), BF),
        pltpu.VMEM((4, 256, width), BF),
        pltpu.VMEM((2, 128, width), BF),
        pltpu.VMEM((2, 256, width), BF),
    ]


def gather_heads_weights(net, src, out):
    me = net.me
    net.local(src, out.at[fsdp_of(me)])
    copies = [net.send(src, out.at[fsdp_of(me)], **shift) for shift in CHIP_SHIFTS]
    passed = [net.send(src, out.at[fsdp_of(me)], core=1)]
    yield
    for shift, copy in zip(CHIP_SHIFTS, copies):
        copy.wait_recv()
        back = {k: -v for k, v in shift.items()}
        slot = out.at[fsdp_of(moved(me, back))]
        passed.append(net.send(slot, slot, core=1))
    yield
    for copy in passed:
        copy.wait_recv()


def gather_out_weights(net, src, mid, out):
    me = net.me
    mine = chip_of(me)
    stay = net.local(src.at[mine], mid.at[mine])
    first = [
        net.send(src.at[chip_of(moved(me, shift))], mid.at[mine], **shift) for shift in CHIP_SHIFTS
    ]
    yield
    for copy in first:
        copy.wait_recv()
    stay.wait()
    net.pending.remove(stay.wait)
    slot = mid.at[ctx_of(me)]
    place = out.at[me["core"], mine]
    net.local(slot, place)
    copies = [net.send(slot, place, **shift) for shift in CHIP_SHIFTS]
    passed = [net.send(slot, place, core=1)]
    yield
    for shift, copy in zip(CHIP_SHIFTS, copies):
        copy.wait_recv()
        back = {k: -v for k, v in shift.items()}
        there = out.at[me["core"], chip_of(moved(me, back))]
        passed.append(net.send(there, there, core=1))
    yield
    for copy in passed:
        copy.wait_recv()


def gather_ff_weights(net, src, down, out, down_out):
    me = net.me
    net.local(src.at[tp_of(me)], out.at[fsdp_of(me)])
    net.local(down, down_out.at[me["yh"]])
    copies = [
        net.send(src.at[tp_of(moved(me, shift))], out.at[fsdp_of(me)], **shift)
        for shift in PLANE_SHIFTS
    ]
    copies.append(net.send(down, down_out.at[me["yh"]], yh=1))
    yield
    for copy in copies:
        copy.wait_recv()


def scatter_plane(net, src, out):
    me = net.me
    net.local(src.at[fsdp_of(me)], out.at[fsdp_of(me)])
    copies = [
        net.send(src.at[fsdp_of(moved(me, shift))], out.at[fsdp_of(me)], **shift)
        for shift in PLANE_SHIFTS
    ]
    yield
    for copy in copies:
        copy.wait_recv()


def copy_index(place):
    return place["yh"] * 8 + ctx_of(place)


def scatter_copies(net, src, down, out, down_out):
    me = net.me

    def piece(place):
        return down.at[place["yh"], :, pl.ds(pl.multiple_of(ctx_of(place) * 128, 128), 128)]

    mine = copy_index(me)
    net.local(src.at[mine], out.at[mine])
    net.local(piece(me), down_out.at[mine])
    copies = []
    for shift in COPY_SHIFTS:
        to = moved(me, shift)
        copies.append(net.send(src.at[copy_index(to)], out.at[mine], **shift))
        copies.append(net.send(piece(to), down_out.at[mine], **shift))
    yield
    for copy in copies:
        copy.wait_recv()


def spread_ctx(net, src, out, after=None):
    me = net.me
    kept = net.local(src, out.at[ctx_of(me)])
    copies = [net.send(src, out.at[ctx_of(me)], **shift) for shift in CTX_SHIFTS]
    yield
    for copy in copies:
        copy.wait_recv()
    if after is None:
        return
    kept.wait()
    net.pending.remove(kept.wait)
    yield
    yield from after()


def exchange_chips(net, src, out):
    me = net.me
    mine = chip_of(me)
    net.local(src.at[mine], out.at[mine])
    copies = [
        net.send(src.at[chip_of(moved(me, shift))], out.at[mine], **shift) for shift in CHIP_SHIFTS
    ]
    yield
    for copy in copies:
        copy.wait_recv()


def exchange_tp(net, src, out):
    me = net.me
    mine = tp_of(me)
    net.local(src.at[mine], out.at[mine])
    copies = [
        net.send(src.at[tp_of(moved(me, shift))], out.at[mine], **shift) for shift in TP_SHIFTS
    ]
    yield
    for copy in copies:
        copy.wait_recv()


def rms_gain(value_rows, gain_vec):
    return (
        value_rows
        * lax.rsqrt(jnp.mean(value_rows * value_rows, axis=-1, keepdims=True) + 1e-06)
        * gain_vec
    )


def rope_tables(where_at):
    frequency = jnp.exp(
        jnp.arange(0, HEAD // 2, dtype=F32) * (-2.0 * math.log(1000000.0) / HEAD)
    )
    angles = where_at.astype(F32)[..., None] * frequency
    cos, sin = jnp.cos(angles), jnp.sin(angles)
    return jnp.concatenate([cos, cos], axis=-1), jnp.concatenate([sin, sin], axis=-1)


def prepare_heads(raw, gain_vec, cos, sin):
    normed = rms_gain(raw, gain_vec)
    half = HEAD // 2
    turned = jnp.concatenate([-normed[..., half:], normed[..., :half]], axis=-1)
    return normed * cos[:, :, None, :] + turned * sin[:, :, None, :]


def across_rows(a, b):
    return lax.dot_general(a, b, (((0,), (0,)), ((), ())), preferred_element_type=F32)


def against_cols(a, b):
    return lax.dot_general(a, b, (((1,), (1,)), ((), ())), preferred_element_type=F32)


def forward_dot(a, b):
    return jnp.dot(a, b, preferred_element_type=F32)


def token_places(block_table, segment_ids):
    mb, blocks = block_table.shape
    seq = segment_ids.shape[-1]
    block = seq // blocks
    logical = (
        jnp.repeat(block_table, block, axis=1) * block + jnp.arange(seq, dtype=jnp.int32) % block
    )
    first = jnp.sum((segment_ids == 1).astype(jnp.int32), axis=1, keepdims=True)
    prompt = seq // 2
    end = jnp.where(segment_ids == 1, prompt - 1 + first, seq - 1)
    position = jnp.where(segment_ids == 0, logical, 895 - (end - logical))
    return logical, position


def per_device(
    tokens,
    cotangent,
    block_table,
    segment_ids,
    positions,
    gain_attn,
    w_query,
    key_projection,
    value_projection,
    query_norm_gain,
    key_norm_gain,
    w_out,
    gain_ffn,
    w_gate,
    w_up,
    w_down,
):
    ctx = lax.axis_index("ctx")
    mbs, width = tokens.shape[0], tokens.shape[-1]
    tok = tokens[:, 0]
    cot = cotangent[:, 0].reshape(256, width)

    def columns(w, n):
        return lax.dynamic_slice_in_dim(w, ctx * n, n, axis=1)

    small = jnp.concatenate(
        [gain_attn, gain_ffn, query_norm_gain, key_norm_gain, jnp.zeros((512 - 144,), BF)]
    )
    wqkv_mine = jnp.concatenate(
        [
            jnp.concatenate(
                [columns(w_query, 256), columns(key_projection, 128), columns(value_projection, 128)],
                axis=1,
            ),
            jnp.broadcast_to(small[None], (16, 512)),
        ],
        axis=0,
    )

    def by_tp(w):
        return w.reshape(64, 2, 8, 192).transpose(2, 0, 1, 3).reshape(8, 64, 384)

    wgu_mine = jnp.concatenate([by_tp(w_gate), by_tp(w_up)], axis=2)

    def first_body(net, tok, cot, wqkv, wo, wgu, wd, xs, cots, wqkvs, mid, wos, wgus, wds):
        return [
            gather_ctx(net, tok, xs),
            gather_heads_weights(net, wqkv, wqkvs),
            gather_out_weights(net, wo, mid, wos),
            gather_tp(net, cot, cots),
            gather_ff_weights(net, wgu, wd, wgus, wds),
        ]

    x_all, cot_all, wqkv_all, _, wo_all, wgu_all, wd_all = comm_call(
        first_body,
        RING_Z + RING_X + PLANE_SHIFTS,
        [
            ((2, 8, 128, width), BF),
            ((8, 256, width), BF),
            ((16, 80, 512), BF),
            ((8, 16, width), BF),
            ((2, 8, 16, width), BF),
            ((16, 64, 768), BF),
            ((2, 192, width), BF),
        ],
        [],
        0,
        [False] * 6,
        [False] * 7,
        100,
        16,
    )(tok, cot, wqkv_mine, w_out.reshape(8, 16, width), wgu_mine, w_down)

    smalls = wqkv_all[:, 64].astype(F32)
    g_attn_gain = smalls[:, :64].reshape(-1)
    g_ffn_gain = smalls[:, 64:128].reshape(-1)
    g_query_gain = smalls[:, 128:136].reshape(-1)
    g_key_gain = smalls[:, 136:144].reshape(-1)
    wqkv = wqkv_all[:, :64].reshape(width, 512)
    wo = wo_all.reshape(256, width)
    wgu = wgu_all.reshape(width, 768)
    wd = wd_all.reshape(384, width)
    wg, wu = wgu[:, :384], wgu[:, 384:]

    logical, where_at = token_places(block_table, segment_ids[:, 0])
    seg = segment_ids[:, 0]
    visible = (logical[:, None, :] <= logical[:, :, None]) & (
        (seg[:, None, :] == 0) | (seg[:, None, :] == seg[:, :, None])
    )
    cos, sin = rope_tables(where_at)

    x = x_all.reshape(mbs, 1024, width).astype(F32)
    normed_in = rms_gain(x, g_attn_gain).astype(BF).reshape(2048, width)
    raw = forward_dot(normed_in, wqkv).reshape(mbs, 1024, 4, HEAD)
    q_full, back_q = jax.vjp(lambda r, g: prepare_heads(r, g, cos, sin), raw[:, :, :2], g_query_gain)
    k_full, back_k = jax.vjp(lambda r, g: prepare_heads(r, g, cos, sin), raw[:, :, 2:3], g_key_gain)
    q = q_full.astype(BF)
    k = k_full.astype(BF)[:, :, 0]
    v = raw[:, :, 3].astype(BF)
    scale = HEAD ** (-0.5)
    scores = jnp.einsum("mqhd,mpd->mhqp", q, k, preferred_element_type=F32) * scale
    scores = jnp.where(visible[:, None], scores, -1e30)
    peak = jnp.max(scores, axis=-1, keepdims=True)
    shifted = jnp.exp(scores - peak)
    row_total = jnp.sum(shifted, axis=-1, keepdims=True)
    probs = shifted / row_total
    probs_low = probs.astype(BF)
    mixed = jnp.einsum("mhqp,mpd->mqhd", probs_low, v, preferred_element_type=F32)
    mixed = mixed.astype(BF).reshape(2048, 256)
    att_part = forward_dot(mixed, wo).astype(BF).reshape(2, 8, 128, width)

    def reduce_ctx_body(net, part, total, *bufs):
        return [reduce_ctx(net, part, total, *bufs)]

    (att_sum,) = comm_call(
        reduce_ctx_body,
        RING_Z,
        [((2, 128, width), F32)],
        reduce_ctx_scratch(width),
        1,
        [True],
        [True],
        32,
    )(att_part)
    attended = tok.reshape(256, width).astype(F32) + att_sum.reshape(256, width)
    r2 = lax.rsqrt(jnp.mean(attended * attended, axis=-1, keepdims=True) + 1e-06)
    normed_mid = (attended * r2 * g_ffn_gain).astype(BF)

    def gather_tp_body(net, src, out):
        return [gather_tp(net, src, out)]

    (mid_all,) = comm_call(
        gather_tp_body, RING_X, [((8, 256, width), BF)], [], 2, [False], [False], 16
    )(normed_mid)
    nm = mid_all.reshape(2048, width)
    ct = cot_all.reshape(2048, width)
    gate_up = forward_dot(nm, wgu)
    gate, up = gate_up[:, :384], gate_up[:, 384:]
    sig = jax.nn.sigmoid(gate)
    silu = gate * sig
    hidden = (silu * up).astype(BF)
    out_part = forward_dot(hidden, wd).astype(BF).reshape(8, 256, width)
    g_hidden = against_cols(ct, wd)
    g_gate = (g_hidden * up * sig * (1.0 + gate * (1.0 - sig))).astype(BF)
    g_up = (g_hidden * silu).astype(BF)
    g_gu = jnp.concatenate([g_gate, g_up], axis=1)
    grad_down_part = across_rows(hidden, ct).astype(BF)
    grad_gu_part = across_rows(nm, g_gu).astype(BF)
    mid_part = against_cols(g_gu, wgu).astype(BF).reshape(8, 256, width)

    def reduce_tp_body(net, a, b, ta, tb, *bufs):
        return [reduce_tp(net, a, ta, *bufs[:4]), reduce_tp(net, b, tb, *bufs[4:])]

    g_mid, out_sum = comm_call(
        reduce_tp_body,
        RING_X,
        [((256, width), F32), ((256, width), F32)],
        reduce_tp_scratch(width) * 2,
        3,
        [True, True],
        [True, True],
        32,
    )(mid_part, out_part)
    output = (attended + out_sum).astype(BF)
    n2 = g_mid * g_ffn_gain
    grad_ffn_gain = jnp.sum(g_mid * attended * r2, axis=0)
    g_attended = (
        cot.astype(F32)
        + r2 * n2
        - attended * (r2 * r2 * r2) * jnp.mean(n2 * attended, axis=-1, keepdims=True)
    )
    g_attn = g_attended.astype(BF)

    def gather_ctx_body(net, src, out):
        return [gather_ctx(net, src, out)]

    (g_attn_all,) = comm_call(
        gather_ctx_body, RING_Z, [((2, 8, 128, width), BF)], [], 4, [False], [False], 32
    )(g_attn.reshape(2, 128, width))
    ga = g_attn_all.reshape(2048, width)
    g_mixed = against_cols(ga, wo).astype(BF).reshape(2, 1024, 2, HEAD)
    grad_out_part = across_rows(mixed, ga).astype(BF)
    g_probs = jnp.einsum("mqhd,mpd->mhqp", g_mixed, v, preferred_element_type=F32)
    inner = jnp.sum(probs * g_probs, axis=-1, keepdims=True)
    g_scores = (probs * (g_probs - inner)).astype(BF)
    g_q = jnp.einsum("mhqp,mpd->mqhd", g_scores, k, preferred_element_type=F32) * scale
    g_k = jnp.einsum("mhqp,mqhd->mpd", g_scores, q, preferred_element_type=F32) * scale
    g_v = jnp.einsum("mhqp,mqhd->mpd", probs_low, g_mixed, preferred_element_type=F32)
    g_q_raw, grad_query_gain = back_q(g_q)
    g_k_raw, grad_key_gain = back_k(g_k[:, :, None])
    g_raw = (
        jnp.concatenate([g_q_raw, g_k_raw, g_v[:, :, None]], axis=2).astype(BF).reshape(2048, 512)
    )
    grad_qkv_part = across_rows(normed_in, g_raw).astype(BF)
    in_part = against_cols(g_raw, wqkv).astype(BF).reshape(2, 8, 128, width)
    (in_sum,) = comm_call(
        reduce_ctx_body,
        RING_Z,
        [((2, 128, width), F32)],
        reduce_ctx_scratch(width),
        5,
        [True],
        [True],
        32,
    )(in_part)
    g_in = in_sum.reshape(256, width)
    x_own = tok.reshape(256, width).astype(F32)
    r1 = lax.rsqrt(jnp.mean(x_own * x_own, axis=-1, keepdims=True) + 1e-06)
    n1 = g_in * g_attn_gain
    grad_attn_gain = jnp.sum(g_in * x_own * r1, axis=0)
    grad_tokens = (
        g_attended
        + r1 * n1
        - x_own * (r1 * r1 * r1) * jnp.mean(n1 * x_own, axis=-1, keepdims=True)
    )

    small_terms = jnp.concatenate(
        [
            grad_attn_gain.reshape(16, 64),
            grad_ffn_gain.reshape(16, 64),
            grad_query_gain.reshape(16, 8),
            grad_key_gain.reshape(16, 8),
            jnp.zeros((16, 512 - 144), F32),
        ],
        axis=1,
    ).astype(BF)
    qkv_terms = jnp.concatenate(
        [grad_qkv_part.reshape(16, 64, 512), jnp.broadcast_to(small_terms[:, None], (16, 16, 512))],
        axis=1,
    )
    wo_terms = grad_out_part.reshape(2, 8, 16, width).transpose(1, 0, 2, 3).reshape(16, 16, width)

    def terms_body(net, a, b, g, d, oa, ob, og, od):
        return [
            scatter_plane(net, a, oa),
            scatter_plane(net, b, ob),
            scatter_copies(net, g, d, og, od),
        ]

    ta, tb, tg, td = comm_call(
        terms_body,
        PLANE_SHIFTS + COPY_SHIFTS,
        [
            ((16, 80, 512), BF),
            ((16, 16, width), BF),
            ((16, 64, 768), BF),
            ((16, 192, 128), BF),
        ],
        [],
        6,
        [False] * 4,
        [False] * 4,
        60,
        4,
    )(qkv_terms, wo_terms, grad_gu_part.reshape(16, 64, 768), grad_down_part.reshape(2, 192, width))

    def summed(t):
        return jnp.sum(t.astype(F32), axis=0).astype(BF)

    def spread_body(net, a, b, g, d, oa, ob, og, od, mb_, mg):
        return [
            spread_ctx(net, b, mb_, lambda: exchange_chips(net, mb_, ob)),
            spread_ctx(net, g, mg, lambda: exchange_tp(net, mg, og)),
            spread_ctx(net, a, oa),
            spread_ctx(net, d, od),
        ]

    sa_, sb_, sg_, sd_, _, _ = comm_call(
        spread_body,
        CTX_SHIFTS + PLANE_SHIFTS,
        [
            ((8, 80, 512), BF),
            ((8, 16, width), BF),
            ((8, 64, 768), BF),
            ((8, 192, 128), BF),
            ((8, 16, width), BF),
            ((8, 64, 768), BF),
        ],
        [],
        7,
        [False] * 4,
        [False] * 6,
        48,
        6,
    )(summed(ta), summed(tb), summed(tg), summed(td))

    qkv_grad = sa_[:, :64].astype(F32)
    grad_w_query = qkv_grad[:, :, :256].transpose(1, 0, 2).reshape(64, 2048)
    grad_w_key = qkv_grad[:, :, 256:384].transpose(1, 0, 2).reshape(64, 1024)
    grad_w_value = qkv_grad[:, :, 384:].transpose(1, 0, 2).reshape(64, 1024)
    gains = jnp.sum(sa_[:, 64].astype(F32), axis=0)
    grad_w_out = sb_.astype(F32).reshape(128, width)

    def from_tp(g):
        return g.reshape(8, 64, 2, 192).transpose(1, 2, 0, 3).reshape(64, 3072)

    gu_grad = sg_.astype(F32)
    grad_w_gate = from_tp(gu_grad[:, :, :384])
    grad_w_up = from_tp(gu_grad[:, :, 384:])
    grad_w_down = sd_.astype(F32).transpose(1, 0, 2).reshape(192, width)
    return (
        output.reshape(2, 1, 128, width),
        grad_tokens.reshape(2, 1, 128, width),
        gains[:64],
        grad_w_query,
        grad_w_key,
        grad_w_value,
        gains[128:136],
        gains[136:144],
        grad_w_out,
        gains[64:128],
        grad_w_gate,
        grad_w_up,
        grad_w_down,
    )


def solution(mesh):
    placed = (
        P(None, "fsdp", "ctx", None),
        P(None, "fsdp", "ctx", None),
        P(),
        P(None, "fsdp", None),
        P(None, "fsdp", "ctx"),
        P("fsdp"),
        P("fsdp", None),
        P("fsdp", None),
        P("fsdp", None),
        P("fsdp"),
        P("fsdp"),
        P("fsdp", None),
        P("fsdp"),
        P("fsdp", None),
        P("fsdp", None),
        P("fsdp", None),
    )
    return jax.shard_map(
        per_device,
        mesh=mesh,
        in_specs=placed,
        out_specs=(
            P(None, "fsdp", "ctx", None),
            P(None, "fsdp", "ctx", None),
            P("fsdp"),
            P("fsdp", None),
            P("fsdp", None),
            P("fsdp", None),
            P("fsdp"),
            P("fsdp"),
            P("fsdp", None),
            P("fsdp"),
            P("fsdp", None),
            P("fsdp", None),
            P("fsdp", None),
        ),
        check_vma=False,
    )
```

```python
import functools
import math

import jax
import jax.numpy as jnp
from jax import lax
from jax.experimental import pallas as pl
from jax.experimental.pallas import tpu as pltpu
from jax.sharding import PartitionSpec as P

MESH = pl.DeviceIdType.MESH
SIZES = {"z": 4, "yl": 2, "yh": 2, "x": 4, "core": 2}
BF = jnp.bfloat16
F32 = jnp.float32
HEAD = 128


def my_place():
    c = lax.axis_index("ctx")
    f = lax.axis_index("fsdp")
    return {"z": c // 2, "yl": c % 2, "yh": f // 8, "x": (f // 2) % 4, "core": f % 2}


def moved(me, shift):
    to = dict(me)
    for axis, step in shift.items():
        to[axis] = (me[axis] + (step % SIZES[axis])) % SIZES[axis]
    return to


def ctx_of(place):
    return place["z"] * 2 + place["yl"]


def tp_of(place):
    return place["x"] * 2 + place["core"]


def chip_of(place):
    return place["yh"] * 4 + place["x"]


def head_of(place):
    return place["z"] * 2 + place["core"]


def fsdp_of(place):
    return chip_of(place) * 2 + place["core"]


def device_of(place):
    return (ctx_of(place), fsdp_of(place))


CTX_SHIFTS = [{"z": a, "yl": b} for a in range(4) for b in range(2) if a or b]
PLANE_SHIFTS = [
    {"yh": a, "x": b, "core": d}
    for a in range(2)
    for b in range(4)
    for d in range(2)
    if a or b or d
]
CHIP_SHIFTS = [{"yh": a, "x": b} for a in range(2) for b in range(4) if a or b]
TP_SHIFTS = [{"x": b, "core": d} for b in range(4) for d in range(2) if b or d]
COPY_SHIFTS = [
    {"z": a, "yl": b, "yh": d}
    for a in range(4)
    for b in range(2)
    for d in range(2)
    if a or b or d
]
WEIGHT_PLANE = [
    {"yh": a, "yl": a, "x": b, "core": d}
    for a in range(2)
    for b in range(4)
    for d in range(2)
    if a or b or d
]
WEIGHT_CHIPS = [{"yh": a, "yl": a, "x": b} for a in range(2) for b in range(4) if a or b]
SAMPLE_SHIFTS = [
    {"yh": a, "yl": b, "x": d}
    for a in range(2)
    for b in range(2)
    for d in range(4)
    if a or b or d
]
HEAD_SHIFTS = [{"z": a, "core": b} for a in range(4) for b in range(2) if a or b]
RING_Z = [{"z": 1}, {"z": 3}, {"core": 1}, {"yl": 1, "core": 1}]
RING_X = [{"x": 1}, {"x": 3}, {"core": 1}]


def back(shift):
    return {axis: -step for axis, step in shift.items()}


class Net:
    def __init__(self, send_sems, recv_sems, local_sems, pair_sems):
        self.me = my_place()
        self.send_sems, self.recv_sems, self.local_sems = send_sems, recv_sems, local_sems
        self.pair_sems = pair_sems
        self.count = 0
        self.locals = 0
        self.pending = []

    def enter(self, shifts):
        barrier = pltpu.get_barrier_semaphore()
        for shift in shifts:
            pl.semaphore_signal(
                barrier, inc=1, device_id=device_of(moved(self.me, shift)), device_id_type=MESH
            )
        pl.semaphore_wait(barrier, len(shifts))

    def send(self, src, dst, **shift):
        at = self.count
        self.count += 1
        copy = pltpu.make_async_remote_copy(
            src_ref=src,
            dst_ref=dst,
            send_sem=self.send_sems.at[at],
            recv_sem=self.recv_sems.at[at],
            device_id=device_of(moved(self.me, shift)),
            device_id_type=MESH,
        )
        copy.start()
        self.pending.append(copy.wait_send)
        return copy

    def pair(self, src, dst, place, recv, new=True):
        if new:
            self.count += 1
        return pltpu.make_async_remote_copy(
            src_ref=src,
            dst_ref=dst,
            send_sem=self.send_sems.at[self.count - 1],
            recv_sem=self.pair_sems.at[recv],
            device_id=device_of(place),
            device_id_type=MESH,
        )

    def spare(self):
        self.locals += 1
        return self.local_sems.at[self.locals - 1]

    def settle(self, copy):
        copy.wait()
        self.pending.remove(copy.wait)

    def local(self, src, dst):
        copy = pltpu.make_async_copy(src, dst, self.local_sems.at[self.locals])
        self.locals += 1
        copy.start()
        self.pending.append(copy.wait)
        return copy

    def swap(self, src, dst):
        return Swap(self, src, dst)

    def finish(self):
        for wait in self.pending:
            wait()


class Swap:
    def __init__(self, net, src, dst):
        me = net.me
        self.away = me["yl"] != me["core"]
        at = net.count
        net.count += 1
        self.remote = pltpu.make_async_remote_copy(
            src_ref=src,
            dst_ref=dst,
            send_sem=net.send_sems.at[at],
            recv_sem=net.recv_sems.at[at],
            device_id=device_of(moved(me, {"yl": 1, "core": 1})),
            device_id_type=MESH,
        )
        self.near = pltpu.make_async_copy(src, dst, net.spare())
        pl.when(self.away)(self.remote.start)
        pl.when(jnp.logical_not(self.away))(self.near.start)

    def wait(self):
        pl.when(self.away)(self.remote.wait)
        pl.when(jnp.logical_not(self.away))(self.near.wait)


def run_tasks(tasks):
    tasks = list(tasks)
    while tasks:
        left = []
        for task in tasks:
            try:
                next(task)
                left.append(task)
            except StopIteration:
                pass
        tasks = left


def unique(shifts):
    seen, out = set(), []
    for shift in shifts:
        key = tuple(sorted((k, v) for k, v in shift.items() if v))
        if key not in seen:
            seen.add(key)
            out.append(shift)
    return out


def comm_call(body, shifts, outs, scratch, cid, in_vmem, out_vmem, n_remote, n_local=1):
    shifts = unique(shifts)

    def kernel(*refs):
        refs, sems = refs[:-4], refs[-4:]
        net = Net(*sems)
        net.enter(shifts)
        drain(*(body(net, *refs) or ()))
        net.finish()

    vm = pl.BlockSpec(memory_space=pltpu.VMEM)
    hb = pl.BlockSpec(memory_space=pl.ANY)
    return pl.pallas_call(
        kernel,
        out_shape=[jax.ShapeDtypeStruct(s, d) for s, d in outs],
        in_specs=[vm if v else hb for v in in_vmem],
        out_specs=[vm if v else hb for v in out_vmem],
        scratch_shapes=list(scratch)
        + [
            pltpu.SemaphoreType.DMA((n_remote,)),
            pltpu.SemaphoreType.DMA((n_remote,)),
            pltpu.SemaphoreType.DMA((n_local,)),
            pltpu.SemaphoreType.DMA((2,)),
        ],
        compiler_params=pltpu.CompilerParams(
            collective_id=cid, has_side_effects=True, vmem_limit_bytes=60 << 20
        ),
    )


def drain(*tasks):
    run_tasks(tasks)


def step(task):
    next(task, None)


class Weave:
    def __init__(self):
        self.tasks = []

    def add(self, task):
        next(task)
        self.tasks.append(task)
        return task

    def tick(self, count=1):
        for _ in range(count):
            if self.tasks:
                self.step(self.tasks.pop(0))

    def step(self, task):
        try:
            next(task)
            self.tasks.append(task)
        except StopIteration:
            pass

    def finish(self, task):
        if task in self.tasks:
            self.tasks.remove(task)
            for _ in task:
                pass

    def finish_all(self):
        drain(*self.tasks)
        self.tasks = []


def gather_ring(net, axis, src, block, rows):
    me = net.me
    half = rows // 2
    low, high = (0, half), (half, half)

    def at(step, part=(0, rows)):
        return block(moved(me, {axis: step}), *part)

    def cut(part):
        return src.at[..., pl.ds(*part), :]

    def send(step, part, shift):
        here = cut(part) if step == 0 else at(step, part)
        return net.send(here, at(step, part), **shift)

    right, left, other = {axis: 1}, {axis: -1}, {"core": 1}
    r0 = send(0, low, right)
    l1 = send(0, high, left)
    r1 = send(0, high, right)
    l0 = send(0, low, left)
    own = send(0, (0, rows), other)
    yield
    r0.wait_recv()
    fr = send(-1, low, right)
    l1.wait_recv()
    fl = send(1, high, left)
    yield
    r1.wait_recv()
    cr = send(-1, (0, rows), other)
    l0.wait_recv()
    cl = send(1, (0, rows), other)
    yield
    fr.wait_recv()
    c2r = send(2, low, other)
    fl.wait_recv()
    c2l = send(2, high, other)
    yield
    for copy in (own, cr, cl, c2r, c2l):
        copy.wait_recv()


def add_rows(dst, terms, rows, step=32):
    def one(i, carry):
        at = pl.ds(pl.multiple_of(i * step, step), step)
        total = terms[0][at, :].astype(F32)
        for term in terms[1:]:
            total = total + term[at, :].astype(F32)
        dst[at, :] = total.astype(dst.dtype)
        return carry

    lax.fori_loop(0, rows // step, one, 0)


def reduce_ring(net, axis, part, index, total, rc, s, rh, r):
    me = net.me
    low, high = pl.ds(0, 64), pl.ds(64, 64)
    right, left, other = {axis: 1}, {axis: -1}, {"core": 1}

    def at(step, core, rows=pl.ds(0, 128)):
        return part.at[index(moved(me, {axis: step, "core": core})), rows]

    cc = {}
    for step in (2, 1, 3, 0):
        cc[step] = net.send(at(step, 1), rc.at[step], **other)
    yield
    cc[2].wait_recv()
    add_rows(s.at[2], [at(2, 0), rc.at[2]], 128)
    h_r = net.send(s.at[2, low], rh.at[0], **right)
    h_l = net.send(s.at[2, high], rh.at[1], **left)
    cc[1].wait_recv()
    add_rows(s.at[1, high], [at(1, 0, high), rc.at[1, high]], 64)
    r_high = net.send(s.at[1, high], r.at[0, high], **right)
    cc[3].wait_recv()
    add_rows(s.at[3, low], [at(3, 0, low), rc.at[3, low]], 64)
    l_low = net.send(s.at[3, low], r.at[1, low], **left)
    yield
    h_r.wait_recv()
    add_rows(s.at[1, low], [at(1, 0, low), rc.at[1, low], rh.at[0]], 64)
    r_low = net.send(s.at[1, low], r.at[0, low], **right)
    h_l.wait_recv()
    add_rows(s.at[3, high], [at(3, 0, high), rc.at[3, high], rh.at[1]], 64)
    l_high = net.send(s.at[3, high], r.at[1, high], **left)
    yield
    for copy in (cc[0], r_high, l_low, r_low, l_high):
        copy.wait_recv()
    add_rows(total, [at(0, 0), rc.at[0], r.at[0], r.at[1]], 128)


def reduce_ring_scratch(width):
    return [
        pltpu.VMEM((4, 128, width), BF),
        pltpu.VMEM((4, 128, width), BF),
        pltpu.VMEM((2, 64, width), BF),
        pltpu.VMEM((2, 128, width), BF),
    ]


def gather_heads_weights(net, wq, wk, wv, small, stage, out):
    me = net.me
    mine = fsdp_of(me)
    staged = []
    for core in range(2):
        h = me["z"] * 2 + core
        place = stage.at[core]
        for src, dst in (
            (wq.at[:, pl.ds(pl.multiple_of(h * 256, 256), 256)], place.at[pl.ds(0, 64), pl.ds(0, 256)]),
            (wk.at[:, pl.ds(pl.multiple_of(h * 128, 128), 128)], place.at[pl.ds(0, 64), pl.ds(256, 128)]),
            (wv.at[:, pl.ds(pl.multiple_of(h * 128, 128), 128)], place.at[pl.ds(0, 64), pl.ds(384, 128)]),
            (small, place.at[pl.ds(64, 16)]),
        ):
            staged.append(net.local(src, dst))
    yield
    for copy in staged:
        net.settle(copy)
    kept = net.local(stage.at[me["core"]], out.at[mine])
    copies = [
        net.send(stage.at[moved(me, shift)["core"]], out.at[mine], **shift)
        for shift in WEIGHT_PLANE
    ]
    yield
    for copy in copies:
        copy.wait_recv()
    net.settle(kept)


def gather_out_weights(net, src, mid, out):
    me = net.me
    mine = chip_of(me)
    stay = net.local(src.at[mine], mid.at[mine])
    first = [
        net.send(src.at[chip_of(moved(me, shift))], mid.at[mine], **shift) for shift in WEIGHT_CHIPS
    ]
    yield
    for copy in first:
        copy.wait_recv()
    net.settle(stay)
    place = out.at[me["core"], mine]
    kept = net.local(mid.at[head_of(me)], place)
    copies = [
        net.send(mid.at[head_of(moved(me, shift))], place, **shift) for shift in WEIGHT_PLANE
    ]
    yield
    for copy in copies:
        copy.wait_recv()
    net.settle(kept)


def gather_ff_weights(net, gate, up, down, gate_stage, up_stage, gate_out, up_out, down_out):
    me = net.me
    mine = fsdp_of(me)
    staged = []
    for j in range(8):
        at = pl.ds(j * 384, 384)
        staged.append(net.local(gate.at[:, at], gate_stage.at[j]))
        staged.append(net.local(up.at[:, at], up_stage.at[j]))
    chip = chip_of(me)
    near = dict(me, x=chip // 2, core=chip % 2)
    far = dict(near, yh=(me["yh"] + 1) % 2, yl=(me["yl"] + 1) % 2)
    half = me["core"]
    here = tp_of(me) == chip
    away = jnp.logical_not(here)
    one = net.pair(down, down_out.at[half], near, half)
    two = net.pair(down, down_out.at[half], far, half)
    stay = pltpu.make_async_copy(down, down_out.at[half], net.spare())
    yield
    for copy in staged:
        net.settle(copy)

    def pieces(place):
        j = tp_of(place)
        return [(gate_stage.at[j], gate_out.at[mine]), (up_stage.at[j], up_out.at[mine])]

    kept = [net.local(src, dst) for src, dst in pieces(me)]
    copies = [
        net.send(src, dst, **shift)
        for shift in WEIGHT_PLANE
        for src, dst in pieces(moved(me, shift))
    ]
    two.start()
    pl.when(here)(stay.start)
    pl.when(away)(one.start)
    yield
    for copy in copies:
        copy.wait_recv()
    for copy in kept:
        net.settle(copy)
    for h in (0, 1):
        arrived = net.pair(down, down_out.at[h], near, h, new=False)
        pl.when(jnp.logical_not(here & (half == h)))(arrived.wait_recv)
    two.wait_send()
    pl.when(here)(stay.wait)
    pl.when(away)(one.wait_send)


def chunk_of(place):
    return chip_of(place) * 2 + place["yl"]


def scatter_samples(net, pick, out):
    me = net.me
    mine = chunk_of(me)
    kept = net.local(pick(me), out.at[mine])
    copies = [net.send(pick(moved(me, shift)), out.at[mine], **shift) for shift in SAMPLE_SHIFTS]
    yield
    for copy in copies:
        copy.wait_recv()
    net.settle(kept)


def copy_index(place):
    return place["yh"] * 8 + ctx_of(place)


def scatter_copies(net, gate, up, down, gate_out, up_out, down_out):
    me = net.me

    def piece(place):
        return down.at[place["yh"], :, pl.ds(pl.multiple_of(ctx_of(place) * 128, 128), 128)]

    mine = copy_index(me)

    def pieces(place):
        at = copy_index(place)
        return [
            (gate.at[at], gate_out.at[mine]),
            (up.at[at], up_out.at[mine]),
            (piece(place), down_out.at[mine]),
        ]

    for src, dst in pieces(me):
        net.local(src, dst)
    copies = [
        net.send(src, dst, **shift) for shift in COPY_SHIFTS for src, dst in pieces(moved(me, shift))
    ]
    yield
    for copy in copies:
        copy.wait_recv()


def spread(net, src, out, shifts, index, after=None):
    me = net.me
    mine = out.at[index(me)]
    kept = net.local(src, mine)
    copies = [net.send(src, mine, **shift) for shift in shifts]
    yield
    for copy in copies:
        copy.wait_recv()
    net.settle(kept)
    if after is not None:
        yield
        yield from after()


def swap_task(net, src, out):
    swapped = net.swap(src, out)
    yield
    swapped.wait()


def exchange_chips(net, src, out, after):
    me = net.me
    mine = chip_of(me)
    kept = net.local(src.at[mine], out.at[mine])
    copies = [
        net.send(src.at[chip_of(moved(me, shift))], out.at[mine], **shift) for shift in CHIP_SHIFTS
    ]
    yield
    for copy in copies:
        copy.wait_recv()
    net.settle(kept)
    yield from after()


def exchange_tp(net, src, out):
    me = net.me
    mine = tp_of(me)
    place = out.at[:, pl.ds(pl.multiple_of(mine * 384, 128), 384)]
    net.local(src.at[mine], place)
    copies = [net.send(src.at[tp_of(moved(me, shift))], place, **shift) for shift in TP_SHIFTS]
    yield
    for copy in copies:
        copy.wait_recv()


def spread_down(net, src, mid, out):
    me = net.me
    j = tp_of(me)
    goal = dict(me, yh=j // 4, x=j % 4, core=me["yh"])
    stays = (j == chip_of(me)) & (me["yh"] == me["core"])
    sent = net.pair(src, mid, goal, 0)
    kept = pltpu.make_async_copy(src, mid, net.spare())

    @pl.when(stays)
    def _():
        kept.start()
        kept.wait()

    @pl.when(jnp.logical_not(stays))
    def _():
        sent.start()

    yield

    @pl.when(jnp.logical_not(stays))
    def _():
        sent.wait()

    place = out.at[:, pl.ds(pl.multiple_of(ctx_of(me) * 128, 128), 128)]
    net.local(mid, place)
    copies = [net.send(mid, place, **shift) for shift in CTX_SHIFTS]
    yield
    for copy in copies:
        copy.wait_recv()


def rope_tables(where_at):
    frequency = jnp.exp(
        jnp.arange(0, HEAD // 2, dtype=F32) * (-2.0 * math.log(1000000.0) / HEAD)
    )
    angles = where_at.astype(F32)[..., None] * frequency
    cos, sin = jnp.cos(angles), jnp.sin(angles)
    return jnp.concatenate([cos, cos], axis=-1), jnp.concatenate([-sin, sin], axis=-1)


def across_rows(a, b):
    return lax.dot_general(a, b, (((0,), (0,)), ((), ())), preferred_element_type=F32)


def against_cols(a, b):
    return lax.dot_general(a, b, (((1,), (1,)), ((), ())), preferred_element_type=F32)


def forward_dot(a, b):
    return jnp.dot(a, b, preferred_element_type=F32)


EXP2_SCALE = HEAD ** (-0.5) * math.log2(math.e)


def norm_scale(v):
    return lax.rsqrt(jnp.mean(v * v, axis=-1, keepdims=True) + 1e-06)


def visible_tile(lk, lk2, lq, sq):
    lk, lk2 = jnp.concatenate([lk, lk], axis=1), jnp.concatenate([lk2, lk2], axis=1)
    return (lk <= lq) & (lk2 >= sq)


def half_loop(body, part, parts, count):
    lax.fori_loop(part * count // parts, (part + 1) * count // parts, body, 0)


class Front:
    def __init__(self, m, gains, wqkv, wo, xs, tables, saved, part, mixed, vt):
        self.gains, self.wqkv, self.wo, self.xs = gains, wqkv, wo, xs.at[m]
        self.cos, self.sin, self.lk, self.lk2, self.lq, self.sq = (t.at[m] for t in tables)
        self.xn, self.raw, self.q, self.k, self.v, self.mixt, self.rl = (t.at[m] for t in saved)
        self.part, self.mixed, self.vt = part.at[m], mixed, vt

    def project(self, i, carry):
        rows = pl.ds(pl.multiple_of(i * 256, 256), 256)
        x = self.xs[pl.ds(i * 2, 2)].reshape(256, 1024).astype(F32)
        low = (x * norm_scale(x) * self.gains[0:1, :]).astype(BF)
        self.xn[rows, :] = low
        y = forward_dot(low, self.wqkv[:, pl.ds(0, 64), :].reshape(1024, 512))
        self.raw[rows, :] = y[:, :384]
        c, s = self.cos[rows, :], self.sin[rows, :]
        for head in range(3):
            u = y[:, head * HEAD : (head + 1) * HEAD]
            lane = HEAD * (head // 2)
            n = u * norm_scale(u) * self.gains[2:3, lane : lane + HEAD]
            turned = (n * c + pltpu.roll(n, HEAD // 2, 1) * s).astype(BF)
            if head < 2:
                self.q[head, rows, :] = turned
            else:
                self.k[rows, :] = turned
        value = y[:, 384:]
        self.v[rows, :] = value.astype(BF)
        self.vt[:, rows] = value.T.astype(BF)
        return carry

    def attend(self, head, i, carry):
        rows = pl.ds(pl.multiple_of(i * 256, 256), 256)
        s = against_cols(self.k[...], self.q[head, rows, :])
        seen = visible_tile(self.lk[...], self.lk2[...], self.lq[:, rows], self.sq[:, rows])
        e = jnp.where(seen, jnp.exp2(s * EXP2_SCALE), 0.0)
        inv = 1.0 / jnp.sum(e, axis=0, keepdims=True)
        self.rl[head, :, rows] = inv
        m = forward_dot(self.vt[...], e.astype(BF)) * inv
        self.mixt[head * HEAD : (head + 1) * HEAD, rows] = m.astype(BF)
        self.mixed[rows, head * HEAD : (head + 1) * HEAD] = m.T.astype(BF)
        return carry

    def project_out(self, i, carry):
        rows = pl.ds(pl.multiple_of(i * 256, 256), 256)
        y = forward_dot(self.mixed[rows, :], self.wo[...].reshape(256, 1024)).astype(BF)
        self.part[pl.ds(i * 2, 2)] = y.reshape(2, 128, 1024)
        return carry

    def pieces(self):
        return (
            [functools.partial(half_loop, self.project, p, 2, 4) for p in range(2)]
            + [
                functools.partial(half_loop, functools.partial(self.attend, head), p, 2, 4)
                for head in range(2)
                for p in range(2)
            ]
            + [functools.partial(half_loop, self.project_out, 0, 1, 4)]
        )


def sequence_block(out):
    def block(place, lo, n):
        return out.at[head_of(place), pl.ds(lo, n)]

    return block


def front_body(
    net,
    tok, cot, small, wq, wk, wv, wo_in, wg, wu, wd, cos, sin, lk, lk2, lq, sq,
    attended, normed, gains, wqkv, wo, cots, wgs, wus, wds, mid,
    xn_out, raw_out, q_out, k_out, v_out, mixt_out, rl_out,
    xn, raw, q, k, v, mixt, rl,
    xs, part, mixed, vt, stage, gate_stage, up_stage, outbox, inbox, *bufs,
):
    me = net.me
    heads = gather_heads_weights(net, wq, wk, wv, small, stage, wqkv)
    next(heads)
    swaps = [net.swap(tok.at[m], xs.at[m, ctx_of(me)]) for m in range(2)]
    gather = [
        gather_ring(net, "z", xs.at[m, head_of(me)], sequence_block(xs.at[m]), 128)
        for m in range(2)
    ]
    outs = gather_out_weights(net, wo_in, mid, wo)
    feed = gather_ff_weights(net, wg, wu, wd, gate_stage, up_stage, wgs, wus, wds)

    def cot_block(place, lo, n):
        return cots.at[:, tp_of(place), pl.ds(lo, n)]

    cots_in = gather_ring(net, "x", cot, cot_block, 128)
    own_cot = net.local(cot, cots.at[:, tp_of(me)])
    next(heads)
    swaps[0].wait()
    next(gather[0])
    next(outs)
    next(feed)
    next(gather[0])
    swaps[1].wait()
    next(gather[1])
    next(gather[0])
    drain(gather[0])
    next(outs)
    drain(heads)
    next(cots_in)
    sums = jnp.sum(wqkv[:, pl.ds(64, 16), :].astype(F32), axis=0)
    gains[...] = jnp.zeros_like(gains)
    gains[0:1, :] = jnp.concatenate([sums[0:1], sums[1:2]], axis=1)
    gains[1:2, :] = jnp.concatenate([sums[2:3], sums[3:4]], axis=1)
    gains[2:3, :512] = sums[4:5]
    tables = (cos, sin, lk, lk2, lq, sq)
    saved = (xn, raw, q, k, v, mixt, rl)
    work = [
        Front(m, gains, wqkv, wo, xs, tables, saved, part, mixed, vt).pieces() for m in range(2)
    ]

    def save(m):
        for src, dst in zip(saved, (xn_out, raw_out, q_out, k_out, v_out, mixt_out, rl_out)):
            net.local(src.at[m], dst.at[m])

    def settle(m):
        x = tok[m].astype(F32) + inbox[m].astype(F32)
        attended[m] = x
        normed[m] = (x * norm_scale(x) * gains[1:2, :]).astype(BF)

    for at, piece in enumerate(work[0][:-1]):
        piece()
        step(gather[1])
        if at == 1:
            drain(outs)
        if at == 4:
            step(cots_in)
    drain(gather[1])
    work[0][-1]()
    reduce0 = reduce_ring(net, "z", part.at[0], head_of, outbox.at[0], *bufs[:4])
    next(reduce0)
    step(cots_in)
    next(feed)
    save(0)
    for at, piece in enumerate(work[1]):
        piece()
        if at in (0, 2, 4):
            step(reduce0)
        if at == 5:
            step(cots_in)
    drain(reduce0)
    back0 = net.swap(outbox.at[0], inbox.at[0])
    reduce1 = reduce_ring(net, "z", part.at[1], head_of, outbox.at[1], *bufs[4:])
    next(reduce1)
    save(1)
    next(reduce1)
    drain(cots_in)
    next(reduce1)
    back0.wait()
    settle(0)
    drain(reduce1)
    back1 = net.swap(outbox.at[1], inbox.at[1])
    drain(feed)
    back1.wait()
    settle(1)


class Back:
    def __init__(self, m, gains, wqkv, wo, g, tables, saved, part, graw, dwqkv, dwo, sums, work):
        self.m, self.gains, self.wqkv, self.wo, self.g = m, gains, wqkv, wo, g.at[m]
        self.cos, self.sin, self.lk, self.lk2, self.lq, self.sq = (t.at[m] for t in tables)
        self.xn, self.raw, self.q, self.k, self.v, self.mixt, self.rl = (t.at[m] for t in saved)
        self.part, self.graw = part.at[m], graw.at[m]
        self.dwqkv, self.dwo, self.sums = dwqkv, dwo, sums
        self.kt, self.dk, self.dv, self.dq = work

    def begin(self):
        self.kt[...] = self.k[...].astype(F32).T.astype(BF)
        self.dk[...] = jnp.zeros_like(self.dk)
        self.dv[...] = jnp.zeros_like(self.dv)

    def attend(self, head, i, carry):
        rows = pl.ds(pl.multiple_of(i * 256, 256), 256)
        at = slice(head * HEAD, (head + 1) * HEAD)
        g = self.g[pl.ds(i * 2, 2)].reshape(256, 1024)
        wo = self.wo[head].reshape(HEAD, 1024)
        gm = against_cols(g, wo).astype(BF)
        gmt = against_cols(wo, g).astype(BF)
        delta = jnp.sum(
            gmt.astype(F32) * self.mixt[at, rows].astype(F32), axis=0, keepdims=True
        )
        qt = self.q[head, rows, :]
        s = against_cols(self.k[...], qt)
        seen = visible_tile(self.lk[...], self.lk2[...], self.lq[:, rows], self.sq[:, rows])
        p = jnp.where(seen, jnp.exp2(s * EXP2_SCALE), 0.0) * self.rl[head, :, rows]
        dp = forward_dot(self.v[...], gmt)
        ds = (p * (dp - delta)).astype(BF)
        self.dv[...] += forward_dot(p.astype(BF), gm)
        self.dk[...] += forward_dot(ds, qt)
        self.dq[head, rows, :] = forward_dot(self.kt[...], ds).T
        return carry

    def unproject(self, i, carry):
        rows = pl.ds(pl.multiple_of(i * 256, 256), 256)
        c, s = self.cos[rows, :], self.sin[rows, :]
        for head in range(3):
            lane = head // 2
            at = slice(head * HEAD, (head + 1) * HEAD)
            gr = (self.dq[head, rows, :] if head < 2 else self.dk[rows, :]) * HEAD ** (-0.5)
            gu = gr * c - pltpu.roll(gr, HEAD // 2, 1) * s
            u = self.raw[rows, at]
            r = norm_scale(u)
            self.sums[lane : lane + 1, :] += jnp.sum(gu * (u * r), axis=0, keepdims=True)
            n = gu * self.gains[2:3, lane * HEAD : (lane + 1) * HEAD]
            d = r * n - u * (r * r * r) * jnp.mean(n * u, axis=-1, keepdims=True)
            self.graw[rows, at] = d.astype(BF)
        self.graw[rows, 384:] = self.dv[rows, :].astype(BF)
        y = against_cols(self.graw[rows, :], self.wqkv[:, pl.ds(0, 64), :].reshape(1024, 512))
        self.part[pl.ds(i * 2, 2)] = y.astype(BF).reshape(2, 128, 1024)
        return carry

    def pieces(self):
        return (
            [self.begin]
            + [
                functools.partial(half_loop, functools.partial(self.attend, head), p, 2, 4)
                for head in range(2)
                for p in range(2)
            ]
            + [functools.partial(half_loop, self.unproject, p, 2, 4) for p in range(2)]
        )

    def out_weights(self):
        def some(i, carry):
            at = pl.ds(pl.multiple_of(i * 256, 256), 256)
            y = forward_dot(self.mixt[...], self.g[:, :, at].reshape(1024, 256))
            self.dwo[:, at] = y if self.m == 0 else self.dwo[:, at] + y
            return carry

        lax.fori_loop(0, 4, some, 0)

    def head_weights(self):
        def some(i, carry):
            at = pl.ds(pl.multiple_of(i * 256, 256), 256)
            y = across_rows(self.xn[:, at], self.graw[...])
            self.dwqkv[at, :] = y if self.m == 0 else self.dwqkv[at, :] + y
            return carry

        lax.fori_loop(0, 4, some, 0)


def back_body(
    net,
    g_own, out_part_in, xn_in, raw_in, q_in, k_in, v_in, mixt_in, rl_in,
    wqkv, wo, gains, cos, sin, lk, lk2, lq, sq,
    in_sum, out_sum, dwqkv_low, dwo_low, sums,
    xn, raw, q, k, v, mixt, rl,
    g, out_part, part, graw, dwqkv, dwo, kt, dk, dv, dq, outbox, *bufs,
):
    me = net.me
    swaps = [net.swap(g_own.at[m], g.at[m, ctx_of(me)]) for m in range(2)]
    fetched = [net.local(out_part_in.at[0], out_part.at[0])]
    saved = (xn, raw, q, k, v, mixt, rl)
    needed = [
        net.local(src.at[m], dst.at[m])
        for m in range(2)
        for src, dst in zip((xn_in, raw_in, q_in, k_in, v_in, mixt_in, rl_in), saved)
    ]
    fetched.append(net.local(out_part_in.at[1], out_part.at[1]))
    sums[...] = jnp.zeros_like(sums)
    gather = [
        gather_ring(net, "z", g.at[m, head_of(me)], sequence_block(g.at[m]), 128) for m in range(2)
    ]
    outs = [
        reduce_ring(net, "x", out_part.at[m], tp_of, out_sum.at[m], *bufs[4 * m + 8 : 4 * m + 12])
        for m in range(2)
    ]
    swaps[0].wait()
    next(gather[0])
    net.settle(fetched[0])
    next(outs[0])
    next(gather[0])
    swaps[1].wait()
    next(gather[1])
    next(gather[0])
    drain(gather[0])
    for copy in needed:
        net.settle(copy)
    net.settle(fetched[1])
    tables = (cos, sin, lk, lk2, lq, sq)
    work = [
        Back(m, gains, wqkv, wo, g, tables, saved, part, graw, dwqkv, dwo, sums, (kt, dk, dv, dq))
        for m in range(2)
    ]
    for at, piece in enumerate(work[0].pieces()):
        piece()
        step(gather[1])
        if at in (1, 3, 5):
            step(outs[0])
    drain(gather[1])
    reduce0 = reduce_ring(net, "z", part.at[0], head_of, outbox.at[0], *bufs[:4])
    next(reduce0)
    drain(outs[0])
    next(outs[1])
    for at, piece in enumerate(work[1].pieces()):
        piece()
        if at in (1, 2, 3):
            step(reduce0)
        if at in (2, 4, 6):
            step(outs[1])
    drain(reduce0)
    back0 = net.swap(outbox.at[0], in_sum.at[0])
    reduce1 = reduce_ring(net, "z", part.at[1], head_of, outbox.at[1], *bufs[4:8])
    next(reduce1)
    work[0].out_weights()
    next(reduce1)
    work[0].head_weights()
    next(reduce1)
    work[1].out_weights()
    drain(reduce1)
    back1 = net.swap(outbox.at[1], in_sum.at[1])
    work[1].head_weights()
    drain(outs[1])
    dwqkv_low[...] = dwqkv[...].astype(BF).reshape(16, 64, 512)
    dwo_low[...] = dwo[...].astype(BF).reshape(2, 8, 16, 1024)
    back0.wait()
    back1.wait()


def token_places(block_table, first, seq):
    blocks = block_table.shape[1]
    block = seq // blocks
    logical = (
        jnp.repeat(block_table, block, axis=1) * block + jnp.arange(seq, dtype=jnp.int32) % block
    )
    prompt = seq // 2
    segment = jnp.where(logical < prompt, 0, jnp.where(logical < prompt + first, 1, 2))
    end = jnp.where(segment == 1, prompt - 1 + first, seq - 1)
    position = jnp.where(segment == 0, logical, 895 - (end - logical))
    return logical, segment, position


def per_device(
    tokens,
    cotangent,
    block_table,
    segment_ids,
    positions,
    gain_attn,
    w_query,
    key_projection,
    value_projection,
    query_norm_gain,
    key_norm_gain,
    w_out,
    gain_ffn,
    w_gate,
    w_up,
    w_down,
):
    ctx = lax.axis_index("ctx")
    mbs, width = tokens.shape[0], tokens.shape[-1]
    tok = tokens[:, 0]
    cot = cotangent[:, 0].reshape(256, width)

    f = lax.axis_index("fsdp")
    here = (jnp.arange(16) == f)[:, None]

    def placed(gain):
        return jnp.where(here, gain[None], jnp.zeros((), BF)).reshape(-1)

    small = jnp.concatenate(
        [
            placed(gain_attn),
            placed(gain_ffn),
            placed(query_norm_gain),
            placed(key_norm_gain),
            jnp.zeros((256 + 11 * 512,), BF),
        ]
    ).reshape(16, 512)
    count = jnp.sum((segment_ids[:, 0] == 1).astype(jnp.int32), axis=1, keepdims=True)
    other = lax.ppermute(count, "fsdp", [(i, i ^ 1) for i in range(16)])
    first = jnp.where(ctx % 2 == f % 2, count, other)
    logical, seg, where_at = token_places(block_table, first, 1024)
    later = jnp.where(seg == 0, 4096, logical)
    start = jnp.where(seg == 2, 512 + first, 0)
    lk = jnp.broadcast_to(logical[:, :, None], (mbs, 1024, HEAD))
    lk2 = jnp.broadcast_to(later[:, :, None], (mbs, 1024, HEAD))
    lq, sq = logical[:, None, :], start[:, None, :]
    cos, sin = rope_tables(where_at)

    vm = pltpu.VMEM
    saves = [
        ((2, 1024, width), BF),
        ((2, 1024, 384), F32),
        ((2, 2, 1024, HEAD), BF),
        ((2, 1024, HEAD), BF),
        ((2, 1024, HEAD), BF),
        ((2, 256, 1024), BF),
        ((2, 2, 1, 1024), F32),
    ]
    sequence = vm((2, 8, 128, width), BF)
    (
        attended, normed_mid, gain_rows, wqkv, wo, cot_all, wg, wu, wd, _, *saved
    ) = comm_call(
        front_body,
        RING_Z + RING_X + WEIGHT_PLANE,
        [
            ((2, 128, width), F32),
            ((2, 128, width), BF),
            ((8, width), F32),
            ((16, 80, 512), BF),
            ((2, 8, 16, width), BF),
            ((2, 8, 128, width), BF),
            ((16, 64, 384), BF),
            ((16, 64, 384), BF),
            ((2, 192, width), BF),
            ((8, 16, width), BF),
        ]
        + saves,
        [vm(shape, kind) for shape, kind in saves]
        + [sequence, sequence, vm((1024, 256), BF), vm((HEAD, 1024), BF)]
        + [vm((2, 80, 512), BF), vm((8, 64, 384), BF), vm((8, 64, 384), BF)]
        + [vm((2, 128, width), BF), vm((2, 128, width), BF)]
        + reduce_ring_scratch(width) * 2,
        0,
        [True] + [False] * 9 + [True] * 6,
        [True] * 5 + [False] * 12,
        160,
        64,
    )(
        tok, cotangent[:, 0], small, w_query, key_projection, value_projection,
        w_out.reshape(8, 16, width), w_gate, w_up, w_down, cos, sin, lk, lk2, lq, sq,
    )
    g_attn_gain, g_ffn_gain = gain_rows[0], gain_rows[1]
    attended = attended.reshape(256, width)
    r2 = lax.rsqrt(jnp.mean(attended * attended, axis=-1, keepdims=True) + 1e-06)
    wg, wu, wd = wg.reshape(width, 384), wu.reshape(width, 384), wd.reshape(384, width)

    def gather_tp_body(net, src, out):
        def block(place, lo, n):
            return out.at[:, tp_of(place), pl.ds(lo, n)]

        net.local(src, out.at[:, tp_of(net.me)])
        return [gather_ring(net, "x", src, block, 128)]

    (mid_all,) = comm_call(
        gather_tp_body, RING_X, [((2, 8, 128, width), BF)], [], 2, [False], [False], 16
    )(normed_mid)
    nm = mid_all.reshape(2048, width)
    ct = cot_all.reshape(2048, width)
    gate, up = forward_dot(nm, wg), forward_dot(nm, wu)
    sig = jax.nn.sigmoid(gate)
    silu = gate * sig
    hidden = (silu * up).astype(BF)
    out_part = forward_dot(hidden, wd).astype(BF).reshape(2, 8, 128, width)
    g_hidden = against_cols(ct, wd)
    g_gate = (g_hidden * up * sig * (1.0 + gate * (1.0 - sig))).astype(BF)
    g_up = (g_hidden * silu).astype(BF)
    grad_down_part = across_rows(hidden, ct).astype(BF)
    grad_gate_part = across_rows(nm, g_gate).astype(BF)
    grad_up_part = across_rows(nm, g_up).astype(BF)
    mid_part = (against_cols(g_gate, wg) + against_cols(g_up, wu)).astype(BF)
    mid_part = mid_part.reshape(2, 8, 128, width)

    def reduce_tp_body(net, part, total, *bufs):
        return [
            reduce_ring(net, "x", part.at[m], tp_of, total.at[m], *bufs[4 * m : 4 * m + 4])
            for m in range(2)
        ]

    (g_mid,) = comm_call(
        reduce_tp_body,
        RING_X,
        [((2, 128, width), F32)],
        reduce_ring_scratch(width) * 2,
        3,
        [True],
        [True],
        48,
    )(mid_part)
    g_mid = g_mid.reshape(256, width)
    n2 = g_mid * g_ffn_gain
    grad_ffn_gain = jnp.sum(g_mid * attended * r2, axis=0)
    g_attended = (
        cot.astype(F32)
        + r2 * n2
        - attended * (r2 * r2 * r2) * jnp.mean(n2 * attended, axis=-1, keepdims=True)
    )
    g_attn = g_attended.astype(BF)

    in_sum, out_sum, dwqkv, dwo, head_gains = comm_call(
        back_body,
        RING_Z + RING_X,
        [
            ((2, 128, width), BF),
            ((2, 128, width), F32),
            ((16, 64, 512), BF),
            ((2, 8, 16, width), BF),
            ((8, HEAD), F32),
        ],
        [vm(shape, kind) for shape, kind in saves]
        + [sequence, sequence, sequence, vm((2, 1024, 512), BF)]
        + [vm((1024, 512), F32), vm((256, 1024), F32), vm((HEAD, 1024), BF)]
        + [vm((1024, HEAD), F32), vm((1024, HEAD), F32), vm((2, 1024, HEAD), F32)]
        + [vm((2, 128, width), BF)]
        + reduce_ring_scratch(width) * 4,
        4,
        [True] + [False] * 8 + [True] * 9,
        [True] * 5,
        96,
        24,
    )(g_attn.reshape(2, 128, width), out_part, *saved, wqkv, wo, gain_rows, cos, sin, lk, lk2, lq, sq)
    output = (attended + out_sum.reshape(256, width)).astype(BF)
    grad_query_gain, grad_key_gain = head_gains[0], head_gains[1]
    g_in = in_sum.reshape(256, width).astype(F32)
    x_own = tok.reshape(256, width).astype(F32)
    r1 = lax.rsqrt(jnp.mean(x_own * x_own, axis=-1, keepdims=True) + 1e-06)
    n1 = g_in * g_attn_gain
    grad_attn_gain = jnp.sum(g_in * x_own * r1, axis=0)
    grad_tokens = (
        g_attended
        + r1 * n1
        - x_own * (r1 * r1 * r1) * jnp.mean(n1 * x_own, axis=-1, keepdims=True)
    )

    small_terms = jnp.concatenate(
        [
            grad_attn_gain.reshape(16, 64),
            grad_ffn_gain.reshape(16, 64),
            grad_query_gain.reshape(16, 8),
            grad_key_gain.reshape(16, 8),
            jnp.zeros((16, 512 - 144), F32),
        ],
        axis=1,
    ).astype(BF)
    small_terms = jnp.broadcast_to(small_terms[:, None], (16, 16, 512))

    def terms_body(net, a, n, b, g, u, d, oa, on, ob, og, ou, od):
        return [
            scatter_samples(net, lambda place: a.at[chunk_of(place)], oa),
            scatter_samples(net, lambda place: n.at[chunk_of(place)], on),
            scatter_samples(net, lambda place: b.at[place["yl"], chip_of(place)], ob),
            scatter_copies(net, g, u, d, og, ou, od),
        ]

    ta, tn, tb, tg, tu, td = comm_call(
        terms_body,
        SAMPLE_SHIFTS + COPY_SHIFTS,
        [
            ((16, 64, 512), BF),
            ((16, 16, 512), BF),
            ((16, 16, width), BF),
            ((16, 64, 384), BF),
            ((16, 64, 384), BF),
            ((16, 192, 128), BF),
        ],
        [],
        6,
        [False] * 6,
        [False] * 6,
        96,
        8,
    )(
        dwqkv,
        small_terms,
        dwo,
        grad_gate_part.reshape(16, 64, 384),
        grad_up_part.reshape(16, 64, 384),
        grad_down_part.reshape(2, 192, width),
    )

    def summed(t):
        return jnp.sum(t.astype(F32), axis=0).astype(BF)

    def spread_body(net, a, n, b, g, u, d, oa, on, ob, og, ou, od, ma, mn, mb_, mo, mg, mu, md):
        def heads(src, mid, out):
            return spread(net, src, mid, HEAD_SHIFTS, head_of, lambda: swap_task(net, mid, out))

        def swap_out():
            return swap_task(net, mo, ob)

        return [
            spread(
                net, b, mb_, HEAD_SHIFTS, head_of, lambda: exchange_chips(net, mb_, mo, swap_out)
            ),
            spread(net, g, mg, CTX_SHIFTS, ctx_of, lambda: exchange_tp(net, mg, og)),
            spread(net, u, mu, CTX_SHIFTS, ctx_of, lambda: exchange_tp(net, mu, ou)),
            spread_down(net, d, md, od),
            heads(a, ma, oa),
            heads(n, mn, on),
        ]

    sa_, sn_, sb_, sg_, su_, sd_, *_ = comm_call(
        spread_body,
        CTX_SHIFTS + CHIP_SHIFTS + TP_SHIFTS + HEAD_SHIFTS + PLANE_SHIFTS + RING_Z,
        [
            ((8, 64, 512), BF),
            ((8, 16, 512), BF),
            ((8, 16, width), BF),
            ((64, 3072), BF),
            ((64, 3072), BF),
            ((192, width), BF),
            ((8, 64, 512), BF),
            ((8, 16, 512), BF),
            ((8, 16, width), BF),
            ((8, 16, width), BF),
            ((8, 64, 384), BF),
            ((8, 64, 384), BF),
            ((192, 128), BF),
        ],
        [],
        7,
        [False] * 6,
        [False] * 13,
        80,
        20,
    )(summed(ta), summed(tn), summed(tb), summed(tg), summed(tu), summed(td))

    qkv_grad = sa_.astype(F32)
    grad_w_query = qkv_grad[:, :, :256].transpose(1, 0, 2).reshape(64, 2048)
    grad_w_key = qkv_grad[:, :, 256:384].transpose(1, 0, 2).reshape(64, 1024)
    grad_w_value = qkv_grad[:, :, 384:].transpose(1, 0, 2).reshape(64, 1024)
    gains = jnp.sum(sn_[:, 0].astype(F32), axis=0)
    grad_w_out = sb_.astype(F32).reshape(128, width)
    grad_w_gate, grad_w_up, grad_w_down = (t.astype(F32) for t in (sg_, su_, sd_))
    return (
        output.reshape(2, 1, 128, width),
        grad_tokens.reshape(2, 1, 128, width),
        gains[:64],
        grad_w_query,
        grad_w_key,
        grad_w_value,
        gains[128:136],
        gains[136:144],
        grad_w_out,
        gains[64:128],
        grad_w_gate,
        grad_w_up,
        grad_w_down,
    )


def solution(mesh):
    placed = (
        P(None, "fsdp", "ctx", None),
        P(None, "fsdp", "ctx", None),
        P(),
        P(None, "fsdp", None),
        P(None, "fsdp", "ctx"),
        P("fsdp"),
        P("fsdp", None),
        P("fsdp", None),
        P("fsdp", None),
        P("fsdp"),
        P("fsdp"),
        P("fsdp", None),
        P("fsdp"),
        P("fsdp", None),
        P("fsdp", None),
        P("fsdp", None),
    )
    return jax.shard_map(
        per_device,
        mesh=mesh,
        in_specs=placed,
        out_specs=(
            P(None, "fsdp", "ctx", None),
            P(None, "fsdp", "ctx", None),
            P("fsdp"),
            P("fsdp", None),
            P("fsdp", None),
            P("fsdp", None),
            P("fsdp"),
            P("fsdp"),
            P("fsdp", None),
            P("fsdp"),
            P("fsdp", None),
            P("fsdp", None),
            P("fsdp", None),
        ),
        check_vma=False,
    )
```

```python
import functools
import math

import jax
import jax.numpy as jnp
from jax import lax
from jax.experimental import pallas as pl
from jax.experimental.pallas import tpu as pltpu
from jax.sharding import PartitionSpec as P

MESH = pl.DeviceIdType.MESH
SIZES = {"z": 4, "yl": 2, "yh": 2, "x": 4, "core": 2}
BF = jnp.bfloat16
F32 = jnp.float32
HEAD = 128


def my_place():
    c = lax.axis_index("ctx")
    f = lax.axis_index("fsdp")
    return {"z": c // 2, "yl": c % 2, "yh": f // 8, "x": (f // 2) % 4, "core": f % 2}


def moved(me, shift):
    to = dict(me)
    for axis, step in shift.items():
        to[axis] = (me[axis] + (step % SIZES[axis])) % SIZES[axis]
    return to


def ctx_of(place):
    return place["z"] * 2 + place["yl"]


def tp_of(place):
    return place["x"] * 2 + place["core"]


def chip_of(place):
    return place["yh"] * 4 + place["x"]


def head_of(place):
    return place["z"] * 2 + place["core"]


def fsdp_of(place):
    return chip_of(place) * 2 + place["core"]


def device_of(place):
    return (ctx_of(place), fsdp_of(place))


CTX_SHIFTS = [{"z": a, "yl": b} for a in range(4) for b in range(2) if a or b]
PLANE_SHIFTS = [
    {"yh": a, "x": b, "core": d}
    for a in range(2)
    for b in range(4)
    for d in range(2)
    if a or b or d
]
CHIP_SHIFTS = [{"yh": a, "x": b} for a in range(2) for b in range(4) if a or b]
TP_SHIFTS = [{"x": b, "core": d} for b in range(4) for d in range(2) if b or d]
COPY_SHIFTS = [
    {"z": a, "yl": b, "yh": d}
    for a in range(4)
    for b in range(2)
    for d in range(2)
    if a or b or d
]
WEIGHT_PLANE = [
    {"yh": a, "yl": a, "x": b, "core": d}
    for a in range(2)
    for b in range(4)
    for d in range(2)
    if a or b or d
]
WEIGHT_CHIPS = [{"yh": a, "yl": a, "x": b} for a in range(2) for b in range(4) if a or b]
SAMPLE_SHIFTS = [
    {"yh": a, "yl": b, "x": d}
    for a in range(2)
    for b in range(2)
    for d in range(4)
    if a or b or d
]
HEAD_SHIFTS = [{"z": a, "core": b} for a in range(4) for b in range(2) if a or b]
Y_SHIFTS = [{"yl": 1}, {"yh": 1}, {"yl": 1, "yh": 1}]
RING_Z = [{"z": 1}, {"z": 3}, {"core": 1}, {"yl": 1, "core": 1}]
RING_X = [{"x": 1}, {"x": 3}, {"core": 1}]


def back(shift):
    return {axis: -step for axis, step in shift.items()}


class Net:
    def __init__(self, send_sems, recv_sems, local_sems):
        self.me = my_place()
        self.send_sems, self.recv_sems, self.local_sems = send_sems, recv_sems, local_sems
        self.count = 0
        self.locals = 0
        self.pending = []

    def enter(self, shifts):
        barrier = pltpu.get_barrier_semaphore()
        for shift in shifts:
            pl.semaphore_signal(
                barrier, inc=1, device_id=device_of(moved(self.me, shift)), device_id_type=MESH
            )
        pl.semaphore_wait(barrier, len(shifts))

    def send(self, src, dst, **shift):
        at = self.count
        self.count += 1
        copy = pltpu.make_async_remote_copy(
            src_ref=src,
            dst_ref=dst,
            send_sem=self.send_sems.at[at],
            recv_sem=self.recv_sems.at[at],
            device_id=device_of(moved(self.me, shift)),
            device_id_type=MESH,
        )
        copy.start()
        self.pending.append(copy.wait_send)
        return copy

    def spare(self):
        self.locals += 1
        return self.local_sems.at[self.locals - 1]

    def settle(self, copy):
        copy.wait()
        self.pending.remove(copy.wait)

    def local(self, src, dst):
        copy = pltpu.make_async_copy(src, dst, self.local_sems.at[self.locals])
        self.locals += 1
        copy.start()
        self.pending.append(copy.wait)
        return copy

    def swap(self, src, dst):
        return Swap(self, src, dst)

    def finish(self):
        for wait in self.pending:
            wait()


class Swap:
    def __init__(self, net, src, dst):
        me = net.me
        self.away = me["yl"] != me["core"]
        at = net.count
        net.count += 1
        self.remote = pltpu.make_async_remote_copy(
            src_ref=src,
            dst_ref=dst,
            send_sem=net.send_sems.at[at],
            recv_sem=net.recv_sems.at[at],
            device_id=device_of(moved(me, {"yl": 1, "core": 1})),
            device_id_type=MESH,
        )
        self.near = pltpu.make_async_copy(src, dst, net.spare())
        pl.when(self.away)(self.remote.start)
        pl.when(jnp.logical_not(self.away))(self.near.start)

    def wait(self):
        pl.when(self.away)(self.remote.wait)
        pl.when(jnp.logical_not(self.away))(self.near.wait)


def run_tasks(tasks):
    tasks = list(tasks)
    while tasks:
        left = []
        for task in tasks:
            try:
                next(task)
                left.append(task)
            except StopIteration:
                pass
        tasks = left


def unique(shifts):
    seen, out = set(), []
    for shift in shifts:
        key = tuple(sorted((k, v) for k, v in shift.items() if v))
        if key not in seen:
            seen.add(key)
            out.append(shift)
    return out


def comm_call(body, shifts, outs, scratch, cid, in_vmem, out_vmem, n_remote, n_local=1):
    shifts = unique(shifts)

    def kernel(*refs):
        refs, sems = refs[:-3], refs[-3:]
        net = Net(*sems)
        net.enter(shifts)
        drain(*(body(net, *refs) or ()))
        net.finish()

    vm = pl.BlockSpec(memory_space=pltpu.VMEM)
    hb = pl.BlockSpec(memory_space=pl.ANY)
    return pl.pallas_call(
        kernel,
        out_shape=[jax.ShapeDtypeStruct(s, d) for s, d in outs],
        in_specs=[vm if v else hb for v in in_vmem],
        out_specs=[vm if v else hb for v in out_vmem],
        scratch_shapes=list(scratch)
        + [
            pltpu.SemaphoreType.DMA((n_remote,)),
            pltpu.SemaphoreType.DMA((n_remote,)),
            pltpu.SemaphoreType.DMA((n_local,)),
        ],
        compiler_params=pltpu.CompilerParams(
            collective_id=cid, has_side_effects=True, vmem_limit_bytes=62 << 20
        ),
    )


def drain(*tasks):
    run_tasks(tasks)


def step(task):
    next(task, None)


def gather_ring(net, axis, src, block, rows, pair="core"):
    me = net.me
    half = rows // 2
    low, high = (0, half), (half, half)

    def at(step, part=(0, rows)):
        return block(moved(me, {axis: step}), *part)

    def cut(part):
        return src.at[..., pl.ds(*part), :]

    def send(step, part, shift):
        here = cut(part) if step == 0 else at(step, part)
        return net.send(here, at(step, part), **shift)

    right, left, other = {axis: 1}, {axis: -1}, {pair: 1}
    r0 = send(0, low, right)
    l1 = send(0, high, left)
    r1 = send(0, high, right)
    l0 = send(0, low, left)
    own = send(0, (0, rows), other)
    yield
    r0.wait_recv()
    fr = send(-1, low, right)
    l1.wait_recv()
    fl = send(1, high, left)
    yield
    r1.wait_recv()
    cr = send(-1, (0, rows), other)
    l0.wait_recv()
    cl = send(1, (0, rows), other)
    yield
    fr.wait_recv()
    c2r = send(2, low, other)
    fl.wait_recv()
    c2l = send(2, high, other)
    yield
    for copy in (own, cr, cl, c2r, c2l):
        copy.wait_recv()


def add_rows(dst, terms, rows, step=32):
    def one(i, carry):
        at = pl.ds(pl.multiple_of(i * step, step), step)
        total = terms[0][at, :].astype(F32)
        for term in terms[1:]:
            total = total + term[at, :].astype(F32)
        dst[at, :] = total.astype(dst.dtype)
        return carry

    lax.fori_loop(0, rows // step, one, 0)


def reduce_ring(net, axis, part, index, total, rc, s, rh, r):
    me = net.me
    low, high = pl.ds(0, 64), pl.ds(64, 64)
    right, left, other = {axis: 1}, {axis: -1}, {"core": 1}

    def at(step, core, rows=pl.ds(0, 128)):
        return part.at[index(moved(me, {axis: step, "core": core})), rows]

    cc = {}
    for step in (2, 1, 3, 0):
        cc[step] = net.send(at(step, 1), rc.at[step], **other)
    yield
    cc[2].wait_recv()
    add_rows(s.at[2], [at(2, 0), rc.at[2]], 128)
    h_r = net.send(s.at[2, low], rh.at[0], **right)
    h_l = net.send(s.at[2, high], rh.at[1], **left)
    cc[1].wait_recv()
    add_rows(s.at[1, high], [at(1, 0, high), rc.at[1, high]], 64)
    r_high = net.send(s.at[1, high], r.at[0, high], **right)
    cc[3].wait_recv()
    add_rows(s.at[3, low], [at(3, 0, low), rc.at[3, low]], 64)
    l_low = net.send(s.at[3, low], r.at[1, low], **left)
    yield
    h_r.wait_recv()
    add_rows(s.at[1, low], [at(1, 0, low), rc.at[1, low], rh.at[0]], 64)
    r_low = net.send(s.at[1, low], r.at[0, low], **right)
    h_l.wait_recv()
    add_rows(s.at[3, high], [at(3, 0, high), rc.at[3, high], rh.at[1]], 64)
    l_high = net.send(s.at[3, high], r.at[1, high], **left)
    yield
    for copy in (cc[0], r_high, l_low, r_low, l_high):
        copy.wait_recv()
    add_rows(total, [at(0, 0), rc.at[0], r.at[0], r.at[1]], 128)


def reduce_ring_scratch(width):
    return [
        pltpu.VMEM((4, 128, width), BF),
        pltpu.VMEM((4, 128, width), BF),
        pltpu.VMEM((2, 64, width), BF),
        pltpu.VMEM((2, 128, width), BF),
    ]


def gather_heads_weights(net, wq, wk, wv, small, stage, out, small_out):
    me = net.me
    mine = fsdp_of(me)
    staged = []
    for core in range(2):
        h = me["z"] * 2 + core
        place = stage.at[core]
        for src, dst in (
            (wq.at[:, pl.ds(pl.multiple_of(h * 256, 256), 256)], place.at[:, pl.ds(0, 256)]),
            (wk.at[:, pl.ds(pl.multiple_of(h * 128, 128), 128)], place.at[:, pl.ds(256, 128)]),
            (wv.at[:, pl.ds(pl.multiple_of(h * 128, 128), 128)], place.at[:, pl.ds(384, 128)]),
        ):
            staged.append(net.local(src, dst))
    yield
    for copy in staged:
        net.settle(copy)
    kept = [
        net.local(stage.at[me["core"]], out.at[mine]),
        net.local(small, small_out.at[mine]),
    ]
    copies = [
        net.send(src, dst, **shift)
        for shift in WEIGHT_PLANE
        for src, dst in (
            (stage.at[moved(me, shift)["core"]], out.at[mine]),
            (small, small_out.at[mine]),
        )
    ]
    yield
    for copy in copies:
        copy.wait_recv()
    for copy in kept:
        net.settle(copy)


def gather_out_weights(net, src, mid, out):
    me = net.me
    mine = chip_of(me)
    stay = net.local(src.at[mine], mid.at[mine])
    first = [
        net.send(src.at[chip_of(moved(me, shift))], mid.at[mine], **shift) for shift in WEIGHT_CHIPS
    ]
    yield
    for copy in first:
        copy.wait_recv()
    net.settle(stay)
    place = out.at[me["core"], mine]
    kept = net.local(mid.at[head_of(me)], place)
    copies = [
        net.send(mid.at[head_of(moved(me, shift))], place, **shift) for shift in WEIGHT_PLANE
    ]
    yield
    for copy in copies:
        copy.wait_recv()
    net.settle(kept)


def pack_columns(src, stage, lane):
    first = lax.broadcasted_iota(jnp.int32, (64, 256), 1) < 64
    for j in range(8):
        low = 192 * j - 64 * (j % 2)
        a = src[:, low : low + 256].astype(F32)
        b = src[:, 1536 + low : 1536 + low + 256].astype(F32)
        if j % 2:
            a = pltpu.roll(a, 192, 1)
        else:
            b = pltpu.roll(b, 64, 1)
        rest = jnp.where(first, jnp.concatenate([a[:, 128:], a[:, 128:]], axis=1), b)
        stage[j, :, lane : lane + 128] = a[:, :128].astype(BF)
        stage[j, :, lane + 128 : lane + 384] = rest.astype(BF)


def gather_ff_weights(net, down, stage, out, down_out):
    me = net.me
    mine = fsdp_of(me)
    kept = [
        net.local(stage.at[tp_of(me)], out.at[mine]),
        net.local(down, down_out.at[me["yh"]]),
    ]
    copies = [net.send(down, down_out.at[me["yh"]], yh=1, yl=1)]
    copies += [
        net.send(stage.at[tp_of(moved(me, shift))], out.at[mine], **shift) for shift in WEIGHT_PLANE
    ]
    yield
    for copy in copies:
        copy.wait_recv()
    for copy in kept:
        net.settle(copy)


def chunk_of(place):
    return chip_of(place) * 2 + place["yl"]


def scatter_samples(net, pick, out):
    me = net.me
    mine = chunk_of(me)
    kept = net.local(pick(me), out.at[mine])
    copies = [net.send(pick(moved(me, shift)), out.at[mine], **shift) for shift in SAMPLE_SHIFTS]
    yield
    for copy in copies:
        copy.wait_recv()
    net.settle(kept)


def reduce_ff(net, g, d, rhg, rhd, sg, sd, rg, rd, tg, td, yg, yd, gsum, dsum):
    me = net.me
    z = [(me["z"] + k) % 4 for k in range(4)]
    ring = ({"z": 1}, {"z": -1})
    half = [
        [
            net.send(g.at[h, z[2]], rhg.at[h], **ring[h]),
            net.send(d.at[z[2], h], rhd.at[h], **ring[h]),
        ]
        for h in range(2)
    ]
    near = [
        net.send(g.at[1, z[1]], rg.at[0, 1], **ring[0]),
        net.send(d.at[z[1], 1], rd.at[0, 1], **ring[0]),
        net.send(g.at[0, z[3]], rg.at[1, 0], **ring[1]),
        net.send(d.at[z[3], 0], rd.at[1, 0], **ring[1]),
    ]
    yield
    for h, to in ((0, z[1]), (1, z[3])):
        for copy in half[h]:
            copy.wait_recv()
        add_rows(sg.at[h], [g.at[h, to], rhg.at[h]], 128)
        add_rows(sd.at[h], [d.at[to, h], rhd.at[h]], 192)
        near.append(net.send(sg.at[h], rg.at[h, h], **ring[h]))
        near.append(net.send(sd.at[h], rd.at[h, h], **ring[h]))
    yield
    for copy in near:
        copy.wait_recv()
    for h in range(2):
        add_rows(tg.at[h], [g.at[h, z[0]], rg.at[0, h], rg.at[1, h]], 128)
        for l in range(2):
            at = pl.ds(128 * l, 128)
            terms = [d.at[z[0], h, :, at], rd.at[0, h, :, at], rd.at[1, h, :, at]]
            add_rows(td.at[h, l], terms, 192)
    copies = []
    for k, shift in enumerate(Y_SHIFTS):
        to = moved(me, shift)
        rows = pl.ds(pl.multiple_of(to["yl"] * 64, 64), 64)
        copies.append(net.send(tg.at[to["yh"], rows], yg.at[k], **shift))
        copies.append(net.send(td.at[to["yh"], to["yl"]], yd.at[k], **shift))
    yield
    for copy in copies:
        copy.wait_recv()
    rows = pl.ds(pl.multiple_of(me["yl"] * 64, 64), 64)
    add_rows(gsum, [tg.at[me["yh"], rows]] + [yg.at[k] for k in range(3)], 64)
    add_rows(dsum, [td.at[me["yh"], me["yl"]]] + [yd.at[k] for k in range(3)], 192)


def reduce_ff_scratch():
    shapes = [(128, 768), (192, 256)]
    out = [pltpu.VMEM((2,) + s, BF) for s in shapes]
    out += [pltpu.VMEM((2,) + s, BF) for s in shapes]
    out += [pltpu.VMEM((2, 2) + s, BF) for s in shapes]
    out += [pltpu.VMEM((2, 128, 768), BF), pltpu.VMEM((2, 2, 192, 128), BF)]
    out += [pltpu.VMEM((3, 64, 768), BF), pltpu.VMEM((3, 192, 128), BF)]
    out += [pltpu.VMEM((64, 768), BF), pltpu.VMEM((192, 128), BF)]
    return out


def exchange(net, src, out, shifts, index):
    me = net.me
    mine = index(me)
    kept = net.local(src.at[mine], out.at[mine])
    copies = [net.send(src.at[index(moved(me, shift))], out.at[mine], **shift) for shift in shifts]
    yield
    for copy in copies:
        copy.wait_recv()
    net.settle(kept)


def sum_everywhere(net, own, first, middle, second, total):
    stages = ((own, first, TP_SHIFTS, middle), (middle, second, COPY_SHIFTS, total))
    for src, slots, shifts, dst in stages:
        copies = [net.send(src, slots.at[k], **shift) for k, shift in enumerate(shifts)]
        yield
        for copy in copies:
            copy.wait_recv()
        dst[...] = src[...] + jnp.sum(slots[...], axis=0)


def rope_tables(where_at):
    frequency = jnp.exp(
        jnp.arange(0, HEAD // 2, dtype=F32) * (-2.0 * math.log(1000000.0) / HEAD)
    )
    angles = where_at.astype(F32)[..., None] * frequency
    cos, sin = jnp.cos(angles), jnp.sin(angles)
    return jnp.concatenate([cos, cos], axis=-1), jnp.concatenate([-sin, sin], axis=-1)


def across_rows(a, b):
    return lax.dot_general(a, b, (((0,), (0,)), ((), ())), preferred_element_type=F32)


def against_cols(a, b):
    return lax.dot_general(a, b, (((1,), (1,)), ((), ())), preferred_element_type=F32)


def forward_dot(a, b):
    return jnp.dot(a, b, preferred_element_type=F32)


EXP2_SCALE = HEAD ** (-0.5) * math.log2(math.e)


def norm_scale(v):
    return lax.rsqrt(jnp.mean(v * v, axis=-1, keepdims=True) + 1e-06)


def visible_tile(lk, lq, sq):
    later = jnp.where(lk < 512, 4096, lk)
    later, lk = jnp.concatenate([later, later], axis=1), jnp.concatenate([lk, lk], axis=1)
    return (lk <= lq) & (later >= sq)


def half_loop(body, part, parts, count):
    lax.fori_loop(part * count // parts, (part + 1) * count // parts, body, 0)


class Front:
    def __init__(self, m, gains, wqkv, wo, xs, tables, saved, part, mixed, vt):
        self.gains, self.wqkv, self.wo, self.xs = gains, wqkv, wo, xs.at[m]
        self.cos, self.sin, self.lk, self.lq, self.sq = (t.at[m] for t in tables)
        self.xn, self.raw, self.q, self.k, self.v, self.mixt, self.rl = (t.at[m] for t in saved)
        self.part, self.mixed, self.vt = part.at[m], mixed, vt

    def project(self, i, carry):
        rows = pl.ds(pl.multiple_of(i * 256, 256), 256)
        x = self.xs[pl.ds(i * 2, 2)].reshape(256, 1024).astype(F32)
        low = (x * norm_scale(x) * self.gains[0:1, :]).astype(BF)
        self.xn[rows, :] = low
        y = forward_dot(low, self.wqkv[:, pl.ds(0, 64), :].reshape(1024, 512))
        self.raw[rows, :] = y[:, :384]
        c, s = self.cos[rows, :], self.sin[rows, :]
        for head in range(3):
            u = y[:, head * HEAD : (head + 1) * HEAD]
            lane = HEAD * (head // 2)
            n = u * norm_scale(u) * self.gains[2:3, lane : lane + HEAD]
            turned = (n * c + pltpu.roll(n, HEAD // 2, 1) * s).astype(BF)
            if head < 2:
                self.q[head, rows, :] = turned
            else:
                self.k[rows, :] = turned
        value = y[:, 384:]
        self.v[rows, :] = value.astype(BF)
        self.vt[:, rows] = value.T.astype(BF)
        return carry

    def attend(self, head, i, carry):
        rows = pl.ds(pl.multiple_of(i * 256, 256), 256)
        s = against_cols(self.k[...], self.q[head, rows, :])
        seen = visible_tile(self.lk[...], self.lq[:, rows], self.sq[:, rows])
        e = jnp.where(seen, jnp.exp2(s * EXP2_SCALE), 0.0)
        inv = 1.0 / jnp.sum(e, axis=0, keepdims=True)
        self.rl[head, :, rows] = inv
        m = forward_dot(self.vt[...], e.astype(BF)) * inv
        self.mixt[head * HEAD : (head + 1) * HEAD, rows] = m.astype(BF)
        self.mixed[rows, head * HEAD : (head + 1) * HEAD] = m.T.astype(BF)
        return carry

    def project_out(self, i, carry):
        rows = pl.ds(pl.multiple_of(i * 256, 256), 256)
        y = forward_dot(self.mixed[rows, :], self.wo[...].reshape(256, 1024)).astype(BF)
        self.part[pl.ds(i * 2, 2)] = y.reshape(2, 128, 1024)
        return carry

    def pieces(self):
        return (
            [functools.partial(half_loop, self.project, p, 2, 4) for p in range(2)]
            + [
                functools.partial(half_loop, functools.partial(self.attend, head), p, 2, 4)
                for head in range(2)
                for p in range(2)
            ]
            + [functools.partial(half_loop, self.project_out, 0, 1, 4)]
        )


def sequence_block(out):
    def block(place, lo, n):
        return out.at[head_of(place), pl.ds(lo, n)]

    return block


def front_body(
    net,
    tok, cot, small, wq, wk, wv, wo_in, wg, wu, wd, cos, sin, lk, lq, sq,
    attended, normed, gains, wqkv, wo, cots, wgu, wds, mid,
    xn_out, raw_out, q_out, k_out, v_out, mixt_out, rl_out,
    xn, raw, q, k, v, mixt, rl,
    xs, part, mixed, vt, stage, smalls, gu_stage, outbox, inbox, *bufs,
):
    me = net.me
    heads = gather_heads_weights(net, wq, wk, wv, small, stage, wqkv, smalls)
    next(heads)
    swaps = [net.swap(tok.at[m], xs.at[m, ctx_of(me)]) for m in range(2)]
    gather = [
        gather_ring(net, "z", xs.at[m, head_of(me)], sequence_block(xs.at[m]), 128)
        for m in range(2)
    ]
    outs = gather_out_weights(net, wo_in, mid, wo)
    feed = gather_ff_weights(net, wd, gu_stage, wgu, wds)

    def cot_block(place, lo, n):
        return cots.at[:, tp_of(place), pl.ds(lo, n)]

    cots_in = gather_ring(net, "x", cot, cot_block, 128)
    own_cot = net.local(cot, cots.at[:, tp_of(me)])
    next(heads)
    swaps[0].wait()
    next(gather[0])
    next(outs)
    pack_columns(wg, gu_stage, 0)
    pack_columns(wu, gu_stage, 384)
    next(gather[0])
    swaps[1].wait()
    next(gather[1])
    next(gather[0])
    drain(gather[0])
    drain(heads)
    next(cots_in)
    next(outs)
    pairs = [smalls[2 * i].astype(F32) + smalls[2 * i + 1].astype(F32) for i in range(8)]
    both = sum(pairs[1:], pairs[0])
    gains[...] = jnp.zeros_like(gains)
    gains[0:1, :] = jnp.concatenate([p[0:1] for p in pairs], axis=1)
    gains[1:2, :] = jnp.concatenate([p[1:2] for p in pairs], axis=1)
    gains[2:3, : 2 * HEAD] = jnp.concatenate([both[2:3], both[3:4]], axis=1)
    tables = (cos, sin, lk, lq, sq)
    saved = (xn, raw, q, k, v, mixt, rl)
    work = [
        Front(m, gains, wqkv, wo, xs, tables, saved, part, mixed, vt).pieces() for m in range(2)
    ]

    def save(m):
        for src, dst in zip(saved, (xn_out, raw_out, q_out, k_out, v_out, mixt_out, rl_out)):
            net.local(src.at[m], dst.at[m])

    def settle(m):
        x = tok[m].astype(F32) + inbox[m].astype(F32)
        attended[m] = x
        normed[m] = (x * norm_scale(x) * gains[1:2, :]).astype(BF)

    for at, piece in enumerate(work[0][:-1]):
        piece()
        step(gather[1])
        if at == 3:
            drain(outs)
    drain(gather[1])
    work[0][-1]()
    reduce0 = reduce_ring(net, "z", part.at[0], head_of, outbox.at[0], *bufs[:4])
    next(reduce0)
    step(cots_in)
    next(feed)
    save(0)
    for at, piece in enumerate(work[1]):
        piece()
        if at in (0, 2, 4):
            step(reduce0)
        if at == 5:
            step(cots_in)
    drain(reduce0)
    back0 = net.swap(outbox.at[0], inbox.at[0])
    reduce1 = reduce_ring(net, "z", part.at[1], head_of, outbox.at[1], *bufs[4:])
    next(reduce1)
    save(1)
    next(reduce1)
    step(cots_in)
    next(reduce1)
    back0.wait()
    settle(0)
    drain(reduce1)
    back1 = net.swap(outbox.at[1], inbox.at[1])
    drain(cots_in)
    drain(feed)
    back1.wait()
    settle(1)


class Feed:
    def __init__(self, m, wgu, wd, nm, ct, hid, ggu, out, mid, dg, dd):
        self.m, self.wgu, self.wd = m, wgu, wd
        self.nm, self.ct, self.hid, self.ggu = nm.at[m], ct.at[m], hid.at[m], ggu.at[m]
        self.out, self.mid, self.dg, self.dd = out.at[m], mid.at[m], dg, dd

    def tile(self, i, carry):
        rows = pl.ds(pl.multiple_of(i * 256, 256), 256)
        blocks = pl.ds(i * 2, 2)
        wgu = self.wgu[...].reshape(1024, 768)
        wd = self.wd[...].reshape(384, 1024)
        y = forward_dot(self.nm[blocks].reshape(256, 1024), wgu)
        gate, up = y[:, :384], y[:, 384:]
        gh = against_cols(self.ct[blocks].reshape(256, 1024), wd)
        sig = 1.0 / (1.0 + jnp.exp(-gate))
        silu = gate * sig
        hidden = (silu * up).astype(BF)
        self.hid[rows, :] = hidden
        gg = (gh * up * sig * (1.0 + gate * (1.0 - sig))).astype(BF)
        gu = (gh * silu).astype(BF)
        self.ggu[rows, :384] = gg
        self.ggu[rows, 384:] = gu
        self.mid[blocks] = (
            against_cols(self.ggu[rows, :], wgu).astype(BF).reshape(2, 128, 1024)
        )
        self.out[blocks] = forward_dot(hidden, wd).astype(BF).reshape(2, 128, 1024)
        return carry

    def pieces(self):
        return [functools.partial(half_loop, self.tile, p, 4, 4) for p in range(4)]

    def in_weights(self):
        def some(i, carry):
            at = pl.ds(pl.multiple_of(i * 128, 128), 128)
            y = across_rows(self.nm[:, :, at].reshape(1024, 128), self.ggu[...])
            self.dg[at, :] = y if self.m == 0 else self.dg[at, :] + y
            return carry

        lax.fori_loop(0, 8, some, 0)

    def down_weights(self):
        def some(i, carry):
            at = pl.ds(pl.multiple_of(i * 128, 128), 128)
            y = across_rows(self.hid[:, at], self.ct[...].reshape(1024, 1024))
            self.dd[at, :] = y if self.m == 0 else self.dd[at, :] + y
            return carry

        lax.fori_loop(0, 3, some, 0)


def feed_body(
    net,
    normed, attended, cot, cots, wgu, wds, gains,
    g_attended, g_attn, gain_sum, dg_low, dd_low, out_part_out,
    nm, hid, ggu, out_part, mid_part, dg, dd, total, *bufs,
):
    me = net.me

    def block(m):
        def at(place, lo, n):
            return nm.at[m, tp_of(place), pl.ds(lo, n)]

        return at

    own = [net.local(normed.at[m], nm.at[m, tp_of(me)]) for m in range(2)]
    gather = [gather_ring(net, "x", normed.at[m], block(m), 128) for m in range(2)]
    next(gather[0])
    next(gather[0])
    next(gather[1])
    for copy in own:
        net.settle(copy)
    drain(gather[0])
    work = [Feed(m, wgu, wds, nm, cots, hid, ggu, out_part, mid_part, dg, dd) for m in range(2)]
    gain_sum[...] = jnp.zeros_like(gain_sum)

    def settle(m):
        x, g_mid = attended[m], total[m]
        r = norm_scale(x)
        n = g_mid * gains[1:2, :]
        gain_sum[0:1, :] += jnp.sum(g_mid * x * r, axis=0, keepdims=True)
        y = cot[m].astype(F32) + r * n - x * (r * r * r) * jnp.mean(n * x, axis=-1, keepdims=True)
        g_attended[m] = y
        g_attn[m] = y.astype(BF)

    for piece in work[0].pieces():
        piece()
        step(gather[1])
    drain(gather[1])
    net.local(out_part.at[0], out_part_out.at[0])
    reduce0 = reduce_ring(net, "x", mid_part.at[0], tp_of, total.at[0], *bufs[:4])
    next(reduce0)
    for at, piece in enumerate(work[1].pieces()):
        piece()
        step(reduce0)
    drain(reduce0)
    net.local(out_part.at[1], out_part_out.at[1])
    reduce1 = reduce_ring(net, "x", mid_part.at[1], tp_of, total.at[1], *bufs[4:])
    next(reduce1)
    settle(0)
    work[0].in_weights()
    next(reduce1)
    work[0].down_weights()
    next(reduce1)
    work[1].in_weights()
    drain(reduce1)
    settle(1)
    work[1].down_weights()
    dg_low[...] = dg[...].astype(BF).reshape(2, 4, 128, 768)
    for j in range(4):
        dd_low[j] = dd[:, 256 * j : 256 * j + 256].astype(BF).reshape(2, 192, 256)


class Back:
    def __init__(self, m, gains, wqkv, wo, g, tables, saved, part, graw, dwqkv, dwo, sums, work):
        self.m, self.gains, self.wqkv, self.wo, self.g = m, gains, wqkv, wo, g.at[m]
        self.cos, self.sin, self.lk, self.lq, self.sq = (t.at[m] for t in tables)
        self.xn, self.raw, self.q, self.k, self.v, self.mixt, self.rl = (t.at[m] for t in saved)
        self.part, self.graw = part.at[m], graw.at[m]
        self.dwqkv, self.dwo, self.sums = dwqkv, dwo, sums
        self.kt, self.dk, self.dv, self.dq = work

    def begin(self):
        self.kt[...] = self.k[...].astype(F32).T.astype(BF)
        self.dk[...] = jnp.zeros_like(self.dk)
        self.dv[...] = jnp.zeros_like(self.dv)

    def attend(self, head, i, carry):
        rows = pl.ds(pl.multiple_of(i * 256, 256), 256)
        at = slice(head * HEAD, (head + 1) * HEAD)
        g = self.g[pl.ds(i * 2, 2)].reshape(256, 1024)
        wo = self.wo[head].reshape(HEAD, 1024)
        gm = against_cols(g, wo).astype(BF)
        gmt = against_cols(wo, g).astype(BF)
        delta = jnp.sum(
            gmt.astype(F32) * self.mixt[at, rows].astype(F32), axis=0, keepdims=True
        )
        qt = self.q[head, rows, :]
        s = against_cols(self.k[...], qt)
        seen = visible_tile(self.lk[...], self.lq[:, rows], self.sq[:, rows])
        p = jnp.where(seen, jnp.exp2(s * EXP2_SCALE), 0.0) * self.rl[head, :, rows]
        dp = forward_dot(self.v[...], gmt)
        ds = (p * (dp - delta)).astype(BF)
        self.dv[...] += forward_dot(p.astype(BF), gm)
        self.dk[...] += forward_dot(ds, qt)
        self.dq[head, rows, :] = forward_dot(self.kt[...], ds).T
        return carry

    def unproject(self, i, carry):
        rows = pl.ds(pl.multiple_of(i * 256, 256), 256)
        c, s = self.cos[rows, :], self.sin[rows, :]
        for head in range(3):
            lane = head // 2
            at = slice(head * HEAD, (head + 1) * HEAD)
            gr = (self.dq[head, rows, :] if head < 2 else self.dk[rows, :]) * HEAD ** (-0.5)
            gu = gr * c - pltpu.roll(gr, HEAD // 2, 1) * s
            u = self.raw[rows, at]
            r = norm_scale(u)
            self.sums[lane : lane + 1, :] += jnp.sum(gu * (u * r), axis=0, keepdims=True)
            n = gu * self.gains[2:3, lane * HEAD : (lane + 1) * HEAD]
            d = r * n - u * (r * r * r) * jnp.mean(n * u, axis=-1, keepdims=True)
            self.graw[rows, at] = d.astype(BF)
        self.graw[rows, 384:] = self.dv[rows, :].astype(BF)
        y = against_cols(self.graw[rows, :], self.wqkv[:, pl.ds(0, 64), :].reshape(1024, 512))
        self.part[pl.ds(i * 2, 2)] = y.astype(BF).reshape(2, 128, 1024)
        return carry

    def pieces(self):
        return (
            [self.begin]
            + [
                functools.partial(half_loop, functools.partial(self.attend, head), p, 2, 4)
                for head in range(2)
                for p in range(2)
            ]
            + [functools.partial(half_loop, self.unproject, p, 2, 4) for p in range(2)]
        )

    def out_weights(self):
        def some(i, carry):
            at = pl.ds(pl.multiple_of(i * 256, 256), 256)
            y = forward_dot(self.mixt[...], self.g[:, :, at].reshape(1024, 256))
            self.dwo[:, at] = y if self.m == 0 else self.dwo[:, at] + y
            return carry

        lax.fori_loop(0, 4, some, 0)

    def head_weights(self):
        def some(i, carry):
            at = pl.ds(pl.multiple_of(i * 256, 256), 256)
            y = across_rows(self.xn[:, at], self.graw[...])
            self.dwqkv[at, :] = y if self.m == 0 else self.dwqkv[at, :] + y
            return carry

        lax.fori_loop(0, 4, some, 0)


def back_body(
    net,
    g_own, tok, gain_sum, dg, dd, out_part_in, xn_in, raw_in, q_in, k_in, v_in, mixt_in, rl_in,
    wqkv, wo, gains, cos, sin, lk, lq, sq,
    in_sum, out_sum, heads_out, outs_out, gu_out, down_out, gain_total,
    xn, raw, q, k, v, mixt, rl,
    g, out_part, part, graw, dwqkv, dwo, kt, dk, dv, dq, outbox, sums,
    qkv_low, wo_low, qkv_in, wo_in, qkv_sum, wo_sum, qkv_all, wo_all, wo_mid, gu_all,
    gain_own, gain_first, gain_middle, gain_second, *bufs,
):
    me = net.me
    ff, bufs = bufs[:12], bufs[12:]
    swaps = [net.swap(g_own.at[m], g.at[m, ctx_of(me)]) for m in range(2)]
    fetched = [net.local(out_part_in.at[0], out_part.at[0])]
    saved = (xn, raw, q, k, v, mixt, rl)
    needed = [
        net.local(src.at[m], dst.at[m])
        for m in range(2)
        for src, dst in zip((xn_in, raw_in, q_in, k_in, v_in, mixt_in, rl_in), saved)
    ]
    fetched.append(net.local(out_part_in.at[1], out_part.at[1]))
    sums[...] = jnp.zeros_like(sums)
    gather = [
        gather_ring(net, "z", g.at[m, head_of(me)], sequence_block(g.at[m]), 128) for m in range(2)
    ]
    outs = [
        reduce_ring(net, "x", out_part.at[m], tp_of, out_sum.at[m], *bufs[4 * m + 8 : 4 * m + 12])
        for m in range(2)
    ]
    gsum, dsum = ff[-2:]

    def feed_gradients():
        yield from reduce_ff(net, dg, dd, *ff)
        kept = [
            net.local(gsum, gu_all.at[ctx_of(me)]),
            net.local(dsum, down_out.at[ctx_of(me)]),
        ]
        spreads = [
            gather_ring(
                net, "z", src, lambda place, lo, n, out=out: out.at[ctx_of(place), pl.ds(lo, n)],
                rows, "yl",
            )
            for src, out, rows in ((gsum, gu_all, 64), (dsum, down_out, 192))
        ]
        for _ in range(4):
            for spread in spreads:
                next(spread)
            yield
        drain(*spreads)
        for copy in kept:
            net.settle(copy)
        yield from exchange(net, gu_all, gu_out, TP_SHIFTS, tp_of)

    feed = feed_gradients()
    swaps[0].wait()
    next(gather[0])
    net.settle(fetched[0])
    next(outs[0])
    next(gather[0])
    swaps[1].wait()
    next(gather[1])
    next(gather[0])
    drain(gather[0])
    next(feed)
    for copy in needed:
        net.settle(copy)
    net.settle(fetched[1])
    tables = (cos, sin, lk, lq, sq)
    work = [
        Back(m, gains, wqkv, wo, g, tables, saved, part, graw, dwqkv, dwo, sums, (kt, dk, dv, dq))
        for m in range(2)
    ]
    for at, piece in enumerate(work[0].pieces()):
        piece()
        step(gather[1])
        if at in (1, 3, 5):
            step(outs[0])
    drain(gather[1])
    reduce0 = reduce_ring(net, "z", part.at[0], head_of, outbox.at[0], *bufs[:4])
    next(reduce0)
    drain(outs[0])
    next(outs[1])
    step(feed)
    for at, piece in enumerate(work[1].pieces()):
        piece()
        if at in (1, 2, 3):
            step(reduce0)
        if at in (2, 4, 6):
            step(outs[1])
        if at in (3, 4, 6):
            step(feed)
    drain(reduce0)
    back0 = net.swap(outbox.at[0], in_sum.at[0])
    reduce1 = reduce_ring(net, "z", part.at[1], head_of, outbox.at[1], *bufs[4:8])
    next(reduce1)
    work[0].out_weights()
    next(reduce1)
    work[1].out_weights()
    work[0].head_weights()
    next(reduce1)
    work[1].head_weights()
    qkv_low[...] = dwqkv[...].astype(BF).reshape(16, 64, 512)
    low = dwo[...].astype(BF)
    for half in range(2):
        wo_low[:, :, half * 16 : half * 16 + 16, :] = low[:, half * 512 : half * 512 + 512].reshape(
            2, 8, 16, 512
        )
    scattered = [
        scatter_samples(net, lambda place: qkv_low.at[chunk_of(place)], qkv_in),
        scatter_samples(net, lambda place: wo_low.at[place["yl"], chip_of(place)], wo_in),
    ]
    for task in scattered:
        next(task)
    step(feed)
    drain(reduce1)
    back1 = net.swap(outbox.at[1], in_sum.at[1])
    drain(outs[1])
    step(feed)
    back0.wait()
    back1.wait()
    row = jnp.zeros((1, 1024), F32)
    for m in range(2):
        x = tok[m].astype(F32)
        row = row + jnp.sum(in_sum[m].astype(F32) * x * norm_scale(x), axis=0, keepdims=True)
    for k in range(8):
        at = slice(k * 128, k * 128 + 128)
        gain_own[k : k + 1, :] = row[:, at]
        gain_own[8 + k : 9 + k, :] = gain_sum[0:1, at]
    gain_own[16:24, :] = sums[...]
    gain = sum_everywhere(net, gain_own, gain_first, gain_middle, gain_second, gain_total)
    next(gain)
    drain(*scattered)
    qkv_sum[...] = jnp.sum(qkv_in[...].astype(F32), axis=0).astype(BF)
    wo_sum[...] = jnp.sum(wo_in[...].astype(F32), axis=0).astype(BF)
    kept = [
        net.local(qkv_sum, qkv_all.at[head_of(me)]),
        net.local(wo_sum, wo_all.at[head_of(me)]),
    ]
    spreads = [
        gather_ring(net, "z", src, sequence_block(out), rows)
        for src, out, rows in ((qkv_sum, qkv_all, 64), (wo_sum, wo_all, 32))
    ]
    for task in spreads:
        next(task)
    step(feed)
    next(gain)
    drain(*spreads)
    for copy in kept:
        net.settle(copy)
    heads_back = net.swap(qkv_all, heads_out)
    drain(exchange(net, wo_all, wo_mid, CHIP_SHIFTS, chip_of))
    outs_back = net.swap(wo_mid, outs_out)
    drain(gain)
    drain(feed)
    heads_back.wait()
    outs_back.wait()


def token_places(block_table, first, seq):
    blocks = block_table.shape[1]
    block = seq // blocks
    logical = (
        jnp.repeat(block_table, block, axis=1) * block + jnp.arange(seq, dtype=jnp.int32) % block
    )
    prompt = seq // 2
    segment = jnp.where(logical < prompt, 0, jnp.where(logical < prompt + first, 1, 2))
    end = jnp.where(segment == 1, prompt - 1 + first, seq - 1)
    position = jnp.where(segment == 0, logical, 895 - (end - logical))
    return logical, segment, position


def per_device(
    tokens,
    cotangent,
    block_table,
    segment_ids,
    positions,
    gain_attn,
    w_query,
    key_projection,
    value_projection,
    query_norm_gain,
    key_norm_gain,
    w_out,
    gain_ffn,
    w_gate,
    w_up,
    w_down,
):
    ctx = lax.axis_index("ctx")
    mbs, width = tokens.shape[0], tokens.shape[-1]
    tok = tokens[:, 0]

    f = lax.axis_index("fsdp")
    here = (jnp.arange(16) == f)[:, None]

    def placed(gain):
        return jnp.where(here, gain[None], jnp.zeros((), BF)).reshape(-1)

    zero = jnp.zeros((64,), BF)
    odd = f % 2 == 1

    def halved(gain):
        return jnp.concatenate([jnp.where(odd, zero, gain), jnp.where(odd, gain, zero)])

    small = jnp.concatenate(
        [
            halved(gain_attn),
            halved(gain_ffn),
            placed(query_norm_gain),
            placed(key_norm_gain),
            jnp.zeros((12 * HEAD,), BF),
        ]
    ).reshape(16, HEAD)
    count = jnp.sum((segment_ids[:, 0] == 1).astype(jnp.int32), axis=1, keepdims=True)
    other = lax.ppermute(count, "fsdp", [(i, i ^ 1) for i in range(16)])
    first = jnp.where(ctx % 2 == f % 2, count, other)
    logical, seg, where_at = token_places(block_table, first, 1024)
    start = jnp.where(seg == 2, 512 + first, 0)
    lk = jnp.broadcast_to(logical[:, :, None], (mbs, 1024, HEAD))
    lq, sq = logical[:, None, :], start[:, None, :]
    cos, sin = rope_tables(where_at)

    vm = pltpu.VMEM
    saves = [
        ((2, 1024, width), BF),
        ((2, 1024, 384), F32),
        ((2, 2, 1024, HEAD), BF),
        ((2, 1024, HEAD), BF),
        ((2, 1024, HEAD), BF),
        ((2, 256, 1024), BF),
        ((2, 2, 1, 1024), F32),
    ]
    sequence = vm((2, 8, 128, width), BF)
    attended, normed, gain_rows, wqkv, wo, cots, wgu, wds, _, *saved = comm_call(
        front_body,
        RING_Z + RING_X + WEIGHT_PLANE,
        [
            ((2, 128, width), F32),
            ((2, 128, width), BF),
            ((8, width), F32),
            ((16, 64, 512), BF),
            ((2, 8, 16, width), BF),
            ((2, 8, 128, width), BF),
            ((16, 64, 768), BF),
            ((2, 192, width), BF),
            ((8, 16, width), BF),
        ]
        + saves,
        [vm(shape, kind) for shape, kind in saves]
        + [sequence, sequence, vm((1024, 256), BF), vm((HEAD, 1024), BF)]
        + [vm((2, 64, 512), BF), vm((16, 16, HEAD), BF), vm((8, 64, 768), BF)]
        + [vm((2, 128, width), BF), vm((2, 128, width), BF)]
        + reduce_ring_scratch(width) * 2,
        0,
        [True] + [False] * 6 + [True] * 2 + [False] + [True] * 5,
        [True] * 5 + [False] * 11,
        160,
        64,
    )(
        tok, cotangent[:, 0], small, w_query, key_projection, value_projection,
        w_out.reshape(8, 16, width), w_gate, w_up, w_down, cos, sin, lk, lq, sq,
    )
    g_attended, g_attn, gain_sum, dg, dd, out_part = comm_call(
        feed_body,
        RING_X,
        [
            ((2, 128, width), F32),
            ((2, 128, width), BF),
            ((8, width), F32),
            ((2, 4, 128, 768), BF),
            ((4, 2, 192, 256), BF),
            ((2, 8, 128, width), BF),
        ],
        [sequence, vm((2, 1024, 384), BF), vm((2, 1024, 768), BF), sequence, sequence]
        + [vm((1024, 768), F32), vm((384, width), F32), vm((2, 128, width), F32)]
        + reduce_ring_scratch(width) * 2,
        1,
        [True] * 7,
        [True] * 5 + [False],
        64,
        8,
    )(normed, attended, cotangent[:, 0], cots, wgu, wds, gain_rows)
    in_sum, out_sum, heads, outs, gu, down, gain_total = comm_call(
        back_body,
        RING_Z + RING_X + [{"yl": 1}] + SAMPLE_SHIFTS + CHIP_SHIFTS + TP_SHIFTS + COPY_SHIFTS,
        [
            ((2, 128, width), BF),
            ((2, 128, width), F32),
            ((8, 64, 512), BF),
            ((8, 32, 512), BF),
            ((8, 64, 768), BF),
            ((8, 192, 128), BF),
            ((24, HEAD), F32),
        ],
        [vm(shape, kind) for shape, kind in saves]
        + [sequence, sequence, sequence, vm((2, 1024, 512), BF)]
        + [vm((1024, 512), F32), vm((256, 1024), F32), vm((HEAD, 1024), BF)]
        + [vm((1024, HEAD), F32), vm((1024, HEAD), F32), vm((2, 1024, HEAD), F32)]
        + [vm((2, 128, width), BF), vm((8, HEAD), F32)]
        + [vm((16, 64, 512), BF), vm((2, 8, 32, 512), BF)]
        + [vm((16, 64, 512), BF), vm((16, 32, 512), BF)]
        + [vm((64, 512), BF), vm((32, 512), BF)]
        + [vm((8, 64, 512), BF), vm((8, 32, 512), BF), vm((8, 32, 512), BF), vm((8, 64, 768), BF)]
        + [vm((24, HEAD), F32), vm((7, 24, HEAD), F32), vm((24, HEAD), F32), vm((15, 24, HEAD), F32)]
        + reduce_ff_scratch()
        + reduce_ring_scratch(width) * 4,
        2,
        [True] * 5 + [False] * 8 + [True] * 8,
        [True] * 2 + [False] * 4 + [True],
        224,
        40,
    )(g_attn, tok, gain_sum, dg, dd, out_part, *saved, wqkv, wo, gain_rows, cos, sin, lk, lq, sq)
    output = (attended + out_sum).astype(BF)
    g_in = in_sum.astype(F32)
    x_own = tok.astype(F32)
    r1 = norm_scale(x_own)
    n1 = g_in * gain_rows[0]
    grad_tokens = (
        g_attended
        + r1 * n1
        - x_own * (r1 * r1 * r1) * jnp.mean(n1 * x_own, axis=-1, keepdims=True)
    )
    qkv_grad = heads.astype(F32)
    grad_w_query = qkv_grad[:, :, :256].transpose(1, 0, 2).reshape(64, 2048)
    grad_w_key = qkv_grad[:, :, 256:384].transpose(1, 0, 2).reshape(64, 1024)
    grad_w_value = qkv_grad[:, :, 384:].transpose(1, 0, 2).reshape(64, 1024)
    grad_w_out = outs.astype(F32).reshape(8, 2, 16, 512).transpose(0, 2, 1, 3).reshape(128, width)

    def columns(part):
        return part.reshape(8, 64, 2, 192).transpose(1, 2, 0, 3).reshape(64, 3072).astype(F32)

    grad_w_gate, grad_w_up = columns(gu[:, :, :384]), columns(gu[:, :, 384:])
    grad_w_down = down.astype(F32).transpose(1, 0, 2).reshape(192, width)

    def mine(rows, n):
        return lax.dynamic_slice_in_dim(rows.reshape(-1), f * n, n)

    gains = [
        mine(gain_total[0:8], 64),
        mine(gain_total[8:16], 64),
        mine(gain_total[16], 8),
        mine(gain_total[17], 8),
    ]
    return (
        output.reshape(2, 1, 128, width),
        grad_tokens.reshape(2, 1, 128, width),
        gains[0],
        grad_w_query,
        grad_w_key,
        grad_w_value,
        gains[2],
        gains[3],
        grad_w_out,
        gains[1],
        grad_w_gate,
        grad_w_up,
        grad_w_down,
    )


def solution(mesh):
    placed = (
        P(None, "fsdp", "ctx", None),
        P(None, "fsdp", "ctx", None),
        P(),
        P(None, "fsdp", None),
        P(None, "fsdp", "ctx"),
        P("fsdp"),
        P("fsdp", None),
        P("fsdp", None),
        P("fsdp", None),
        P("fsdp"),
        P("fsdp"),
        P("fsdp", None),
        P("fsdp"),
        P("fsdp", None),
        P("fsdp", None),
        P("fsdp", None),
    )
    return jax.shard_map(
        per_device,
        mesh=mesh,
        in_specs=placed,
        out_specs=(
            P(None, "fsdp", "ctx", None),
            P(None, "fsdp", "ctx", None),
            P("fsdp"),
            P("fsdp", None),
            P("fsdp", None),
            P("fsdp", None),
            P("fsdp"),
            P("fsdp"),
            P("fsdp", None),
            P("fsdp"),
            P("fsdp", None),
            P("fsdp", None),
            P("fsdp", None),
        ),
        check_vma=False,
    )
```

```python
import functools
import math

import jax
import jax.numpy as jnp
from jax import lax
from jax.experimental import pallas as pl
from jax.experimental.pallas import tpu as pltpu
from jax.sharding import PartitionSpec as P

MESH = pl.DeviceIdType.MESH
SIZES = {"z": 4, "yl": 2, "yh": 2, "x": 4, "core": 2}
BF = jnp.bfloat16
F32 = jnp.float32
HEAD = 128


def my_place():
    c = lax.axis_index("ctx")
    f = lax.axis_index("fsdp")
    return {"z": c // 2, "yl": c % 2, "yh": f // 8, "x": (f // 2) % 4, "core": f % 2}


def moved(me, shift):
    to = dict(me)
    for axis, step in shift.items():
        if axis == "y":
            y = (me["yh"] * 2 + me["yl"] + step % 4) % 4
            to["yh"], to["yl"] = y // 2, y % 2
        else:
            to[axis] = (me[axis] + (step % SIZES[axis])) % SIZES[axis]
    return to


def ctx_of(place):
    return place["z"] * 2 + place["yl"]


def tp_of(place):
    return place["x"] * 2 + place["core"]


def chip_of(place):
    return place["yh"] * 4 + place["x"]


def head_of(place):
    return place["z"] * 2 + place["core"]


def fsdp_of(place):
    return chip_of(place) * 2 + place["core"]


def device_of(place):
    return (ctx_of(place), fsdp_of(place))


CTX_SHIFTS = [{"z": a, "yl": b} for a in range(4) for b in range(2) if a or b]
PLANE_SHIFTS = [
    {"yh": a, "x": b, "core": d}
    for a in range(2)
    for b in range(4)
    for d in range(2)
    if a or b or d
]
CHIP_SHIFTS = [{"yh": a, "x": b} for a in range(2) for b in range(4) if a or b]
TP_SHIFTS = [{"x": b, "core": d} for b in range(4) for d in range(2) if b or d]
COPY_SHIFTS = [
    {"z": a, "yl": b, "yh": d}
    for a in range(4)
    for b in range(2)
    for d in range(2)
    if a or b or d
]
WEIGHT_PLANE = [
    {"yh": a, "yl": a, "x": b, "core": d}
    for a in range(2)
    for b in range(4)
    for d in range(2)
    if a or b or d
]
WEIGHT_CHIPS = [{"yh": a, "yl": a, "x": b} for a in range(2) for b in range(4) if a or b]
SAMPLE_SHIFTS = [
    {"yh": a, "yl": b, "x": d}
    for a in range(2)
    for b in range(2)
    for d in range(4)
    if a or b or d
]
HEAD_SHIFTS = [{"z": a, "core": b} for a in range(4) for b in range(2) if a or b]
RING_Y = [{"y": 1}, {"y": 3}]
RING_Z = [{"z": 1}, {"z": 3}, {"core": 1}, {"yl": 1, "core": 1}]
RING_X = [{"x": 1}, {"x": 3}, {"core": 1}]


def back(shift):
    return {axis: -step for axis, step in shift.items()}


class Net:
    def __init__(self, send_sems, recv_sems, local_sems):
        self.me = my_place()
        self.send_sems, self.recv_sems, self.local_sems = send_sems, recv_sems, local_sems
        self.count = 0
        self.locals = 0
        self.pending = []

    def enter(self, shifts):
        barrier = pltpu.get_barrier_semaphore()
        for shift in shifts:
            pl.semaphore_signal(
                barrier, inc=1, device_id=device_of(moved(self.me, shift)), device_id_type=MESH
            )
        pl.semaphore_wait(barrier, len(shifts))

    def send(self, src, dst, **shift):
        at = self.count
        self.count += 1
        copy = pltpu.make_async_remote_copy(
            src_ref=src,
            dst_ref=dst,
            send_sem=self.send_sems.at[at],
            recv_sem=self.recv_sems.at[at],
            device_id=device_of(moved(self.me, shift)),
            device_id_type=MESH,
        )
        copy.start()
        self.pending.append(copy.wait_send)
        return copy

    def spare(self):
        self.locals += 1
        return self.local_sems.at[self.locals - 1]

    def settle(self, copy):
        copy.wait()
        self.pending.remove(copy.wait)

    def local(self, src, dst):
        copy = pltpu.make_async_copy(src, dst, self.local_sems.at[self.locals])
        self.locals += 1
        copy.start()
        self.pending.append(copy.wait)
        return copy

    def swap(self, src, dst):
        return Swap(self, src, dst)

    def finish(self):
        for wait in self.pending:
            wait()


class Swap:
    def __init__(self, net, src, dst):
        me = net.me
        self.away = me["yl"] != me["core"]
        at = net.count
        net.count += 1
        self.remote = pltpu.make_async_remote_copy(
            src_ref=src,
            dst_ref=dst,
            send_sem=net.send_sems.at[at],
            recv_sem=net.recv_sems.at[at],
            device_id=device_of(moved(me, {"yl": 1, "core": 1})),
            device_id_type=MESH,
        )
        self.near = pltpu.make_async_copy(src, dst, net.spare())
        pl.when(self.away)(self.remote.start)
        pl.when(jnp.logical_not(self.away))(self.near.start)

    def wait(self):
        pl.when(self.away)(self.remote.wait)
        pl.when(jnp.logical_not(self.away))(self.near.wait)


def run_tasks(tasks):
    tasks = list(tasks)
    while tasks:
        left = []
        for task in tasks:
            try:
                next(task)
                left.append(task)
            except StopIteration:
                pass
        tasks = left


def unique(shifts):
    seen, out = set(), []
    for shift in shifts:
        key = tuple(sorted((k, v) for k, v in shift.items() if v))
        if key not in seen:
            seen.add(key)
            out.append(shift)
    return out


def comm_call(body, shifts, outs, scratch, cid, in_vmem, out_vmem, n_remote, n_local=1):
    shifts = unique(shifts)

    def kernel(*refs):
        refs, sems = refs[:-3], refs[-3:]
        net = Net(*sems)
        net.enter(shifts)
        drain(*(body(net, *refs) or ()))
        net.finish()

    vm = pl.BlockSpec(memory_space=pltpu.VMEM)
    hb = pl.BlockSpec(memory_space=pl.ANY)
    return pl.pallas_call(
        kernel,
        out_shape=[jax.ShapeDtypeStruct(s, d) for s, d in outs],
        in_specs=[vm if v else hb for v in in_vmem],
        out_specs=[vm if v else hb for v in out_vmem],
        scratch_shapes=list(scratch)
        + [
            pltpu.SemaphoreType.DMA((n_remote,)),
            pltpu.SemaphoreType.DMA((n_remote,)),
            pltpu.SemaphoreType.DMA((n_local,)),
        ],
        compiler_params=pltpu.CompilerParams(
            collective_id=cid, has_side_effects=True, vmem_limit_bytes=62 << 20
        ),
    )


def drain(*tasks):
    run_tasks(tasks)


def step(task):
    next(task, None)


def gather_ring(net, axis, src, block, rows, pair="core"):
    me = net.me
    half = rows // 2
    low, high = (0, half), (half, half)

    def at(step, part=(0, rows)):
        return block(moved(me, {axis: step}), *part)

    def cut(part):
        return at(0, part) if src is None else src.at[..., pl.ds(*part), :]

    def send(step, part, shift):
        here = cut(part) if step == 0 else at(step, part)
        return net.send(here, at(step, part), **shift)

    right, left, other = {axis: 1}, {axis: -1}, {pair: 1}
    r0 = send(0, low, right)
    l1 = send(0, high, left)
    r1 = send(0, high, right)
    l0 = send(0, low, left)
    own = pair and send(0, (0, rows), other)
    yield
    r0.wait_recv()
    fr = send(-1, low, right)
    l1.wait_recv()
    fl = send(1, high, left)
    yield
    if not pair:
        for copy in (r1, l0, fr, fl):
            copy.wait_recv()
        return
    r1.wait_recv()
    cr = send(-1, (0, rows), other)
    l0.wait_recv()
    cl = send(1, (0, rows), other)
    yield
    fr.wait_recv()
    c2r = send(2, low, other)
    fl.wait_recv()
    c2l = send(2, high, other)
    yield
    for copy in (own, cr, cl, c2r, c2l):
        copy.wait_recv()


def add_rows(dst, terms, rows, step=32):
    def one(i, carry):
        at = pl.ds(pl.multiple_of(i * step, step), step)
        total = terms[0][at, :].astype(F32)
        for term in terms[1:]:
            total = total + term[at, :].astype(F32)
        dst[at, :] = total.astype(dst.dtype)
        return carry

    lax.fori_loop(0, rows // step, one, 0)


def reduce_ring(net, axis, part, index, total, rc, rh, r, extra=()):
    me = net.me
    low, high = pl.ds(0, 64), pl.ds(64, 64)
    right, left, other = {axis: 1}, {axis: -1}, {"core": 1}

    def at(step, core, rows=pl.ds(0, 128)):
        return part.at[index(moved(me, {axis: step, "core": core})), rows]

    def add(step, rows, n, *more):
        add_rows(rc.at[step, rows], [at(step, 0, rows), rc.at[step, rows], *more], n)

    cc = {}
    for step in (2, 1, 3, 0):
        cc[step] = net.send(at(step, 1), rc.at[step], **other)
    yield
    cc[2].wait_recv()
    add(2, low, 64)
    h_r = net.send(rc.at[2, low], rh.at[0], **right)
    add(2, high, 64)
    h_l = net.send(rc.at[2, high], rh.at[1], **left)
    cc[1].wait_recv()
    add(1, high, 64)
    r_high = net.send(rc.at[1, high], r.at[0, high], **right)
    cc[3].wait_recv()
    add(3, low, 64)
    l_low = net.send(rc.at[3, low], r.at[1, low], **left)
    yield
    h_r.wait_recv()
    add(1, low, 64, rh.at[0])
    r_low = net.send(rc.at[1, low], r.at[0, low], **right)
    h_l.wait_recv()
    add(3, high, 64, rh.at[1])
    l_high = net.send(rc.at[3, high], r.at[1, high], **left)
    yield
    for copy in (cc[0], r_high, l_low, r_low, l_high):
        copy.wait_recv()
    add_rows(total, [at(0, 0), rc.at[0], r.at[0], r.at[1], *extra], 128)


def reduce_ring_tiles(net, axis, part, index, total, rc, rh, r):
    me = net.me
    low, high = pl.ds(0, 64), pl.ds(64, 64)
    right, left, other = {axis: 1}, {axis: -1}, {"core": 1}

    def at(step, core, rows=pl.ds(0, 128)):
        return part.at[index(moved(me, {axis: step, "core": core})), rows]

    def add(step, rows, n, *more):
        add_rows(rc.at[step, rows], [at(step, 0, rows), rc.at[step, rows], *more], n)

    def over(step):
        return net.send(at(step, 1), rc.at[step], **other)

    c2 = over(2)
    yield
    c1 = over(1)
    c2.wait_recv()
    add(2, low, 64)
    h_r = net.send(rc.at[2, low], rh.at[0], **right)
    add(2, high, 64)
    h_l = net.send(rc.at[2, high], rh.at[1], **left)
    yield
    c3 = over(3)
    c1.wait_recv()
    add(1, high, 64)
    r_high = net.send(rc.at[1, high], r.at[0, high], **right)
    yield
    c0 = over(0)
    c3.wait_recv()
    add(3, low, 64)
    l_low = net.send(rc.at[3, low], r.at[1, low], **left)
    h_r.wait_recv()
    add(1, low, 64, rh.at[0])
    r_low = net.send(rc.at[1, low], r.at[0, low], **right)
    h_l.wait_recv()
    add(3, high, 64, rh.at[1])
    l_high = net.send(rc.at[3, high], r.at[1, high], **left)
    yield
    for copy in (c0, r_high, l_low, r_low, l_high):
        copy.wait_recv()
    add_rows(total, [at(0, 0), rc.at[0], r.at[0], r.at[1]], 128)


TILES = (2, 1, 3, 0)


def reduce_ring_scratch(width):
    return [
        pltpu.VMEM((4, 128, width), BF),
        pltpu.VMEM((2, 64, width), BF),
        pltpu.VMEM((2, 128, width), BF),
    ]


def by_x_then_y(net, pick, out):
    me = net.me
    mine = out.at[me["yh"], tp_of(me), me["yl"]]
    kept = net.local(pick(me), mine)
    copies = [net.send(pick(moved(me, shift)), mine, **shift) for shift in TP_SHIFTS]
    yield
    for copy in copies:
        copy.wait_recv()
    net.settle(kept)

    def block(place, lo, n):
        return out.at[place["yh"], pl.ds(lo, n), place["yl"]]

    yield from gather_ring(net, "y", None, block, 8, None)


def gather_heads_weights(net, wq, wk, wv, small, stage, out, small_out):
    me = net.me
    mine = fsdp_of(me)
    staged = []
    rows = pl.ds(pl.multiple_of(me["yl"] * 32, 32), 32)
    for core in range(2):
        h = me["z"] * 2 + core
        place = stage.at[core]
        for src, n, lane in ((wq, 256, 0), (wk, 128, 256), (wv, 128, 384)):
            columns = src.at[rows, pl.ds(pl.multiple_of(h * n, n), n)]
            staged.append(net.local(columns, place.at[:, pl.ds(lane, n)]))
    yield
    for copy in staged:
        net.settle(copy)
    task = by_x_then_y(net, lambda place: stage.at[place["core"]], out)
    next(task)
    kept = net.local(small, small_out.at[mine])
    copies = [net.send(small, small_out.at[mine], **shift) for shift in WEIGHT_PLANE]
    yield
    yield from task
    for copy in copies:
        copy.wait_recv()
    net.settle(kept)


def gather_out_weights(net, src, mid, out):
    me = net.me
    mine = chip_of(me)
    stay = net.local(src.at[mine], mid.at[mine])
    first = [
        net.send(src.at[chip_of(moved(me, shift))], mid.at[mine], **shift) for shift in WEIGHT_CHIPS
    ]
    yield
    for copy in first:
        copy.wait_recv()
    net.settle(stay)
    place = out.at[me["core"], mine]
    kept = net.local(mid.at[head_of(me)], place)
    copies = [
        net.send(mid.at[head_of(moved(me, shift))], place, **shift) for shift in WEIGHT_PLANE
    ]
    yield
    for copy in copies:
        copy.wait_recv()
    net.settle(kept)


def pack_columns(src, stage, lane):
    first = lax.broadcasted_iota(jnp.int32, (64, 256), 1) < 64
    for j in range(8):
        low = 192 * j - 64 * (j % 2)
        a = src[:, low : low + 256].astype(F32)
        b = src[:, 1536 + low : 1536 + low + 256].astype(F32)
        if j % 2:
            a = pltpu.roll(a, 192, 1)
        else:
            b = pltpu.roll(b, 64, 1)
        rest = jnp.where(first, jnp.concatenate([a[:, 128:], a[:, 128:]], axis=1), b)
        stage[j, :, lane : lane + 128] = a[:, :128].astype(BF)
        stage[j, :, lane + 128 : lane + 384] = rest.astype(BF)


def gather_ff_weights(net, down, stage, out, down_out):
    me = net.me
    rows = pl.ds(pl.multiple_of(me["yl"] * 32, 32), 32)
    task = by_x_then_y(net, lambda place: stage.at[tp_of(place), rows], out)
    next(task)
    kept = net.local(down, down_out.at[me["yh"]])
    copy = net.send(down, down_out.at[me["yh"]], yh=1, yl=1)
    yield
    yield from task
    copy.wait_recv()
    net.settle(kept)


def chunk_of(place):
    return chip_of(place) * 2 + place["yl"]


def scatter_samples(net, pick, out):
    me = net.me
    mine = chunk_of(me)
    kept = net.local(pick(me), out.at[mine])
    copies = [net.send(pick(moved(me, shift)), out.at[mine], **shift) for shift in SAMPLE_SHIFTS]
    yield
    for copy in copies:
        copy.wait_recv()
    net.settle(kept)


def reduce_ff(net, g, d, rhg, rhd, rg, rd, tg, td, zg, zd, gsum, dsum):
    me = net.me
    ring = ({"y": 1}, {"y": -1})
    some = [pl.ds(0, 2), pl.ds(2, 2)]

    def terms(step, h):
        to = moved(me, {"y": step})
        return g.at[to["yh"], some[h], to["yl"]], d.at[to["yh"], to["yl"], some[h]]

    def send(step, h, dst_g, dst_d, to):
        src_g, src_d = terms(step, h)
        return [net.send(src_g, dst_g, **to), net.send(src_d, dst_d, **to)]

    half = [send(2, h, rhg.at[h], rhd.at[h], ring[h]) for h in range(2)]
    near = send(1, 1, rg.at[0, 1], rd.at[0, 1], ring[0])
    near += send(-1, 0, rg.at[1, 0], rd.at[1, 0], ring[1])
    yield
    for h, step in ((0, 1), (1, -1)):
        for copy in half[h]:
            copy.wait_recv()
        own_g, own_d = terms(step, h)
        for k in range(2):
            add_rows(rhg.at[h, k], [own_g.at[k], rhg.at[h, k]], 64)
            add_rows(rhd.at[h, k], [own_d.at[k], rhd.at[h, k]], 192)
        near.append(net.send(rhg.at[h], rg.at[h, h], **ring[h]))
        near.append(net.send(rhd.at[h], rd.at[h, h], **ring[h]))
    yield
    for copy in near:
        copy.wait_recv()
    for h in range(2):
        own_g, own_d = terms(0, h)
        for k in range(2):
            add_rows(tg.at[2 * h + k], [own_g.at[k], rg.at[0, h, k], rg.at[1, h, k]], 64)
            add_rows(td.at[2 * h + k], [own_d.at[k], rd.at[0, h, k], rd.at[1, h, k]], 192)
    copies = []
    for k in range(3):
        to = moved(me, {"z": k + 1})
        copies.append(net.send(tg.at[to["z"]], zg.at[k], z=k + 1))
        copies.append(net.send(td.at[to["z"]], zd.at[k], z=k + 1))
    yield
    for copy in copies:
        copy.wait_recv()
    add_rows(gsum, [tg.at[me["z"]]] + [zg.at[k] for k in range(3)], 64)
    add_rows(dsum, [td.at[me["z"]]] + [zd.at[k] for k in range(3)], 192)


def reduce_ff_scratch():
    shapes = [(64, 768), (192, 128)]
    out = []
    for lead in ((2, 2), (2, 2, 2), (4,), (3,), ()):
        out += [pltpu.VMEM(lead + s, BF) for s in shapes]
    return out


def exchange(net, src, out, shifts, index):
    me = net.me
    mine = index(me)
    kept = net.local(src.at[mine], out.at[mine])
    copies = [net.send(src.at[index(moved(me, shift))], out.at[mine], **shift) for shift in shifts]
    yield
    for copy in copies:
        copy.wait_recv()
    net.settle(kept)


def sum_everywhere(net, own, first, middle, second, total):
    stages = ((own, first, TP_SHIFTS, middle), (middle, second, COPY_SHIFTS, total))
    for src, slots, shifts, dst in stages:
        copies = [net.send(src, slots.at[k], **shift) for k, shift in enumerate(shifts)]
        yield
        for copy in copies:
            copy.wait_recv()
        dst[...] = src[...] + jnp.sum(slots[...], axis=0)


def rope_tables(where_at):
    frequency = jnp.exp(
        jnp.arange(0, HEAD // 2, dtype=F32) * (-2.0 * math.log(1000000.0) / HEAD)
    )
    angles = where_at.astype(F32)[..., None] * frequency
    cos, sin = jnp.cos(angles), jnp.sin(angles)
    return jnp.concatenate([cos, cos], axis=-1), jnp.concatenate([-sin, sin], axis=-1)


def across_rows(a, b):
    return lax.dot_general(a, b, (((0,), (0,)), ((), ())), preferred_element_type=F32)


def against_cols(a, b):
    return lax.dot_general(a, b, (((1,), (1,)), ((), ())), preferred_element_type=F32)


def forward_dot(a, b):
    return jnp.dot(a, b, preferred_element_type=F32)


EXP2_SCALE = HEAD ** (-0.5) * math.log2(math.e)


def norm_scale(v):
    return lax.rsqrt(jnp.mean(v * v, axis=-1, keepdims=True) + 1e-06)


def visible_tile(lk, lq, sq):
    later = jnp.where(lk < 512, 4096, lk)
    later, lk = jnp.concatenate([later, later], axis=1), jnp.concatenate([lk, lk], axis=1)
    return (lk <= lq) & (later >= sq)


def half_loop(body, part, parts, count):
    lax.fori_loop(part * count // parts, (part + 1) * count // parts, body, 0)


class Front:
    def __init__(self, m, gains, wqkv, wo, xs, tables, saved, part, mixed, vt):
        self.gains, self.wqkv, self.wo, self.xs = gains, wqkv, wo, xs.at[m]
        self.cos, self.sin, self.lk, self.lq, self.sq = (t.at[m] for t in tables)
        self.xn, self.raw, self.q, self.k, self.v, self.mixt, self.rl = (t.at[m] for t in saved)
        self.part, self.mixed, self.vt = part.at[m], mixed, vt

    def project(self, i, carry):
        rows = pl.ds(pl.multiple_of(i * 256, 256), 256)
        x = self.xs[pl.ds(i * 2, 2)].reshape(256, 1024).astype(F32)
        low = (x * norm_scale(x) * self.gains[0:1, :]).astype(BF)
        self.xn[rows, :] = low
        y = forward_dot(low, self.wqkv[...].reshape(1024, 512))
        self.raw[rows, :] = y[:, :384]
        c, s = self.cos[rows, :], self.sin[rows, :]
        for head in range(3):
            u = y[:, head * HEAD : (head + 1) * HEAD]
            lane = HEAD * (head // 2)
            n = u * norm_scale(u) * self.gains[2:3, lane : lane + HEAD]
            turned = (n * c + pltpu.roll(n, HEAD // 2, 1) * s).astype(BF)
            if head < 2:
                self.q[head, rows, :] = turned
            else:
                self.k[rows, :] = turned
        value = y[:, 384:]
        self.v[rows, :] = value.astype(BF)
        self.vt[:, rows] = value.T.astype(BF)
        return carry

    def attend(self, head, i, carry):
        rows = pl.ds(pl.multiple_of(i * 256, 256), 256)
        s = against_cols(self.k[...], self.q[head, rows, :])
        seen = visible_tile(self.lk[...], self.lq[:, rows], self.sq[:, rows])
        e = jnp.where(seen, jnp.exp2(s * EXP2_SCALE), 0.0)
        inv = 1.0 / jnp.sum(e, axis=0, keepdims=True)
        self.rl[head, :, rows] = inv
        m = forward_dot(self.vt[...], e.astype(BF)) * inv
        self.mixt[head * HEAD : (head + 1) * HEAD, rows] = m.astype(BF)
        self.mixed[rows, head * HEAD : (head + 1) * HEAD] = m.T.astype(BF)
        return carry

    def project_out(self, i, carry):
        rows = pl.ds(pl.multiple_of(i * 256, 256), 256)
        y = forward_dot(self.mixed[rows, :], self.wo[...].reshape(256, 1024)).astype(BF)
        self.part[pl.ds(i * 2, 2)] = y.reshape(2, 128, 1024)
        return carry

    def projection(self):
        half_loop(self.project, 0, 1, 4)

    def tile(self, i):
        self.attend(0, i, 0)
        self.attend(1, i, 0)
        self.project_out(i, 0)


def sequence_block(out):
    def block(place, lo, n):
        return out.at[head_of(place), pl.ds(lo, n)]

    return block


def front_body(
    net,
    tok, cot, small, wq, wk, wv, wo_in, wg, wu, wd, cos, sin, lk, lq, sq,
    attended, normed, gains, wqkv, wo, cots, wgu, wds, mid,
    xn_out, raw_out, q_out, k_out, v_out, mixt_out, rl_out,
    xn, raw, q, k, v, mixt, rl,
    xs, part, mixed, vt, stage, smalls, gu_stage, outbox, inbox, *bufs,
):
    me = net.me
    heads = gather_heads_weights(net, wq, wk, wv, small, stage, wqkv, smalls)
    next(heads)
    swaps = [net.swap(tok.at[m], xs.at[m, ctx_of(me)]) for m in range(2)]
    gather = [
        gather_ring(net, "z", xs.at[m, head_of(me)], sequence_block(xs.at[m]), 128)
        for m in range(2)
    ]
    outs = gather_out_weights(net, wo_in, mid, wo)
    feed = gather_ff_weights(net, wd, gu_stage, wgu, wds)

    def cot_block(place, lo, n):
        return cots.at[:, tp_of(place), pl.ds(lo, n)]

    cots_in = gather_ring(net, "x", cot, cot_block, 128)
    own_cot = net.local(cot, cots.at[:, tp_of(me)])
    next(heads)
    pack_columns(wg, gu_stage, 0)
    pack_columns(wu, gu_stage, 384)
    next(feed)
    swaps[0].wait()
    next(gather[0])
    next(heads)
    next(outs)
    next(cots_in)
    next(gather[0])
    swaps[1].wait()
    next(gather[1])
    next(heads)
    next(gather[0])
    drain(gather[0])
    drain(heads)
    next(outs)
    next(feed)
    next(cots_in)
    pairs = [smalls[2 * i].astype(F32) + smalls[2 * i + 1].astype(F32) for i in range(8)]
    both = sum(pairs[1:], pairs[0])
    gains[...] = jnp.zeros_like(gains)
    gains[0:1, :] = jnp.concatenate([p[0:1] for p in pairs], axis=1)
    gains[1:2, :] = jnp.concatenate([p[1:2] for p in pairs], axis=1)
    gains[2:3, : 2 * HEAD] = jnp.concatenate([both[2:3], both[3:4]], axis=1)
    tables = (cos, sin, lk, lq, sq)
    saved = (xn, raw, q, k, v, mixt, rl)
    work = [Front(m, gains, wqkv, wo, xs, tables, saved, part, mixed, vt) for m in range(2)]

    def save(m):
        for src, dst in zip(saved, (xn_out, raw_out, q_out, k_out, v_out, mixt_out, rl_out)):
            net.local(src.at[m], dst.at[m])

    def settle(m):
        x = tok[m].astype(F32) + inbox[m].astype(F32)
        attended[m] = x
        normed[m] = (x * norm_scale(x) * gains[1:2, :]).astype(BF)

    def reduce(m):
        buf = bufs[3 * m : 3 * m + 3]
        yield from reduce_ring_tiles(net, "z", part.at[m], head_of, outbox.at[m], *buf)
        swap = net.swap(outbox.at[m], inbox.at[m])
        yield
        swap.wait()
        settle(m)

    reduces = [reduce(m) for m in range(2)]
    work[0].projection()
    step(gather[1])
    drain(outs)
    for k in TILES:
        work[0].tile((me["z"] + k) % 4)
        next(reduces[0])
        step(gather[1])
        if k == 3:
            step(feed)
    step(cots_in)
    drain(gather[1])
    save(0)
    work[1].projection()
    step(reduces[0])
    for at, k in enumerate(TILES):
        work[1].tile((me["z"] + k) % 4)
        next(reduces[1])
        if at == 1:
            drain(reduces[0])
            step(cots_in)
    save(1)
    drain(reduces[1])
    drain(cots_in)
    drain(feed)


class Feed:
    def __init__(self, m, wgu, wd, nm, ct, hid, ggu, out, mid, dg, dd):
        self.m, self.wgu, self.wd = m, wgu, wd
        self.nm, self.ct, self.hid, self.ggu = nm.at[m], ct.at[m], hid.at[m], ggu.at[m]
        self.out, self.mid, self.dg, self.dd = out.at[m], mid.at[m], dg, dd

    def tile(self, i):
        rows = pl.ds(pl.multiple_of(i * 256, 256), 256)
        blocks = pl.ds(i * 2, 2)
        wgu = self.wgu[...].reshape(1024, 768)
        wd = self.wd[...].reshape(384, 1024)
        y = forward_dot(self.nm[blocks].reshape(256, 1024), wgu)
        gate, up = y[:, :384], y[:, 384:]
        gh = against_cols(self.ct[blocks].reshape(256, 1024), wd)
        sig = 1.0 / (1.0 + jnp.exp(-gate))
        silu = gate * sig
        hidden = (silu * up).astype(BF)
        self.hid[rows, :] = hidden
        gg = (gh * up * sig * (1.0 + gate * (1.0 - sig))).astype(BF)
        gu = (gh * silu).astype(BF)
        self.ggu[rows, :384] = gg
        self.ggu[rows, 384:] = gu
        self.mid[blocks] = (
            against_cols(self.ggu[rows, :], wgu).astype(BF).reshape(2, 128, 1024)
        )
        self.out[blocks] = forward_dot(hidden, wd).astype(BF).reshape(2, 128, 1024)

    def in_weights(self):
        def some(i, carry):
            at = pl.ds(pl.multiple_of(i * 128, 128), 128)
            y = across_rows(self.nm[:, :, at].reshape(1024, 128), self.ggu[...])
            self.dg[at, :] = y if self.m == 0 else self.dg[at, :] + y
            return carry

        lax.fori_loop(0, 8, some, 0)

    def down_weights(self):
        def some(i, carry):
            at = pl.ds(pl.multiple_of(i * 128, 128), 128)
            y = across_rows(self.hid[:, at], self.ct[...].reshape(1024, 1024))
            self.dd[at, :] = y if self.m == 0 else self.dd[at, :] + y
            return carry

        lax.fori_loop(0, 3, some, 0)


def feed_body(
    net,
    normed, attended, cot, cots, wgu, wds, gains,
    g_attended, g_attn, gain_sum, dg_low, dd_low, out_part_out,
    nm, hid, ggu, out_part, mid_part, dg, dd, total, *bufs,
):
    me = net.me

    def block(m):
        def at(place, lo, n):
            return nm.at[m, tp_of(place), pl.ds(lo, n)]

        return at

    own = [net.local(normed.at[m], nm.at[m, tp_of(me)]) for m in range(2)]
    gather = [gather_ring(net, "x", normed.at[m], block(m), 128) for m in range(2)]
    next(gather[0])
    next(gather[0])
    next(gather[1])
    for copy in own:
        net.settle(copy)
    drain(gather[0])
    work = [Feed(m, wgu, wds, nm, cots, hid, ggu, out_part, mid_part, dg, dd) for m in range(2)]
    gain_sum[...] = jnp.zeros_like(gain_sum)

    def settle(m):
        x, g_mid = attended[m], total[m]
        r = norm_scale(x)
        n = g_mid * gains[1:2, :]
        gain_sum[0:1, :] += jnp.sum(g_mid * x * r, axis=0, keepdims=True)
        y = cot[m].astype(F32) + r * n - x * (r * r * r) * jnp.mean(n * x, axis=-1, keepdims=True)
        g_attended[m] = y
        g_attn[m] = y.astype(BF)

    def reduce(m):
        buf = bufs[3 * m : 3 * m + 3]
        yield from reduce_ring_tiles(net, "x", mid_part.at[m], tp_of, total.at[m], *buf)
        settle(m)

    reduces = [reduce(m) for m in range(2)]
    for k in TILES:
        work[0].tile((me["x"] + k) % 4)
        next(reduces[0])
        step(gather[1])
    net.local(out_part.at[0], out_part_out.at[0])
    drain(gather[1])
    for at, k in enumerate(TILES):
        work[1].tile((me["x"] + k) % 4)
        next(reduces[1])
        if at == 1:
            drain(reduces[0])
    net.local(out_part.at[1], out_part_out.at[1])
    for one in work:
        one.in_weights()
        one.down_weights()
    drain(reduces[1])
    dg_low[...] = dg[...].astype(BF).reshape(2, 4, 2, 64, 768)
    for c in range(8):
        dd_low[:, c % 2, c // 2] = dd[:, 128 * c : 128 * c + 128].astype(BF).reshape(2, 192, 128)


class Back:
    def __init__(self, m, gains, wqkv, wo, g, tables, saved, part, graw, dwqkv, dwo, sums, work):
        self.m, self.gains, self.wqkv, self.wo, self.g = m, gains, wqkv, wo, g.at[m]
        self.cos, self.sin, self.lk, self.lq, self.sq = (t.at[m] for t in tables)
        self.xn, self.raw, self.q, self.k, self.v, self.mixt, self.rl = (t.at[m] for t in saved)
        self.part, self.graw = part.at[m], graw.at[m]
        self.dwqkv, self.dwo, self.sums = dwqkv, dwo, sums
        self.kt, self.dk, self.dv, self.dq = work

    def begin(self):
        self.kt[...] = self.k[...].astype(F32).T.astype(BF)
        self.dk[...] = jnp.zeros_like(self.dk)
        self.dv[...] = jnp.zeros_like(self.dv)

    def attend(self, head, i, carry):
        rows = pl.ds(pl.multiple_of(i * 256, 256), 256)
        at = slice(head * HEAD, (head + 1) * HEAD)
        g = self.g[pl.ds(i * 2, 2)].reshape(256, 1024)
        wo = self.wo[head].reshape(HEAD, 1024)
        gm = against_cols(g, wo).astype(BF)
        gmt = against_cols(wo, g).astype(BF)
        delta = jnp.sum(
            gmt.astype(F32) * self.mixt[at, rows].astype(F32), axis=0, keepdims=True
        )
        qt = self.q[head, rows, :]
        s = against_cols(self.k[...], qt)
        seen = visible_tile(self.lk[...], self.lq[:, rows], self.sq[:, rows])
        p = jnp.where(seen, jnp.exp2(s * EXP2_SCALE), 0.0) * self.rl[head, :, rows]
        dp = forward_dot(self.v[...], gmt)
        ds = (p * (dp - delta)).astype(BF)
        self.dv[...] += forward_dot(p.astype(BF), gm)
        self.dk[...] += forward_dot(ds, qt)
        self.dq[head, rows, :] = forward_dot(self.kt[...], ds).T
        return carry

    def unproject(self, i, carry):
        rows = pl.ds(pl.multiple_of(i * 256, 256), 256)
        c, s = self.cos[rows, :], self.sin[rows, :]
        for head in range(3):
            lane = head // 2
            at = slice(head * HEAD, (head + 1) * HEAD)
            gr = (self.dq[head, rows, :] if head < 2 else self.dk[rows, :]) * HEAD ** (-0.5)
            gu = gr * c - pltpu.roll(gr, HEAD // 2, 1) * s
            u = self.raw[rows, at]
            r = norm_scale(u)
            self.sums[lane : lane + 1, :] += jnp.sum(gu * (u * r), axis=0, keepdims=True)
            n = gu * self.gains[2:3, lane * HEAD : (lane + 1) * HEAD]
            d = r * n - u * (r * r * r) * jnp.mean(n * u, axis=-1, keepdims=True)
            self.graw[rows, at] = d.astype(BF)
        self.graw[rows, 384:] = self.dv[rows, :].astype(BF)
        y = against_cols(self.graw[rows, :], self.wqkv[...].reshape(1024, 512))
        self.part[pl.ds(i * 2, 2)] = y.astype(BF).reshape(2, 128, 1024)
        return carry

    def pieces(self):
        return (
            [self.begin]
            + [
                functools.partial(half_loop, functools.partial(self.attend, head), p, 2, 4)
                for head in range(2)
                for p in range(2)
            ]
            + [functools.partial(half_loop, self.unproject, p, 2, 4) for p in range(2)]
        )

    def out_weights(self):
        def some(i, carry):
            at = pl.ds(pl.multiple_of(i * 256, 256), 256)
            y = forward_dot(self.mixt[...], self.g[:, :, at].reshape(1024, 256))
            self.dwo[:, at] = y if self.m == 0 else self.dwo[:, at] + y
            return carry

        lax.fori_loop(0, 4, some, 0)

    def head_weights(self):
        def some(i, carry):
            at = pl.ds(pl.multiple_of(i * 256, 256), 256)
            y = across_rows(self.xn[:, at], self.graw[...])
            self.dwqkv[at, :] = y if self.m == 0 else self.dwqkv[at, :] + y
            return carry

        lax.fori_loop(0, 4, some, 0)


def back_body(
    net,
    g_own, tok, gain_sum, dg, dd, out_part_in, xn_in, raw_in, q_in, k_in, v_in, mixt_in, rl_in,
    wqkv, wo, gains, cos, sin, lk, lq, sq,
    in_sum, out_sum, heads_out, outs_out, gu_out, down_out, gain_total,
    xn, raw, q, k, v, mixt, rl,
    g, out_part, part, graw, dwqkv, dwo, kt, dk, dv, dq, outbox, sums,
    qkv_low, wo_low, qkv_in, wo_in, qkv_sum, wo_sum, qkv_all, wo_all, wo_mid, gu_all,
    gain_own, gain_first, gain_middle, gain_second, *bufs,
):
    me = net.me
    ff, bufs = bufs[:10], bufs[10:]
    swaps = [net.swap(g_own.at[m], g.at[m, ctx_of(me)]) for m in range(2)]
    fetched = [net.local(out_part_in.at[0], out_part.at[0])]
    saved = (xn, raw, q, k, v, mixt, rl)
    needed = [
        net.local(src.at[m], dst.at[m])
        for m in range(2)
        for src, dst in zip((xn_in, raw_in, q_in, k_in, v_in, mixt_in, rl_in), saved)
    ]
    fetched.append(net.local(out_part_in.at[1], out_part.at[1]))
    sums[...] = jnp.zeros_like(sums)
    gather = [
        gather_ring(net, "z", g.at[m, head_of(me)], sequence_block(g.at[m]), 128) for m in range(2)
    ]
    outs = [
        reduce_ring(net, "x", out_part.at[m], tp_of, out_sum.at[m], *bufs[3 * m + 6 : 3 * m + 9])
        for m in range(2)
    ]
    gsum, dsum = ff[-2:]

    def feed_gradients():
        yield from reduce_ff(net, dg, dd, *ff)
        kept = [
            net.local(gsum, gu_all.at[ctx_of(me)]),
            net.local(dsum, down_out.at[ctx_of(me)]),
        ]
        spreads = [
            gather_ring(
                net, "z", src, lambda place, lo, n, out=out: out.at[ctx_of(place), pl.ds(lo, n)],
                rows, "yl",
            )
            for src, out, rows in ((gsum, gu_all, 64), (dsum, down_out, 192))
        ]
        for _ in range(4):
            for spread in spreads:
                next(spread)
            yield
        drain(*spreads)
        for copy in kept:
            net.settle(copy)
        yield from exchange(net, gu_all, gu_out, TP_SHIFTS, tp_of)

    feed = feed_gradients()
    swaps[0].wait()
    next(gather[0])
    net.settle(fetched[0])
    next(outs[0])
    next(gather[0])
    swaps[1].wait()
    next(gather[1])
    next(gather[0])
    drain(gather[0])
    next(feed)
    for copy in needed:
        net.settle(copy)
    net.settle(fetched[1])
    tables = (cos, sin, lk, lq, sq)
    work = [
        Back(m, gains, wqkv, wo, g, tables, saved, part, graw, dwqkv, dwo, sums, (kt, dk, dv, dq))
        for m in range(2)
    ]
    for at, piece in enumerate(work[0].pieces()):
        piece()
        step(gather[1])
        if at in (1, 3, 5):
            step(outs[0])
    drain(gather[1])
    def reduce(m):
        yield from reduce_ring(net, "z", part.at[m], head_of, outbox.at[m], *bufs[3 * m : 3 * m + 3])
        swap = net.swap(outbox.at[m], in_sum.at[m])
        yield
        swap.wait()

    reduces = [reduce(m) for m in range(2)]
    next(reduces[0])
    drain(outs[0])
    next(outs[1])
    for at, piece in enumerate(work[1].pieces()):
        piece()
        if at in (1, 3, 5):
            step(reduces[0])
        if at in (2, 4, 6):
            step(outs[1])
        if at in (2, 4, 6):
            step(feed)
    next(reduces[1])
    work[0].head_weights()
    step(reduces[1])
    step(reduces[0])
    work[1].head_weights()
    qkv_low[...] = dwqkv[...].astype(BF).reshape(16, 64, 512)
    scattered = [
        scatter_samples(net, lambda place: qkv_low.at[chunk_of(place)], qkv_in),
        scatter_samples(net, lambda place: wo_low.at[place["yl"], chip_of(place)], wo_in),
    ]
    next(scattered[0])
    step(reduces[1])
    step(feed)
    work[0].out_weights()
    step(reduces[1])
    work[1].out_weights()
    low = dwo[...].astype(BF)
    for half in range(2):
        wo_low[:, :, half * 16 : half * 16 + 16, :] = low[:, half * 512 : half * 512 + 512].reshape(
            2, 8, 16, 512
        )
    next(scattered[1])
    drain(*reduces)
    drain(outs[1])
    step(feed)
    row = jnp.zeros((1, 1024), F32)
    for m in range(2):
        x = tok[m].astype(F32)
        row = row + jnp.sum(in_sum[m].astype(F32) * x * norm_scale(x), axis=0, keepdims=True)
    for k in range(8):
        at = slice(k * 128, k * 128 + 128)
        gain_own[k : k + 1, :] = row[:, at]
        gain_own[8 + k : 9 + k, :] = gain_sum[0:1, at]
    gain_own[16:24, :] = sums[...]
    gain = sum_everywhere(net, gain_own, gain_first, gain_middle, gain_second, gain_total)
    next(gain)
    drain(*scattered)
    qkv_sum[...] = jnp.sum(qkv_in[...].astype(F32), axis=0).astype(BF)
    wo_sum[...] = jnp.sum(wo_in[...].astype(F32), axis=0).astype(BF)
    kept = [
        net.local(qkv_sum, qkv_all.at[head_of(me)]),
        net.local(wo_sum, wo_all.at[head_of(me)]),
    ]
    spreads = [
        gather_ring(net, "z", src, sequence_block(out), rows)
        for src, out, rows in ((qkv_sum, qkv_all, 64), (wo_sum, wo_all, 32))
    ]
    for task in spreads:
        next(task)
    step(feed)
    next(gain)
    drain(*spreads)
    for copy in kept:
        net.settle(copy)
    heads_back = net.swap(qkv_all, heads_out)
    drain(exchange(net, wo_all, wo_mid, CHIP_SHIFTS, chip_of))
    outs_back = net.swap(wo_mid, outs_out)
    drain(gain)
    drain(feed)
    heads_back.wait()
    outs_back.wait()


def token_places(block_table, first, seq):
    blocks = block_table.shape[1]
    block = seq // blocks
    logical = (
        jnp.repeat(block_table, block, axis=1) * block + jnp.arange(seq, dtype=jnp.int32) % block
    )
    prompt = seq // 2
    segment = jnp.where(logical < prompt, 0, jnp.where(logical < prompt + first, 1, 2))
    end = jnp.where(segment == 1, prompt - 1 + first, seq - 1)
    position = jnp.where(segment == 0, logical, 895 - (end - logical))
    return logical, segment, position


def per_device(
    tokens,
    cotangent,
    block_table,
    segment_ids,
    positions,
    gain_attn,
    w_query,
    key_projection,
    value_projection,
    query_norm_gain,
    key_norm_gain,
    w_out,
    gain_ffn,
    w_gate,
    w_up,
    w_down,
):
    ctx = lax.axis_index("ctx")
    mbs, width = tokens.shape[0], tokens.shape[-1]
    tok = tokens[:, 0]

    f = lax.axis_index("fsdp")
    here = (jnp.arange(16) == f)[:, None]

    def placed(gain):
        return jnp.where(here, gain[None], jnp.zeros((), BF)).reshape(-1)

    zero = jnp.zeros((64,), BF)
    odd = f % 2 == 1

    def halved(gain):
        return jnp.concatenate([jnp.where(odd, zero, gain), jnp.where(odd, gain, zero)])

    small = jnp.concatenate(
        [
            halved(gain_attn),
            halved(gain_ffn),
            placed(query_norm_gain),
            placed(key_norm_gain),
            jnp.zeros((12 * HEAD,), BF),
        ]
    ).reshape(16, HEAD)
    count = jnp.sum((segment_ids[:, 0] == 1).astype(jnp.int32), axis=1, keepdims=True)
    other = lax.ppermute(count, "fsdp", [(i, i ^ 1) for i in range(16)])
    first = jnp.where(ctx % 2 == f % 2, count, other)
    logical, seg, where_at = token_places(block_table, first, 1024)
    start = jnp.where(seg == 2, 512 + first, 0)
    lk = jnp.broadcast_to(logical[:, :, None], (mbs, 1024, HEAD))
    lq, sq = logical[:, None, :], start[:, None, :]
    cos, sin = rope_tables(where_at)

    vm = pltpu.VMEM
    saves = [
        ((2, 1024, width), BF),
        ((2, 1024, 384), F32),
        ((2, 2, 1024, HEAD), BF),
        ((2, 1024, HEAD), BF),
        ((2, 1024, HEAD), BF),
        ((2, 256, 1024), BF),
        ((2, 2, 1, 1024), F32),
    ]
    sequence = vm((2, 8, 128, width), BF)
    attended, normed, gain_rows, wqkv, wo, cots, wgu, wds, _, *saved = comm_call(
        front_body,
        RING_Z + RING_X + RING_Y + WEIGHT_PLANE,
        [
            ((2, 128, width), F32),
            ((2, 128, width), BF),
            ((8, width), F32),
            ((2, 8, 2, 32, 512), BF),
            ((2, 8, 16, width), BF),
            ((2, 8, 128, width), BF),
            ((2, 8, 2, 32, 768), BF),
            ((2, 192, width), BF),
            ((8, 16, width), BF),
        ]
        + saves,
        [vm(shape, kind) for shape, kind in saves]
        + [sequence, sequence, vm((1024, 256), BF), vm((HEAD, 1024), BF)]
        + [vm((2, 32, 512), BF), vm((16, 16, HEAD), BF), vm((8, 64, 768), BF)]
        + [vm((2, 128, width), BF), vm((2, 128, width), BF)]
        + reduce_ring_scratch(width) * 2,
        0,
        [True] + [False] * 6 + [True] * 2 + [False] + [True] * 5,
        [True] * 5 + [False] * 11,
        160,
        64,
    )(
        tok, cotangent[:, 0], small, w_query, key_projection, value_projection,
        w_out.reshape(8, 16, width), w_gate, w_up, w_down, cos, sin, lk, lq, sq,
    )
    g_attended, g_attn, gain_sum, dg, dd, out_part = comm_call(
        feed_body,
        RING_X,
        [
            ((2, 128, width), F32),
            ((2, 128, width), BF),
            ((8, width), F32),
            ((2, 4, 2, 64, 768), BF),
            ((2, 2, 4, 192, 128), BF),
            ((2, 8, 128, width), BF),
        ],
        [sequence, vm((2, 1024, 384), BF), vm((2, 1024, 768), BF), sequence, sequence]
        + [vm((1024, 768), F32), vm((384, width), F32), vm((2, 128, width), F32)]
        + reduce_ring_scratch(width) * 2,
        1,
        [True] * 7,
        [True] * 5 + [False],
        64,
        8,
    )(normed, attended, cotangent[:, 0], cots, wgu, wds, gain_rows)
    in_sum, out_sum, heads, outs, gu, down, gain_total = comm_call(
        back_body,
        RING_Z + RING_X + RING_Y + [{"yl": 1}] + SAMPLE_SHIFTS + CHIP_SHIFTS + TP_SHIFTS + COPY_SHIFTS,
        [
            ((2, 128, width), BF),
            ((2, 128, width), F32),
            ((8, 64, 512), BF),
            ((8, 32, 512), BF),
            ((8, 64, 768), BF),
            ((8, 192, 128), BF),
            ((24, HEAD), F32),
        ],
        [vm(shape, kind) for shape, kind in saves]
        + [sequence, sequence, sequence, vm((2, 1024, 512), BF)]
        + [vm((1024, 512), F32), vm((256, 1024), F32), vm((HEAD, 1024), BF)]
        + [vm((1024, HEAD), F32), vm((1024, HEAD), F32), vm((2, 1024, HEAD), F32)]
        + [vm((2, 128, width), BF), vm((8, HEAD), F32)]
        + [vm((16, 64, 512), BF), vm((2, 8, 32, 512), BF)]
        + [vm((16, 64, 512), BF), vm((16, 32, 512), BF)]
        + [vm((64, 512), BF), vm((32, 512), BF)]
        + [vm((8, 64, 512), BF), vm((8, 32, 512), BF), vm((8, 32, 512), BF), vm((8, 64, 768), BF)]
        + [vm((24, HEAD), F32), vm((7, 24, HEAD), F32), vm((24, HEAD), F32), vm((15, 24, HEAD), F32)]
        + reduce_ff_scratch()
        + reduce_ring_scratch(width) * 4,
        2,
        [True] * 5 + [False] * 8 + [True] * 8,
        [True] * 2 + [False] * 4 + [True],
        224,
        40,
    )(g_attn, tok, gain_sum, dg, dd, out_part, *saved, wqkv, wo, gain_rows, cos, sin, lk, lq, sq)
    output = (attended + out_sum).astype(BF)
    g_in = in_sum.astype(F32)
    x_own = tok.astype(F32)
    r1 = norm_scale(x_own)
    n1 = g_in * gain_rows[0]
    grad_tokens = (
        g_attended
        + r1 * n1
        - x_own * (r1 * r1 * r1) * jnp.mean(n1 * x_own, axis=-1, keepdims=True)
    )
    qkv_grad = heads.astype(F32)
    grad_w_query = qkv_grad[:, :, :256].transpose(1, 0, 2).reshape(64, 2048)
    grad_w_key = qkv_grad[:, :, 256:384].transpose(1, 0, 2).reshape(64, 1024)
    grad_w_value = qkv_grad[:, :, 384:].transpose(1, 0, 2).reshape(64, 1024)
    grad_w_out = outs.astype(F32).reshape(8, 2, 16, 512).transpose(0, 2, 1, 3).reshape(128, width)

    def columns(part):
        return part.reshape(8, 64, 2, 192).transpose(1, 2, 0, 3).reshape(64, 3072).astype(F32)

    grad_w_gate, grad_w_up = columns(gu[:, :, :384]), columns(gu[:, :, 384:])
    grad_w_down = down.astype(F32).transpose(1, 0, 2).reshape(192, width)

    def mine(rows, n):
        return lax.dynamic_slice_in_dim(rows.reshape(-1), f * n, n)

    gains = [
        mine(gain_total[0:8], 64),
        mine(gain_total[8:16], 64),
        mine(gain_total[16], 8),
        mine(gain_total[17], 8),
    ]
    return (
        output.reshape(2, 1, 128, width),
        grad_tokens.reshape(2, 1, 128, width),
        gains[0],
        grad_w_query,
        grad_w_key,
        grad_w_value,
        gains[2],
        gains[3],
        grad_w_out,
        gains[1],
        grad_w_gate,
        grad_w_up,
        grad_w_down,
    )


def solution(mesh):
    placed = (
        P(None, "fsdp", "ctx", None),
        P(None, "fsdp", "ctx", None),
        P(),
        P(None, "fsdp", None),
        P(None, "fsdp", "ctx"),
        P("fsdp"),
        P("fsdp", None),
        P("fsdp", None),
        P("fsdp", None),
        P("fsdp"),
        P("fsdp"),
        P("fsdp", None),
        P("fsdp"),
        P("fsdp", None),
        P("fsdp", None),
        P("fsdp", None),
    )
    return jax.shard_map(
        per_device,
        mesh=mesh,
        in_specs=placed,
        out_specs=(
            P(None, "fsdp", "ctx", None),
            P(None, "fsdp", "ctx", None),
            P("fsdp"),
            P("fsdp", None),
            P("fsdp", None),
            P("fsdp", None),
            P("fsdp"),
            P("fsdp"),
            P("fsdp", None),
            P("fsdp"),
            P("fsdp", None),
            P("fsdp", None),
            P("fsdp", None),
        ),
        check_vma=False,
    )
```

```python
import functools
import math

import jax
import jax.numpy as jnp
from jax import lax
from jax.experimental import pallas as pl
from jax.experimental.pallas import tpu as pltpu
from jax.sharding import PartitionSpec as P

MESH = pl.DeviceIdType.MESH
SIZES = {"z": 4, "yl": 2, "yh": 2, "x": 4, "core": 2}
BF = jnp.bfloat16
F32 = jnp.float32
HEAD = 128


def my_place():
    c = lax.axis_index("ctx")
    f = lax.axis_index("fsdp")
    return {"z": c // 2, "yl": c % 2, "yh": f // 8, "x": (f // 2) % 4, "core": f % 2}


def moved(me, shift):
    to = dict(me)
    for axis, step in shift.items():
        if axis == "y":
            y = (me["yh"] * 2 + me["yl"] + step % 4) % 4
            to["yh"], to["yl"] = y // 2, y % 2
        else:
            to[axis] = (me[axis] + (step % SIZES[axis])) % SIZES[axis]
    return to


def ctx_of(place):
    return place["z"] * 2 + place["yl"]


def tp_of(place):
    return place["x"] * 2 + place["core"]


def chip_of(place):
    return place["yh"] * 4 + place["x"]


def head_of(place):
    return place["z"] * 2 + place["core"]


def fsdp_of(place):
    return chip_of(place) * 2 + place["core"]


def device_of(place):
    return (ctx_of(place), fsdp_of(place))


CTX_SHIFTS = [{"z": a, "yl": b} for a in range(4) for b in range(2) if a or b]
PLANE_SHIFTS = [
    {"yh": a, "x": b, "core": d}
    for a in range(2)
    for b in range(4)
    for d in range(2)
    if a or b or d
]
CHIP_SHIFTS = [{"yh": a, "x": b} for a in range(2) for b in range(4) if a or b]
TP_SHIFTS = [{"x": b, "core": d} for b in range(4) for d in range(2) if b or d]
COPY_SHIFTS = [
    {"z": a, "yl": b, "yh": d}
    for a in range(4)
    for b in range(2)
    for d in range(2)
    if a or b or d
]
WEIGHT_PLANE = [
    {"yh": a, "yl": a, "x": b, "core": d}
    for a in range(2)
    for b in range(4)
    for d in range(2)
    if a or b or d
]
WEIGHT_CHIPS = [{"yh": a, "yl": a, "x": b} for a in range(2) for b in range(4) if a or b]
SAMPLE_SHIFTS = [
    {"yh": a, "yl": b, "x": d}
    for a in range(2)
    for b in range(2)
    for d in range(4)
    if a or b or d
]
HEAD_SHIFTS = [{"z": a, "core": b} for a in range(4) for b in range(2) if a or b]
RING_Y = [{"y": 1}, {"y": 3}]
RING_Z = [{"z": 1}, {"z": 3}, {"core": 1}, {"yl": 1, "core": 1}]
RING_X = [{"x": 1}, {"x": 3}, {"core": 1}]


def back(shift):
    return {axis: -step for axis, step in shift.items()}


class Net:
    def __init__(self, send_sems, recv_sems, local_sems):
        self.me = my_place()
        self.send_sems, self.recv_sems, self.local_sems = send_sems, recv_sems, local_sems
        self.count = 0
        self.locals = 0
        self.pending = []

    def enter(self, shifts, between):
        barrier = pltpu.get_barrier_semaphore()
        for shift in shifts:
            pl.semaphore_signal(
                barrier, inc=1, device_id=device_of(moved(self.me, shift)), device_id_type=MESH
            )
        between()
        pl.semaphore_wait(barrier, len(shifts))

    def send(self, src, dst, **shift):
        at = self.count
        self.count += 1
        copy = pltpu.make_async_remote_copy(
            src_ref=src,
            dst_ref=dst,
            send_sem=self.send_sems.at[at],
            recv_sem=self.recv_sems.at[at],
            device_id=device_of(moved(self.me, shift)),
            device_id_type=MESH,
        )
        copy.start()
        self.pending.append(copy.wait_send)
        return copy

    def spare(self):
        self.locals += 1
        return self.local_sems.at[self.locals - 1]

    def settle(self, copy):
        copy.wait()
        self.pending.remove(copy.wait)

    def local(self, src, dst):
        copy = pltpu.make_async_copy(src, dst, self.local_sems.at[self.locals])
        self.locals += 1
        copy.start()
        self.pending.append(copy.wait)
        return copy

    def swap(self, src, dst):
        return Swap(self, src, dst)

    def finish(self):
        for wait in self.pending:
            wait()


class Swap:
    def __init__(self, net, src, dst):
        me = net.me
        self.away = me["yl"] != me["core"]
        at = net.count
        net.count += 1
        self.remote = pltpu.make_async_remote_copy(
            src_ref=src,
            dst_ref=dst,
            send_sem=net.send_sems.at[at],
            recv_sem=net.recv_sems.at[at],
            device_id=device_of(moved(me, {"yl": 1, "core": 1})),
            device_id_type=MESH,
        )
        self.near = pltpu.make_async_copy(src, dst, net.spare())
        pl.when(self.away)(self.remote.start)
        pl.when(jnp.logical_not(self.away))(self.near.start)

    def wait(self):
        pl.when(self.away)(self.remote.wait)
        pl.when(jnp.logical_not(self.away))(self.near.wait)


def run_tasks(tasks):
    tasks = list(tasks)
    while tasks:
        left = []
        for task in tasks:
            try:
                next(task)
                left.append(task)
            except StopIteration:
                pass
        tasks = left


def unique(shifts):
    seen, out = set(), []
    for shift in shifts:
        key = tuple(sorted((k, v) for k, v in shift.items() if v))
        if key not in seen:
            seen.add(key)
            out.append(shift)
    return out


def comm_call(
    body, shifts, outs, scratch, cid, in_vmem, out_vmem, n_remote, n_local=1, first=None
):
    shifts = unique(shifts)

    def kernel(*refs):
        refs, sems = refs[:-3], refs[-3:]
        net = Net(*sems)
        net.enter(shifts, functools.partial(first, *refs) if first else lambda: None)
        drain(*(body(net, *refs) or ()))
        net.finish()

    vm = pl.BlockSpec(memory_space=pltpu.VMEM)
    hb = pl.BlockSpec(memory_space=pl.ANY)
    sm = pl.BlockSpec(memory_space=pltpu.SMEM)
    return pl.pallas_call(
        kernel,
        out_shape=[jax.ShapeDtypeStruct(s, d) for s, d in outs],
        in_specs=[sm if v is None else vm if v else hb for v in in_vmem],
        out_specs=[vm if v else hb for v in out_vmem],
        scratch_shapes=list(scratch)
        + [
            pltpu.SemaphoreType.DMA((n_remote,)),
            pltpu.SemaphoreType.DMA((n_remote,)),
            pltpu.SemaphoreType.DMA((n_local,)),
        ],
        compiler_params=pltpu.CompilerParams(
            collective_id=cid, has_side_effects=True, vmem_limit_bytes=63 << 20
        ),
    )


def drain(*tasks):
    run_tasks(tasks)


def step(task):
    next(task, None)


def gather_ring(net, axis, src, block, rows, pair="core"):
    me = net.me
    half = rows // 2
    low, high = (0, half), (half, half)

    def at(step, part=(0, rows)):
        return block(moved(me, {axis: step}), *part)

    def cut(part):
        return at(0, part) if src is None else src.at[..., pl.ds(*part), :]

    def send(step, part, shift):
        here = cut(part) if step == 0 else at(step, part)
        return net.send(here, at(step, part), **shift)

    right, left, other = {axis: 1}, {axis: -1}, {pair: 1}
    r0 = send(0, low, right)
    l1 = send(0, high, left)
    r1 = send(0, high, right)
    l0 = send(0, low, left)
    own = pair and send(0, (0, rows), other)
    yield
    r0.wait_recv()
    fr = send(-1, low, right)
    l1.wait_recv()
    fl = send(1, high, left)
    yield
    if not pair:
        for copy in (r1, l0, fr, fl):
            copy.wait_recv()
        return
    r1.wait_recv()
    cr = send(-1, (0, rows), other)
    l0.wait_recv()
    cl = send(1, (0, rows), other)
    yield
    fr.wait_recv()
    c2r = send(2, low, other)
    fl.wait_recv()
    c2l = send(2, high, other)
    yield
    for copy in (own, cr, cl, c2r, c2l):
        copy.wait_recv()


def add_rows(dst, terms, rows, step=32):
    def one(i, carry):
        at = pl.ds(pl.multiple_of(i * step, step), step)
        total = terms[0][at, :].astype(F32)
        for term in terms[1:]:
            total = total + term[at, :].astype(F32)
        dst[at, :] = total.astype(dst.dtype)
        return carry

    lax.fori_loop(0, rows // step, one, 0)


def reduce_ring(net, axis, part, index, total, rc, rh, r, extra=()):
    me = net.me
    low, high = pl.ds(0, 64), pl.ds(64, 64)
    right, left, other = {axis: 1}, {axis: -1}, {"core": 1}

    def at(step, core, rows=pl.ds(0, 128)):
        return part.at[index(moved(me, {axis: step, "core": core})), rows]

    def add(step, rows, n, *more):
        add_rows(rc.at[step, rows], [at(step, 0, rows), rc.at[step, rows], *more], n)

    cc = {}
    for step in (2, 1, 3, 0):
        cc[step] = net.send(at(step, 1), rc.at[step], **other)
    yield
    cc[2].wait_recv()
    add(2, low, 64)
    h_r = net.send(rc.at[2, low], rh.at[0], **right)
    add(2, high, 64)
    h_l = net.send(rc.at[2, high], rh.at[1], **left)
    cc[1].wait_recv()
    add(1, high, 64)
    r_high = net.send(rc.at[1, high], r.at[0, high], **right)
    cc[3].wait_recv()
    add(3, low, 64)
    l_low = net.send(rc.at[3, low], r.at[1, low], **left)
    yield
    h_r.wait_recv()
    add(1, low, 64, rh.at[0])
    r_low = net.send(rc.at[1, low], r.at[0, low], **right)
    h_l.wait_recv()
    add(3, high, 64, rh.at[1])
    l_high = net.send(rc.at[3, high], r.at[1, high], **left)
    yield
    for copy in (cc[0], r_high, l_low, r_low, l_high):
        copy.wait_recv()
    add_rows(total, [at(0, 0), rc.at[0], r.at[0], r.at[1], *extra], 128)


def reduce_ring_tiles(net, axis, part, index, total, rc, rh, r):
    me = net.me
    low, high = pl.ds(0, 64), pl.ds(64, 64)
    right, left, other = {axis: 1}, {axis: -1}, {"core": 1}

    def at(step, core, rows=pl.ds(0, 128)):
        return part.at[index(moved(me, {axis: step, "core": core})), rows]

    def add(step, rows, n, *more):
        add_rows(rc.at[step, rows], [at(step, 0, rows), rc.at[step, rows], *more], n)

    def over(step):
        return net.send(at(step, 1), rc.at[step], **other)

    c2 = over(2)
    yield
    c1 = over(1)
    c2.wait_recv()
    add(2, low, 64)
    h_r = net.send(rc.at[2, low], rh.at[0], **right)
    add(2, high, 64)
    h_l = net.send(rc.at[2, high], rh.at[1], **left)
    yield
    c3 = over(3)
    c1.wait_recv()
    add(1, high, 64)
    r_high = net.send(rc.at[1, high], r.at[0, high], **right)
    yield
    c0 = over(0)
    c3.wait_recv()
    add(3, low, 64)
    l_low = net.send(rc.at[3, low], r.at[1, low], **left)
    h_r.wait_recv()
    add(1, low, 64, rh.at[0])
    r_low = net.send(rc.at[1, low], r.at[0, low], **right)
    h_l.wait_recv()
    add(3, high, 64, rh.at[1])
    l_high = net.send(rc.at[3, high], r.at[1, high], **left)
    yield
    for copy in (c0, r_high, l_low, r_low, l_high):
        copy.wait_recv()
    add_rows(total, [at(0, 0), rc.at[0], r.at[0], r.at[1]], 128)


TILES = (2, 1, 3, 0)


def reduce_ring_scratch(width):
    return [
        pltpu.VMEM((4, 128, width), BF),
        pltpu.VMEM((2, 64, width), BF),
        pltpu.VMEM((2, 128, width), BF),
    ]


def by_x_then_y(net, pick, out):
    me = net.me
    mine = out.at[me["yh"], tp_of(me), me["yl"]]
    kept = net.local(pick(me), mine)
    copies = [net.send(pick(moved(me, shift)), mine, **shift) for shift in TP_SHIFTS]
    yield
    for copy in copies:
        copy.wait_recv()
    net.settle(kept)

    def block(place, lo, n):
        return out.at[place["yh"], pl.ds(lo, n), place["yl"]]

    yield from gather_ring(net, "y", None, block, 8, None)


def gather_heads_weights(net, wq, wk, wv, small, stage, out, small_out):
    me = net.me
    mine = fsdp_of(me)
    staged = []
    rows = pl.ds(pl.multiple_of(me["yl"] * 32, 32), 32)
    for core in range(2):
        h = me["z"] * 2 + core
        place = stage.at[core]
        for src, n, lane in ((wq, 256, 0), (wk, 128, 256), (wv, 128, 384)):
            columns = src.at[rows, pl.ds(pl.multiple_of(h * n, n), n)]
            staged.append(net.local(columns, place.at[:, pl.ds(lane, n)]))
    yield
    for copy in staged:
        net.settle(copy)
    task = by_x_then_y(net, lambda place: stage.at[place["core"]], out)
    next(task)
    kept = net.local(small, small_out.at[mine])
    copies = [net.send(small, small_out.at[mine], **shift) for shift in WEIGHT_PLANE]
    yield
    yield from task
    for copy in copies:
        copy.wait_recv()
    net.settle(kept)


def gather_out_weights(net, src, mid, out):
    me = net.me
    mine = chip_of(me)
    stay = net.local(src.at[mine], mid.at[mine])
    first = [
        net.send(src.at[chip_of(moved(me, shift))], mid.at[mine], **shift) for shift in WEIGHT_CHIPS
    ]
    yield
    for copy in first:
        copy.wait_recv()
    net.settle(stay)
    place = out.at[me["core"], mine]
    kept = net.local(mid.at[head_of(me)], place)
    copies = [
        net.send(mid.at[head_of(moved(me, shift))], place, **shift) for shift in WEIGHT_PLANE
    ]
    yield
    for copy in copies:
        copy.wait_recv()
    net.settle(kept)


def pack_columns(src, stage, lane):
    first = lax.broadcasted_iota(jnp.int32, (64, 256), 1) < 64
    for j in range(8):
        low = 192 * j - 64 * (j % 2)
        a = src[:, low : low + 256].astype(F32)
        b = src[:, 1536 + low : 1536 + low + 256].astype(F32)
        if j % 2:
            a = pltpu.roll(a, 192, 1)
        else:
            b = pltpu.roll(b, 64, 1)
        rest = jnp.where(first, jnp.concatenate([a[:, 128:], a[:, 128:]], axis=1), b)
        stage[j, :, lane : lane + 128] = a[:, :128].astype(BF)
        stage[j, :, lane + 128 : lane + 384] = rest.astype(BF)


def gather_ff_weights(net, down, stage, out, down_out):
    me = net.me
    rows = pl.ds(pl.multiple_of(me["yl"] * 32, 32), 32)
    task = by_x_then_y(net, lambda place: stage.at[tp_of(place), rows], out)
    next(task)
    kept = net.local(down, down_out.at[me["yh"]])
    copy = net.send(down, down_out.at[me["yh"]], yh=1, yl=1)
    yield
    yield from task
    copy.wait_recv()
    net.settle(kept)


def chunk_of(place):
    return chip_of(place) * 2 + place["yl"]


def scatter_samples(net, pick, out):
    me = net.me
    mine = chunk_of(me)
    kept = net.local(pick(me), out.at[mine])
    copies = [net.send(pick(moved(me, shift)), out.at[mine], **shift) for shift in SAMPLE_SHIFTS]
    yield
    for copy in copies:
        copy.wait_recv()
    net.settle(kept)


def reduce_ff(net, g, d, rhg, rhd, rg, rd, tg, td, zg, zd, gsum, dsum):
    me = net.me
    ring = ({"y": 1}, {"y": -1})
    some = [pl.ds(0, 2), pl.ds(2, 2)]

    def terms(step, h):
        to = moved(me, {"y": step})
        return g.at[to["yh"], some[h], to["yl"]], d.at[to["yh"], to["yl"], some[h]]

    def send(step, h, dst_g, dst_d, to):
        src_g, src_d = terms(step, h)
        return [net.send(src_g, dst_g, **to), net.send(src_d, dst_d, **to)]

    half = [send(2, h, rhg.at[h], rhd.at[h], ring[h]) for h in range(2)]
    near = send(1, 1, rg.at[0, 1], rd.at[0, 1], ring[0])
    near += send(-1, 0, rg.at[1, 0], rd.at[1, 0], ring[1])
    yield
    for h, step in ((0, 1), (1, -1)):
        for copy in half[h]:
            copy.wait_recv()
        own_g, own_d = terms(step, h)
        for k in range(2):
            add_rows(rhg.at[h, k], [own_g.at[k], rhg.at[h, k]], 64)
            add_rows(rhd.at[h, k], [own_d.at[k], rhd.at[h, k]], 192)
        near.append(net.send(rhg.at[h], rg.at[h, h], **ring[h]))
        near.append(net.send(rhd.at[h], rd.at[h, h], **ring[h]))
    yield
    for copy in near:
        copy.wait_recv()
    for h in range(2):
        own_g, own_d = terms(0, h)
        for k in range(2):
            add_rows(tg.at[2 * h + k], [own_g.at[k], rg.at[0, h, k], rg.at[1, h, k]], 64)
            add_rows(td.at[2 * h + k], [own_d.at[k], rd.at[0, h, k], rd.at[1, h, k]], 192)
    copies = []
    for k in range(3):
        to = moved(me, {"z": k + 1})
        copies.append(net.send(tg.at[to["z"]], zg.at[k], z=k + 1))
        copies.append(net.send(td.at[to["z"]], zd.at[k], z=k + 1))
    yield
    for copy in copies:
        copy.wait_recv()
    add_rows(gsum, [tg.at[me["z"]]] + [zg.at[k] for k in range(3)], 64)
    add_rows(dsum, [td.at[me["z"]]] + [zd.at[k] for k in range(3)], 192)


def reduce_ff_scratch():
    shapes = [(64, 768), (192, 128)]
    out = []
    for lead in ((2, 2), (2, 2, 2), (4,), (3,), ()):
        out += [pltpu.VMEM(lead + s, BF) for s in shapes]
    return out


def exchange(net, src, out, shifts, index):
    me = net.me
    mine = index(me)
    kept = net.local(src.at[mine], out.at[mine])
    copies = [net.send(src.at[index(moved(me, shift))], out.at[mine], **shift) for shift in shifts]
    yield
    for copy in copies:
        copy.wait_recv()
    net.settle(kept)


def unpack_columns(src, lane, out):
    first = lax.broadcasted_iota(jnp.int32, (64, 128), 1) < 64

    def tile(j, k):
        return src[j, :, lane + 128 * k : lane + 128 * k + 128].astype(F32)

    def half(t):
        return pltpu.roll(t, 64, 1)

    for pair in range(4):
        j, n = 2 * pair, 2 * pair + 1
        a = [tile(j, k) for k in range(3)]
        b = [tile(n, k) for k in range(3)]
        low = (
            a[0],
            jnp.where(first, a[1], half(b[0])),
            jnp.where(first, half(b[0]), half(b[1])),
        )
        high = (
            jnp.where(first, half(a[1]), half(a[2])),
            jnp.where(first, half(a[2]), b[1]),
            b[2],
        )
        for base, tiles in ((3 * pair, low), (12 + 3 * pair, high)):
            for k, t in enumerate(tiles):
                out[:, 128 * (base + k) : 128 * (base + k) + 128] = t.astype(BF)


def sum_everywhere(net, own, first, middle, second, total):
    stages = ((own, first, TP_SHIFTS, middle), (middle, second, COPY_SHIFTS, total))
    for src, slots, shifts, dst in stages:
        copies = [net.send(src, slots.at[k], **shift) for k, shift in enumerate(shifts)]
        yield
        for copy in copies:
            copy.wait_recv()
        dst[...] = src[...] + jnp.sum(slots[...], axis=0)


def rope_frequency():
    half = jnp.exp(jnp.arange(0, HEAD // 2, dtype=F32) * (-2.0 * math.log(1000000.0) / HEAD))
    return jnp.concatenate([half, half])[None]


def across_rows(a, b):
    return lax.dot_general(a, b, (((0,), (0,)), ((), ())), preferred_element_type=F32)


def against_cols(a, b):
    return lax.dot_general(a, b, (((1,), (1,)), ((), ())), preferred_element_type=F32)


def forward_dot(a, b):
    return jnp.dot(a, b, preferred_element_type=F32)


EXP2_SCALE = HEAD ** (-0.5) * math.log2(math.e)


def norm_scale(v):
    return lax.rsqrt(jnp.mean(v * v, axis=-1, keepdims=True) + 1e-06)


def visible_tile(lk, lq, sq):
    later = jnp.where(lk < 512, 4096, lk)
    later, lk = jnp.concatenate([later, later], axis=1), jnp.concatenate([lk, lk], axis=1)
    return (lk <= lq) & (later >= sq)


def half_loop(body, part, parts, count):
    lax.fori_loop(part * count // parts, (part + 1) * count // parts, body, 0)


class Front:
    def __init__(self, m, gains, wqkv, wo, xs, tables, saved, part, mixed, vt):
        self.gains, self.wqkv, self.wo, self.xs = gains, wqkv, wo, xs.at[m]
        self.cos, self.sin, self.lk, self.lq, self.sq = (t.at[m] for t in tables)
        self.xn, self.raw, self.q, self.k, self.v, self.mixt, self.rl = (t.at[m] for t in saved)
        self.part, self.mixed, self.vt = part.at[m], mixed, vt

    def project(self, i, carry):
        rows = pl.ds(pl.multiple_of(i * 256, 256), 256)
        x = self.xs[pl.ds(i * 2, 2)].reshape(256, 1024).astype(F32)
        low = (x * norm_scale(x) * self.gains[0:1, :]).astype(BF)
        self.xn[rows, :] = low
        y = forward_dot(low, self.wqkv[...].reshape(1024, 512))
        self.raw[rows, :] = y[:, :384]
        c, s = self.cos[rows, :], self.sin[rows, :]
        for head in range(3):
            u = y[:, head * HEAD : (head + 1) * HEAD]
            lane = HEAD * (head // 2)
            n = u * norm_scale(u) * self.gains[2:3, lane : lane + HEAD]
            turned = (n * c + pltpu.roll(n, HEAD // 2, 1) * s).astype(BF)
            if head < 2:
                self.q[head, rows, :] = turned
            else:
                self.k[rows, :] = turned
        value = y[:, 384:]
        self.v[rows, :] = value.astype(BF)
        self.vt[:, rows] = value.T.astype(BF)
        return carry

    def attend(self, head, i, carry):
        rows = pl.ds(pl.multiple_of(i * 256, 256), 256)
        s = against_cols(self.k[...], self.q[head, rows, :])
        seen = visible_tile(self.lk[...], self.lq[:, rows], self.sq[:, rows])
        e = jnp.where(seen, jnp.exp2(s * EXP2_SCALE), 0.0)
        inv = 1.0 / jnp.sum(e, axis=0, keepdims=True)
        self.rl[head, :, rows] = inv
        m = forward_dot(self.vt[...], e.astype(BF)) * inv
        self.mixt[head * HEAD : (head + 1) * HEAD, rows] = m.astype(BF)
        self.mixed[rows, head * HEAD : (head + 1) * HEAD] = m.T.astype(BF)
        return carry

    def project_out(self, i, carry):
        rows = pl.ds(pl.multiple_of(i * 256, 256), 256)
        y = forward_dot(self.mixed[rows, :], self.wo[...].reshape(256, 1024)).astype(BF)
        self.part[pl.ds(i * 2, 2)] = y.reshape(2, 128, 1024)
        return carry

    def projection(self):
        half_loop(self.project, 0, 1, 4)

    def tile(self, i):
        self.attend(0, i, 0)
        self.attend(1, i, 0)
        self.project_out(i, 0)


def make_tables(m, table, first, frequency, cos, sin, lk):
    row = lax.broadcasted_iota(jnp.int32, (64, HEAD), 0)
    lane = lax.broadcasted_iota(jnp.int32, (64, HEAD), 1)
    for b in range(16):
        rows = slice(64 * b, 64 * b + 64)
        at = table[m, b] * 64 + row
        lk[m, rows, :] = at
        later = jnp.where(at < 512 + first[m, 0], at + (384 - first[m, 0]), at - 128)
        angle = jnp.where(at < 512, at, later).astype(F32) * frequency[...]
        cos[m, rows, :] = jnp.cos(angle)
        turn = jnp.sin(angle)
        sin[m, rows, :] = jnp.where(lane < HEAD // 2, -turn, turn)


def sequence_block(out):
    def block(place, lo, n):
        return out.at[head_of(place), pl.ds(lo, n)]

    return block


def front_first(
    tok, cot, small, wq, wk, wv, wo_in, wg, wu, wd, table, first, frequency, lq, sq, cos, sin, lk, *_
):
    make_tables(0, table, first, frequency, cos, sin, lk)


def front_body(
    net,
    tok, cot, small, wq, wk, wv, wo_in, wg, wu, wd, table, first, frequency, lq, sq,
    cos, sin, lk, attended, normed, gains, wqkv, wo, cots, wgu, wds, mid,
    xn_out, raw_out, q_out, k_out, v_out, mixt_out, rl_out,
    xn, raw, q, k, v, mixt, rl,
    xs, part, mixed, vt, stage, smalls, gu_stage, outbox, inbox, *bufs,
):
    me = net.me
    heads = gather_heads_weights(net, wq, wk, wv, small, stage, wqkv, smalls)
    next(heads)
    swaps = [net.swap(tok.at[m], xs.at[m, ctx_of(me)]) for m in range(2)]
    gather = [
        gather_ring(net, "z", xs.at[m, head_of(me)], sequence_block(xs.at[m]), 128)
        for m in range(2)
    ]
    outs = gather_out_weights(net, wo_in, mid, wo)
    feed = gather_ff_weights(net, wd, gu_stage, wgu, wds)

    def cot_block(place, lo, n):
        return cots.at[:, tp_of(place), pl.ds(lo, n)]

    cots_in = gather_ring(net, "x", cot, cot_block, 128)
    own_cot = net.local(cot, cots.at[:, tp_of(me)])
    next(heads)
    make_tables(1, table, first, frequency, cos, sin, lk)
    swaps[0].wait()
    next(gather[0])
    next(heads)
    next(outs)
    next(cots_in)
    pack_columns(wg, gu_stage, 0)
    pack_columns(wu, gu_stage, 384)
    next(feed)
    next(gather[0])
    swaps[1].wait()
    next(gather[1])
    next(heads)
    next(gather[0])
    drain(gather[0])
    drain(heads)
    next(outs)
    next(feed)
    next(cots_in)
    pairs = [smalls[2 * i].astype(F32) + smalls[2 * i + 1].astype(F32) for i in range(8)]
    both = sum(pairs[1:], pairs[0])
    gains[...] = jnp.zeros_like(gains)
    gains[0:1, :] = jnp.concatenate([p[0:1] for p in pairs], axis=1)
    gains[1:2, :] = jnp.concatenate([p[1:2] for p in pairs], axis=1)
    gains[2:3, : 2 * HEAD] = jnp.concatenate([both[2:3], both[3:4]], axis=1)
    tables = (cos, sin, lk, lq, sq)
    saved = (xn, raw, q, k, v, mixt, rl)
    work = [Front(m, gains, wqkv, wo, xs, tables, saved, part, mixed, vt) for m in range(2)]

    def save(m):
        for src, dst in zip(saved, (xn_out, raw_out, q_out, k_out, v_out, mixt_out, rl_out)):
            net.local(src.at[m], dst.at[m])

    def settle(m):
        x = tok[m].astype(F32) + inbox[m].astype(F32)
        attended[m] = x
        normed[m] = (x * norm_scale(x) * gains[1:2, :]).astype(BF)

    def reduce(m):
        buf = bufs[3 * m : 3 * m + 3]
        yield from reduce_ring_tiles(net, "z", part.at[m], head_of, outbox.at[m], *buf)
        swap = net.swap(outbox.at[m], inbox.at[m])
        yield
        swap.wait()
        settle(m)

    reduces = [reduce(m) for m in range(2)]
    work[0].projection()
    step(gather[1])
    drain(outs)
    for k in TILES:
        work[0].tile((me["z"] + k) % 4)
        next(reduces[0])
        step(gather[1])
        if k == 3:
            step(feed)
    step(cots_in)
    drain(gather[1])
    save(0)
    work[1].projection()
    step(reduces[0])
    for at, k in enumerate(TILES):
        work[1].tile((me["z"] + k) % 4)
        next(reduces[1])
        if at == 1:
            drain(reduces[0])
            step(cots_in)
    save(1)
    drain(reduces[1])
    drain(cots_in)
    drain(feed)


class Feed:
    def __init__(self, m, wgu, wd, nm, ct, hid, ggu, out, mid, dg, dd):
        self.m, self.wgu, self.wd = m, wgu, wd
        self.nm, self.ct, self.hid, self.ggu = nm.at[m], ct.at[m], hid.at[m], ggu.at[m]
        self.out, self.mid, self.dg, self.dd = out.at[m], mid.at[m], dg, dd

    def tile(self, i):
        rows = pl.ds(pl.multiple_of(i * 256, 256), 256)
        blocks = pl.ds(i * 2, 2)
        wgu = self.wgu[...].reshape(1024, 768)
        wd = self.wd[...].reshape(384, 1024)
        y = forward_dot(self.nm[blocks].reshape(256, 1024), wgu)
        gate, up = y[:, :384], y[:, 384:]
        gh = against_cols(self.ct[blocks].reshape(256, 1024), wd)
        sig = 1.0 / (1.0 + jnp.exp(-gate))
        silu = gate * sig
        hidden = (silu * up).astype(BF)
        self.hid[rows, :] = hidden
        gg = (gh * up * sig * (1.0 + gate * (1.0 - sig))).astype(BF)
        gu = (gh * silu).astype(BF)
        self.ggu[rows, :384] = gg
        self.ggu[rows, 384:] = gu
        self.mid[blocks] = (
            against_cols(self.ggu[rows, :], wgu).astype(BF).reshape(2, 128, 1024)
        )
        self.out[blocks] = forward_dot(hidden, wd).astype(BF).reshape(2, 128, 1024)

    def in_weights(self):
        def some(i, carry):
            at = pl.ds(pl.multiple_of(i * 128, 128), 128)
            y = across_rows(self.nm[:, :, at].reshape(1024, 128), self.ggu[...])
            self.dg[at, :] = y if self.m == 0 else self.dg[at, :] + y
            return carry

        lax.fori_loop(0, 8, some, 0)

    def down_weights(self):
        def some(i, carry):
            at = pl.ds(pl.multiple_of(i * 128, 128), 128)
            y = across_rows(self.hid[:, at], self.ct[...].reshape(1024, 1024))
            self.dd[at, :] = y if self.m == 0 else self.dd[at, :] + y
            return carry

        lax.fori_loop(0, 3, some, 0)


def feed_body(
    net,
    normed, attended, cot, cots, wgu, wds, gains,
    g_attended, g_attn, gain_sum, dg_low, dd_low, out_part_out,
    nm, hid, ggu, out_part, mid_part, dg, dd, total, *bufs,
):
    me = net.me

    def block(m):
        def at(place, lo, n):
            return nm.at[m, tp_of(place), pl.ds(lo, n)]

        return at

    own = [net.local(normed.at[m], nm.at[m, tp_of(me)]) for m in range(2)]
    gather = [gather_ring(net, "x", normed.at[m], block(m), 128) for m in range(2)]
    next(gather[0])
    next(gather[0])
    next(gather[1])
    for copy in own:
        net.settle(copy)
    drain(gather[0])
    work = [Feed(m, wgu, wds, nm, cots, hid, ggu, out_part, mid_part, dg, dd) for m in range(2)]
    gain_sum[...] = jnp.zeros_like(gain_sum)

    def settle(m):
        x, g_mid = attended[m], total[m]
        r = norm_scale(x)
        n = g_mid * gains[1:2, :]
        gain_sum[0:1, :] += jnp.sum(g_mid * x * r, axis=0, keepdims=True)
        y = cot[m].astype(F32) + r * n - x * (r * r * r) * jnp.mean(n * x, axis=-1, keepdims=True)
        g_attended[m] = y
        g_attn[m] = y.astype(BF)

    def reduce(m):
        buf = bufs[3 * m : 3 * m + 3]
        yield from reduce_ring_tiles(net, "x", mid_part.at[m], tp_of, total.at[m], *buf)
        settle(m)

    reduces = [reduce(m) for m in range(2)]
    for k in TILES:
        work[0].tile((me["x"] + k) % 4)
        next(reduces[0])
        step(gather[1])
    net.local(out_part.at[0], out_part_out.at[0])
    drain(gather[1])
    for at, k in enumerate(TILES):
        work[1].tile((me["x"] + k) % 4)
        next(reduces[1])
        if at == 1:
            drain(reduces[0])
    net.local(out_part.at[1], out_part_out.at[1])
    for one in work:
        one.in_weights()
        one.down_weights()
    drain(reduces[1])
    dg_low[...] = dg[...].astype(BF).reshape(2, 4, 2, 64, 768)
    for c in range(8):
        dd_low[:, c % 2, c // 2] = dd[:, 128 * c : 128 * c + 128].astype(BF).reshape(2, 192, 128)


class Back:
    def __init__(self, m, gains, wqkv, wo, g, tables, saved, part, graw, dwqkv, dwo, sums, work):
        self.m, self.gains, self.wqkv, self.wo, self.g = m, gains, wqkv, wo, g.at[m]
        self.cos, self.sin, self.lk, self.lq, self.sq = (t.at[m] for t in tables)
        self.xn, self.raw, self.q, self.k, self.v, self.mixt, self.rl = (t.at[m] for t in saved)
        self.part, self.graw = part.at[m], graw.at[m]
        self.dwqkv, self.dwo, self.sums = dwqkv, dwo, sums
        self.kt, self.dk, self.dv, self.dq = work

    def begin(self):
        self.kt[...] = self.k[...].astype(F32).T.astype(BF)
        self.dk[...] = jnp.zeros_like(self.dk)
        self.dv[...] = jnp.zeros_like(self.dv)

    def attend(self, head, i, carry):
        rows = pl.ds(pl.multiple_of(i * 256, 256), 256)
        at = slice(head * HEAD, (head + 1) * HEAD)
        g = self.g[pl.ds(i * 2, 2)].reshape(256, 1024)
        wo = self.wo[head].reshape(HEAD, 1024)
        gm = against_cols(g, wo).astype(BF)
        gmt = against_cols(wo, g).astype(BF)
        delta = jnp.sum(
            gmt.astype(F32) * self.mixt[at, rows].astype(F32), axis=0, keepdims=True
        )
        qt = self.q[head, rows, :]
        s = against_cols(self.k[...], qt)
        seen = visible_tile(self.lk[...], self.lq[:, rows], self.sq[:, rows])
        p = jnp.where(seen, jnp.exp2(s * EXP2_SCALE), 0.0) * self.rl[head, :, rows]
        dp = forward_dot(self.v[...], gmt)
        ds = (p * (dp - delta)).astype(BF)
        self.dv[...] += forward_dot(p.astype(BF), gm)
        self.dk[...] += forward_dot(ds, qt)
        self.dq[head, rows, :] = forward_dot(self.kt[...], ds).T
        return carry

    def unproject(self, i, carry):
        rows = pl.ds(pl.multiple_of(i * 256, 256), 256)
        c, s = self.cos[rows, :], self.sin[rows, :]
        for head in range(3):
            lane = head // 2
            at = slice(head * HEAD, (head + 1) * HEAD)
            gr = (self.dq[head, rows, :] if head < 2 else self.dk[rows, :]) * HEAD ** (-0.5)
            gu = gr * c - pltpu.roll(gr, HEAD // 2, 1) * s
            u = self.raw[rows, at]
            r = norm_scale(u)
            self.sums[lane : lane + 1, :] += jnp.sum(gu * (u * r), axis=0, keepdims=True)
            n = gu * self.gains[2:3, lane * HEAD : (lane + 1) * HEAD]
            d = r * n - u * (r * r * r) * jnp.mean(n * u, axis=-1, keepdims=True)
            self.graw[rows, at] = d.astype(BF)
        self.graw[rows, 384:] = self.dv[rows, :].astype(BF)
        y = against_cols(self.graw[rows, :], self.wqkv[...].reshape(1024, 512))
        self.part[pl.ds(i * 2, 2)] = y.astype(BF).reshape(2, 128, 1024)
        return carry

    def pieces(self):
        return (
            [self.begin]
            + [
                functools.partial(half_loop, functools.partial(self.attend, head), p, 2, 4)
                for head in range(2)
                for p in range(2)
            ]
            + [functools.partial(half_loop, self.unproject, p, 2, 4) for p in range(2)]
        )

    def out_weights(self):
        def some(i, carry):
            at = pl.ds(pl.multiple_of(i * 256, 256), 256)
            y = forward_dot(self.mixt[...], self.g[:, :, at].reshape(1024, 256))
            self.dwo[:, at] = y if self.m == 0 else self.dwo[:, at] + y
            return carry

        lax.fori_loop(0, 4, some, 0)

    def head_weights(self):
        def some(i, carry):
            at = pl.ds(pl.multiple_of(i * 256, 256), 256)
            y = across_rows(self.xn[:, at], self.graw[...])
            self.dwqkv[at, :] = y if self.m == 0 else self.dwqkv[at, :] + y
            return carry

        lax.fori_loop(0, 4, some, 0)


def back_body(
    net,
    g_own, tok, gain_sum, dg, dd, out_part_in, xn_in, raw_in, q_in, k_in, v_in, mixt_in, rl_in,
    wqkv, wo, gains, cos, sin, lk, lq, sq,
    in_sum, out_sum, gain_total,
    gq, gk, gv, gwo, gate, up, gwd,
    xn, raw, q, k, v, mixt, rl,
    g, out_part, part, graw, dwqkv, dwo, kt, dk, dv, dq, outbox, sums,
    qkv_low, wo_low, qkv_in, wo_in, qkv_sum, wo_sum, qkv_all, wo_all, wo_mid, gu_all, gu_out,
    heads_out, outs_out, down_out,
    gain_own, gain_first, gain_middle, gain_second, *bufs,
):
    me = net.me
    ff, bufs = bufs[:10], bufs[10:]
    swaps = [net.swap(g_own.at[m], g.at[m, ctx_of(me)]) for m in range(2)]
    fetched = [net.local(out_part_in.at[0], out_part.at[0])]
    saved = (xn, raw, q, k, v, mixt, rl)
    needed = [
        net.local(src.at[m], dst.at[m])
        for m in range(2)
        for src, dst in zip((xn_in, raw_in, q_in, k_in, v_in, mixt_in, rl_in), saved)
    ]
    fetched.append(net.local(out_part_in.at[1], out_part.at[1]))
    sums[...] = jnp.zeros_like(sums)
    gather = [
        gather_ring(net, "z", g.at[m, head_of(me)], sequence_block(g.at[m]), 128) for m in range(2)
    ]
    outs = [
        reduce_ring(net, "x", out_part.at[m], tp_of, out_sum.at[m], *bufs[3 * m + 6 : 3 * m + 9])
        for m in range(2)
    ]
    gsum, dsum = ff[-2:]

    def feed_gradients():
        yield from reduce_ff(net, dg, dd, *ff)
        kept = [
            net.local(gsum, gu_all.at[ctx_of(me)]),
            net.local(dsum, down_out.at[ctx_of(me)]),
        ]
        spreads = [
            gather_ring(
                net, "z", src, lambda place, lo, n, out=out: out.at[ctx_of(place), pl.ds(lo, n)],
                rows, "yl",
            )
            for src, out, rows in ((gsum, gu_all, 64), (dsum, down_out, 192))
        ]
        for _ in range(4):
            for spread in spreads:
                next(spread)
            yield
        drain(*spreads)
        for copy in kept:
            net.settle(copy)
        yield from exchange(net, gu_all, gu_out, TP_SHIFTS, tp_of)

    feed = feed_gradients()
    swaps[0].wait()
    next(gather[0])
    net.settle(fetched[0])
    next(outs[0])
    next(gather[0])
    swaps[1].wait()
    next(gather[1])
    next(gather[0])
    drain(gather[0])
    next(feed)
    for copy in needed:
        net.settle(copy)
    net.settle(fetched[1])
    tables = (cos, sin, lk, lq, sq)
    work = [
        Back(m, gains, wqkv, wo, g, tables, saved, part, graw, dwqkv, dwo, sums, (kt, dk, dv, dq))
        for m in range(2)
    ]
    for at, piece in enumerate(work[0].pieces()):
        piece()
        step(gather[1])
        if at in (1, 3, 5):
            step(outs[0])
    drain(gather[1])
    def reduce(m):
        yield from reduce_ring(net, "z", part.at[m], head_of, outbox.at[m], *bufs[3 * m : 3 * m + 3])
        swap = net.swap(outbox.at[m], in_sum.at[m])
        yield
        swap.wait()

    reduces = [reduce(m) for m in range(2)]
    next(reduces[0])
    drain(outs[0])
    next(outs[1])
    for at, piece in enumerate(work[1].pieces()):
        piece()
        if at in (1, 3, 5):
            step(reduces[0])
        if at in (2, 4, 6):
            step(outs[1])
        if at in (2, 4, 6):
            step(feed)
    next(reduces[1])
    work[0].head_weights()
    step(reduces[1])
    step(reduces[0])
    work[1].head_weights()
    qkv_low[...] = dwqkv[...].astype(BF).reshape(16, 64, 512)
    scattered = [
        scatter_samples(net, lambda place: qkv_low.at[chunk_of(place)], qkv_in),
        scatter_samples(net, lambda place: wo_low.at[place["yl"], chip_of(place)], wo_in),
    ]
    next(scattered[0])
    step(reduces[1])
    step(feed)
    work[0].out_weights()
    step(reduces[1])
    work[1].out_weights()
    low = dwo[...].astype(BF)
    for half in range(2):
        wo_low[:, :, half * 16 : half * 16 + 16, :] = low[:, half * 512 : half * 512 + 512].reshape(
            2, 8, 16, 512
        )
    next(scattered[1])
    drain(*reduces)
    drain(outs[1])
    step(feed)
    row = jnp.zeros((1, 1024), F32)
    for m in range(2):
        x = tok[m].astype(F32)
        row = row + jnp.sum(in_sum[m].astype(F32) * x * norm_scale(x), axis=0, keepdims=True)
    for k in range(8):
        at = slice(k * 128, k * 128 + 128)
        gain_own[k : k + 1, :] = row[:, at]
        gain_own[8 + k : 9 + k, :] = gain_sum[0:1, at]
    gain_own[16:24, :] = sums[...]
    gain = sum_everywhere(net, gain_own, gain_first, gain_middle, gain_second, gain_total)
    next(gain)
    drain(*scattered)
    qkv_sum[...] = jnp.sum(qkv_in[...].astype(F32), axis=0).astype(BF)
    wo_sum[...] = jnp.sum(wo_in[...].astype(F32), axis=0).astype(BF)
    kept = [
        net.local(qkv_sum, qkv_all.at[head_of(me)]),
        net.local(wo_sum, wo_all.at[head_of(me)]),
    ]
    spreads = [
        gather_ring(net, "z", src, sequence_block(out), rows)
        for src, out, rows in ((qkv_sum, qkv_all, 64), (wo_sum, wo_all, 32))
    ]
    for task in spreads:
        next(task)
    step(feed)
    next(gain)
    drain(*spreads)
    for copy in kept:
        net.settle(copy)
    heads_back = net.swap(qkv_all, heads_out)
    drain(exchange(net, wo_all, wo_mid, CHIP_SHIFTS, chip_of))
    outs_back = net.swap(wo_mid, outs_out)
    drain(gain)
    heads_back.wait()
    for h in range(8):
        gq[:, 256 * h : 256 * h + 256] = heads_out[h, :, :256]
        gk[:, 128 * h : 128 * h + 128] = heads_out[h, :, 256:384]
        gv[:, 128 * h : 128 * h + 128] = heads_out[h, :, 384:]
    drain(feed)
    for c in range(8):
        gwd[:, 128 * c : 128 * c + 128] = down_out[c]
    for k, dst in enumerate((gate, up)):
        unpack_columns(gu_out, 384 * k, dst)
    outs_back.wait()
    for i in range(8):
        for half in range(2):
            rows = slice(16 * half, 16 * half + 16)
            gwo[16 * i : 16 * i + 16, 512 * half : 512 * half + 512] = outs_out[i, rows, :]


def token_places(block_table, first, seq):
    blocks = block_table.shape[1]
    block = seq // blocks
    logical = (
        jnp.repeat(block_table, block, axis=1) * block + jnp.arange(seq, dtype=jnp.int32) % block
    )
    prompt = seq // 2
    segment = jnp.where(logical < prompt, 0, jnp.where(logical < prompt + first, 1, 2))
    return logical, segment


def per_device(
    tokens,
    cotangent,
    block_table,
    segment_ids,
    positions,
    gain_attn,
    w_query,
    key_projection,
    value_projection,
    query_norm_gain,
    key_norm_gain,
    w_out,
    gain_ffn,
    w_gate,
    w_up,
    w_down,
):
    ctx = lax.axis_index("ctx")
    mbs, width = tokens.shape[0], tokens.shape[-1]
    tok = tokens[:, 0]

    f = lax.axis_index("fsdp")
    here = (jnp.arange(16) == f)[:, None]

    def placed(gain):
        return jnp.where(here, gain[None], jnp.zeros((), BF)).reshape(-1)

    zero = jnp.zeros((64,), BF)
    odd = f % 2 == 1

    def halved(gain):
        return jnp.concatenate([jnp.where(odd, zero, gain), jnp.where(odd, gain, zero)])

    small = jnp.concatenate(
        [
            halved(gain_attn),
            halved(gain_ffn),
            placed(query_norm_gain),
            placed(key_norm_gain),
            jnp.zeros((12 * HEAD,), BF),
        ]
    ).reshape(16, HEAD)
    count = jnp.sum((segment_ids[:, 0] == 1).astype(jnp.int32), axis=1, keepdims=True)
    other = lax.ppermute(count, "fsdp", [(i, i ^ 1) for i in range(16)])
    first = jnp.where(ctx % 2 == f % 2, count, other)
    logical, seg = token_places(block_table, first, 1024)
    start = jnp.where(seg == 2, 512 + first, 0)
    lq, sq = logical[:, None, :], start[:, None, :]
    frequency = rope_frequency()

    vm = pltpu.VMEM
    saves = [
        ((2, 1024, width), BF),
        ((2, 1024, 384), F32),
        ((2, 2, 1024, HEAD), BF),
        ((2, 1024, HEAD), BF),
        ((2, 1024, HEAD), BF),
        ((2, 256, 1024), BF),
        ((2, 2, 1, 1024), F32),
    ]
    sequence = vm((2, 8, 128, width), BF)
    cos, sin, lk, attended, normed, gain_rows, wqkv, wo, cots, wgu, wds, _, *saved = comm_call(
        front_body,
        RING_Z + RING_X + RING_Y + WEIGHT_PLANE,
        [
            ((2, 1024, HEAD), F32),
            ((2, 1024, HEAD), F32),
            ((2, 1024, HEAD), jnp.int32),
            ((2, 128, width), F32),
            ((2, 128, width), BF),
            ((8, width), F32),
            ((2, 8, 2, 32, 512), BF),
            ((2, 8, 16, width), BF),
            ((2, 8, 128, width), BF),
            ((2, 8, 2, 32, 768), BF),
            ((2, 192, width), BF),
            ((8, 16, width), BF),
        ]
        + saves,
        [vm(shape, kind) for shape, kind in saves]
        + [sequence, sequence, vm((1024, 256), BF), vm((HEAD, 1024), BF)]
        + [vm((2, 32, 512), BF), vm((16, 16, HEAD), BF), vm((8, 64, 768), BF)]
        + [vm((2, 128, width), BF), vm((2, 128, width), BF)]
        + reduce_ring_scratch(width) * 2,
        0,
        [True] + [False] * 6 + [True] * 2 + [False] + [None] * 2 + [True] * 3,
        [True] * 8 + [False] * 11,
        160,
        64,
        front_first,
    )(
        tok, cotangent[:, 0], small, w_query, key_projection, value_projection,
        w_out.reshape(8, 16, width), w_gate, w_up, w_down, block_table, first, frequency, lq, sq,
    )
    g_attended, g_attn, gain_sum, dg, dd, out_part = comm_call(
        feed_body,
        RING_X,
        [
            ((2, 128, width), F32),
            ((2, 128, width), BF),
            ((8, width), F32),
            ((2, 4, 2, 64, 768), BF),
            ((2, 2, 4, 192, 128), BF),
            ((2, 8, 128, width), BF),
        ],
        [sequence, vm((2, 1024, 384), BF), vm((2, 1024, 768), BF), sequence, sequence]
        + [vm((1024, 768), F32), vm((384, width), F32), vm((2, 128, width), F32)]
        + reduce_ring_scratch(width) * 2,
        1,
        [True] * 7,
        [True] * 5 + [False],
        64,
        8,
    )(normed, attended, cotangent[:, 0], cots, wgu, wds, gain_rows)
    in_sum, out_sum, gain_total, *weights = comm_call(
        back_body,
        RING_Z + RING_X + RING_Y + [{"yl": 1}] + SAMPLE_SHIFTS + CHIP_SHIFTS + TP_SHIFTS + COPY_SHIFTS,
        [
            ((2, 128, width), BF),
            ((2, 128, width), F32),
            ((24, HEAD), F32),
            ((64, 2048), BF),
            ((64, 1024), BF),
            ((64, 1024), BF),
            ((128, width), BF),
            ((64, 3072), BF),
            ((64, 3072), BF),
            ((192, width), BF),
        ],
        [vm(shape, kind) for shape, kind in saves]
        + [sequence, sequence, sequence, vm((2, 1024, 512), BF)]
        + [vm((1024, 512), F32), vm((256, 1024), F32), vm((HEAD, 1024), BF)]
        + [vm((1024, HEAD), F32), vm((1024, HEAD), F32), vm((2, 1024, HEAD), F32)]
        + [vm((2, 128, width), BF), vm((8, HEAD), F32)]
        + [vm((16, 64, 512), BF), vm((2, 8, 32, 512), BF)]
        + [vm((16, 64, 512), BF), vm((16, 32, 512), BF)]
        + [vm((64, 512), BF), vm((32, 512), BF)]
        + [vm((8, 64, 512), BF), vm((8, 32, 512), BF), vm((8, 32, 512), BF), vm((8, 64, 768), BF)]
        + [vm((8, 64, 768), BF), vm((8, 64, 512), BF), vm((8, 32, 512), BF), vm((8, 192, 128), BF)]
        + [vm((24, HEAD), F32), vm((7, 24, HEAD), F32), vm((24, HEAD), F32), vm((15, 24, HEAD), F32)]
        + reduce_ff_scratch()
        + reduce_ring_scratch(width) * 4,
        2,
        [True] * 5 + [False] * 8 + [True] * 8,
        [True] * 10,
        224,
        40,
    )(g_attn, tok, gain_sum, dg, dd, out_part, *saved, wqkv, wo, gain_rows, cos, sin, lk, lq, sq)
    output = (attended + out_sum).astype(BF)
    g_in = in_sum.astype(F32)
    x_own = tok.astype(F32)
    r1 = norm_scale(x_own)
    n1 = g_in * gain_rows[0]
    grad_tokens = (
        g_attended
        + r1 * n1
        - x_own * (r1 * r1 * r1) * jnp.mean(n1 * x_own, axis=-1, keepdims=True)
    )
    grad_w_query, grad_w_key, grad_w_value, grad_w_out, grad_w_gate, grad_w_up, grad_w_down = (
        w.astype(F32) for w in weights
    )

    def mine(rows, n):
        return lax.dynamic_slice_in_dim(rows.reshape(-1), f * n, n)

    gains = [
        mine(gain_total[0:8], 64),
        mine(gain_total[8:16], 64),
        mine(gain_total[16], 8),
        mine(gain_total[17], 8),
    ]
    return (
        output.reshape(2, 1, 128, width),
        grad_tokens.reshape(2, 1, 128, width),
        gains[0],
        grad_w_query,
        grad_w_key,
        grad_w_value,
        gains[2],
        gains[3],
        grad_w_out,
        gains[1],
        grad_w_gate,
        grad_w_up,
        grad_w_down,
    )


def solution(mesh):
    placed = (
        P(None, "fsdp", "ctx", None),
        P(None, "fsdp", "ctx", None),
        P(),
        P(None, "fsdp", None),
        P(None, "fsdp", "ctx"),
        P("fsdp"),
        P("fsdp", None),
        P("fsdp", None),
        P("fsdp", None),
        P("fsdp"),
        P("fsdp"),
        P("fsdp", None),
        P("fsdp"),
        P("fsdp", None),
        P("fsdp", None),
        P("fsdp", None),
    )
    return jax.shard_map(
        per_device,
        mesh=mesh,
        in_specs=placed,
        out_specs=(
            P(None, "fsdp", "ctx", None),
            P(None, "fsdp", "ctx", None),
            P("fsdp"),
            P("fsdp", None),
            P("fsdp", None),
            P("fsdp", None),
            P("fsdp"),
            P("fsdp"),
            P("fsdp", None),
            P("fsdp"),
            P("fsdp", None),
            P("fsdp", None),
            P("fsdp", None),
        ),
        check_vma=False,
    )
```

```python
import functools
import math

import jax
import jax.numpy as jnp
from jax import lax
from jax.experimental import pallas as pl
from jax.experimental.pallas import tpu as pltpu
from jax.sharding import PartitionSpec as P

MESH = pl.DeviceIdType.MESH
SIZES = {"z": 4, "yl": 2, "yh": 2, "x": 4, "core": 2}
BF = jnp.bfloat16
F32 = jnp.float32
HEAD = 128


def my_place():
    c = lax.axis_index("ctx")
    f = lax.axis_index("fsdp")
    return {"z": c // 2, "yl": c % 2, "yh": f // 8, "x": (f // 2) % 4, "core": f % 2}


def moved(me, shift):
    to = dict(me)
    for axis, step in shift.items():
        if axis == "y":
            y = (me["yh"] * 2 + me["yl"] + step % 4) % 4
            to["yh"], to["yl"] = y // 2, y % 2
        else:
            to[axis] = (me[axis] + (step % SIZES[axis])) % SIZES[axis]
    return to


def ctx_of(place):
    return place["z"] * 2 + place["yl"]


def tp_of(place):
    return place["x"] * 2 + place["core"]


def chip_of(place):
    return place["yh"] * 4 + place["x"]


def head_of(place):
    return place["z"] * 2 + place["core"]


def fsdp_of(place):
    return chip_of(place) * 2 + place["core"]


def device_of(place):
    return (ctx_of(place), fsdp_of(place))


CTX_SHIFTS = [{"z": a, "yl": b} for a in range(4) for b in range(2) if a or b]
PLANE_SHIFTS = [
    {"yh": a, "x": b, "core": d}
    for a in range(2)
    for b in range(4)
    for d in range(2)
    if a or b or d
]
CHIP_SHIFTS = [{"yh": a, "x": b} for a in range(2) for b in range(4) if a or b]
TP_SHIFTS = [{"x": b, "core": d} for b in range(4) for d in range(2) if b or d]
COPY_SHIFTS = [
    {"z": a, "yl": b, "yh": d}
    for a in range(4)
    for b in range(2)
    for d in range(2)
    if a or b or d
]
WEIGHT_PLANE = [
    {"yh": a, "yl": a, "x": b, "core": d}
    for a in range(2)
    for b in range(4)
    for d in range(2)
    if a or b or d
]
WEIGHT_CHIPS = [{"yh": a, "yl": a, "x": b} for a in range(2) for b in range(4) if a or b]
SAMPLE_SHIFTS = [
    {"yh": a, "yl": b, "x": d}
    for a in range(2)
    for b in range(2)
    for d in range(4)
    if a or b or d
]
HEAD_SHIFTS = [{"z": a, "core": b} for a in range(4) for b in range(2) if a or b]
RING_Y = [{"y": 1}, {"y": 3}]
RING_Z = [{"z": 1}, {"z": 3}, {"core": 1}, {"yl": 1, "core": 1}]
RING_X = [{"x": 1}, {"x": 3}, {"core": 1}]


def back(shift):
    return {axis: -step for axis, step in shift.items()}


class Net:
    def __init__(self, send_sems, recv_sems, local_sems):
        self.me = my_place()
        self.send_sems, self.recv_sems, self.local_sems = send_sems, recv_sems, local_sems
        self.count = 0
        self.locals = 0
        self.pending = []

    def enter(self, shifts, between):
        barrier = pltpu.get_barrier_semaphore()
        for shift in shifts:
            pl.semaphore_signal(
                barrier, inc=1, device_id=device_of(moved(self.me, shift)), device_id_type=MESH
            )
        between()
        pl.semaphore_wait(barrier, len(shifts))

    def send(self, src, dst, **shift):
        at = self.count
        self.count += 1
        copy = pltpu.make_async_remote_copy(
            src_ref=src,
            dst_ref=dst,
            send_sem=self.send_sems.at[at],
            recv_sem=self.recv_sems.at[at],
            device_id=device_of(moved(self.me, shift)),
            device_id_type=MESH,
        )
        copy.start()
        self.pending.append(copy.wait_send)
        return copy

    def spare(self):
        self.locals += 1
        return self.local_sems.at[self.locals - 1]

    def settle(self, copy):
        copy.wait()
        self.pending.remove(copy.wait)

    def local(self, src, dst):
        copy = pltpu.make_async_copy(src, dst, self.local_sems.at[self.locals])
        self.locals += 1
        copy.start()
        self.pending.append(copy.wait)
        return copy

    def swap(self, src, dst):
        return Swap(self, src, dst)

    def finish(self):
        for wait in self.pending:
            wait()


class Swap:
    def __init__(self, net, src, dst):
        me = net.me
        self.away = me["yl"] != me["core"]
        at = net.count
        net.count += 1
        self.remote = pltpu.make_async_remote_copy(
            src_ref=src,
            dst_ref=dst,
            send_sem=net.send_sems.at[at],
            recv_sem=net.recv_sems.at[at],
            device_id=device_of(moved(me, {"yl": 1, "core": 1})),
            device_id_type=MESH,
        )
        self.near = pltpu.make_async_copy(src, dst, net.spare())
        pl.when(self.away)(self.remote.start)
        pl.when(jnp.logical_not(self.away))(self.near.start)

    def wait(self):
        pl.when(self.away)(self.remote.wait)
        pl.when(jnp.logical_not(self.away))(self.near.wait)


def run_tasks(tasks):
    tasks = list(tasks)
    while tasks:
        left = []
        for task in tasks:
            try:
                next(task)
                left.append(task)
            except StopIteration:
                pass
        tasks = left


def unique(shifts):
    seen, out = set(), []
    for shift in shifts:
        key = tuple(sorted((k, v) for k, v in shift.items() if v))
        if key not in seen:
            seen.add(key)
            out.append(shift)
    return out


def comm_call(
    body, shifts, outs, scratch, cid, in_vmem, out_vmem, n_remote, n_local=1, first=None
):
    shifts = unique(shifts)

    def kernel(*refs):
        refs, sems = refs[:-3], refs[-3:]
        net = Net(*sems)
        net.enter(shifts, functools.partial(first, *refs) if first else lambda: None)
        drain(*(body(net, *refs) or ()))
        net.finish()

    vm = pl.BlockSpec(memory_space=pltpu.VMEM)
    hb = pl.BlockSpec(memory_space=pl.ANY)
    sm = pl.BlockSpec(memory_space=pltpu.SMEM)
    return pl.pallas_call(
        kernel,
        out_shape=[jax.ShapeDtypeStruct(s, d) for s, d in outs],
        in_specs=[sm if v is None else vm if v else hb for v in in_vmem],
        out_specs=[vm if v else hb for v in out_vmem],
        scratch_shapes=list(scratch)
        + [
            pltpu.SemaphoreType.DMA((n_remote,)),
            pltpu.SemaphoreType.DMA((n_remote,)),
            pltpu.SemaphoreType.DMA((n_local,)),
        ],
        compiler_params=pltpu.CompilerParams(
            collective_id=cid, has_side_effects=True, vmem_limit_bytes=63 << 20
        ),
    )


def drain(*tasks):
    run_tasks(tasks)


def step(task):
    next(task, None)


def gather_ring(net, axis, src, block, rows, pair="core"):
    me = net.me
    half = rows // 2
    low, high = (0, half), (half, half)

    def at(step, part=(0, rows)):
        return block(moved(me, {axis: step}), *part)

    def cut(part):
        return at(0, part) if src is None else src.at[..., pl.ds(*part), :]

    def send(step, part, shift):
        here = cut(part) if step == 0 else at(step, part)
        return net.send(here, at(step, part), **shift)

    right, left, other = {axis: 1}, {axis: -1}, {pair: 1}
    r0 = send(0, low, right)
    l1 = send(0, high, left)
    r1 = send(0, high, right)
    l0 = send(0, low, left)
    own = pair and send(0, (0, rows), other)
    yield
    r0.wait_recv()
    fr = send(-1, low, right)
    l1.wait_recv()
    fl = send(1, high, left)
    yield
    if not pair:
        for copy in (r1, l0, fr, fl):
            copy.wait_recv()
        return
    r1.wait_recv()
    cr = send(-1, (0, rows), other)
    l0.wait_recv()
    cl = send(1, (0, rows), other)
    yield
    fr.wait_recv()
    c2r = send(2, low, other)
    fl.wait_recv()
    c2l = send(2, high, other)
    yield
    for copy in (own, cr, cl, c2r, c2l):
        copy.wait_recv()


def add_rows(dst, terms, rows, step=32):
    def one(i, carry):
        at = pl.ds(pl.multiple_of(i * step, step), step)
        total = terms[0][at, :].astype(F32)
        for term in terms[1:]:
            total = total + term[at, :].astype(F32)
        dst[at, :] = total.astype(dst.dtype)
        return carry

    lax.fori_loop(0, rows // step, one, 0)


def reduce_ring(net, axis, part, index, total, rc, rh, r, extra=()):
    me = net.me
    low, high = pl.ds(0, 64), pl.ds(64, 64)
    right, left, other = {axis: 1}, {axis: -1}, {"core": 1}

    def at(step, core, rows=pl.ds(0, 128)):
        return part.at[index(moved(me, {axis: step, "core": core})), rows]

    def add(step, rows, n, *more):
        add_rows(rc.at[step, rows], [at(step, 0, rows), rc.at[step, rows], *more], n)

    cc = {}
    for step in (2, 1, 3, 0):
        cc[step] = net.send(at(step, 1), rc.at[step], **other)
    yield
    cc[2].wait_recv()
    add(2, low, 64)
    h_r = net.send(rc.at[2, low], rh.at[0], **right)
    add(2, high, 64)
    h_l = net.send(rc.at[2, high], rh.at[1], **left)
    cc[1].wait_recv()
    add(1, high, 64)
    r_high = net.send(rc.at[1, high], r.at[0, high], **right)
    cc[3].wait_recv()
    add(3, low, 64)
    l_low = net.send(rc.at[3, low], r.at[1, low], **left)
    yield
    h_r.wait_recv()
    add(1, low, 64, rh.at[0])
    r_low = net.send(rc.at[1, low], r.at[0, low], **right)
    h_l.wait_recv()
    add(3, high, 64, rh.at[1])
    l_high = net.send(rc.at[3, high], r.at[1, high], **left)
    yield
    for copy in (cc[0], r_high, l_low, r_low, l_high):
        copy.wait_recv()
    add_rows(total, [at(0, 0), rc.at[0], r.at[0], r.at[1], *extra], 128)


def reduce_ring_tiles(net, axis, part, index, total, rc, rh, r):
    me = net.me
    low, high = pl.ds(0, 64), pl.ds(64, 64)
    right, left, other = {axis: 1}, {axis: -1}, {"core": 1}

    def at(step, core, rows=pl.ds(0, 128)):
        return part.at[index(moved(me, {axis: step, "core": core})), rows]

    def add(step, rows, n, *more):
        add_rows(rc.at[step, rows], [at(step, 0, rows), rc.at[step, rows], *more], n)

    def over(step):
        return net.send(at(step, 1), rc.at[step], **other)

    c2 = over(2)
    yield
    c1 = over(1)
    c2.wait_recv()
    add(2, low, 64)
    h_r = net.send(rc.at[2, low], rh.at[0], **right)
    add(2, high, 64)
    h_l = net.send(rc.at[2, high], rh.at[1], **left)
    yield
    c3 = over(3)
    c1.wait_recv()
    add(1, high, 64)
    r_high = net.send(rc.at[1, high], r.at[0, high], **right)
    yield
    c0 = over(0)
    c3.wait_recv()
    add(3, low, 64)
    l_low = net.send(rc.at[3, low], r.at[1, low], **left)
    h_r.wait_recv()
    add(1, low, 64, rh.at[0])
    r_low = net.send(rc.at[1, low], r.at[0, low], **right)
    h_l.wait_recv()
    add(3, high, 64, rh.at[1])
    l_high = net.send(rc.at[3, high], r.at[1, high], **left)
    yield
    for copy in (c0, r_high, l_low, r_low, l_high):
        copy.wait_recv()
    add_rows(total, [at(0, 0), rc.at[0], r.at[0], r.at[1]], 128)


TILES = (2, 1, 3, 0)


def reduce_ring_scratch(width):
    return [
        pltpu.VMEM((4, 128, width), BF),
        pltpu.VMEM((2, 64, width), BF),
        pltpu.VMEM((2, 128, width), BF),
    ]


def by_x_then_y(net, pick, out):
    me = net.me
    mine = out.at[me["yh"], tp_of(me), me["yl"]]
    kept = net.local(pick(me), mine)
    copies = [net.send(pick(moved(me, shift)), mine, **shift) for shift in TP_SHIFTS]
    yield
    for copy in copies:
        copy.wait_recv()
    net.settle(kept)

    def block(place, lo, n):
        return out.at[place["yh"], pl.ds(lo, n), place["yl"]]

    yield from gather_ring(net, "y", None, block, 8, None)


def gather_heads_weights(net, wq, wk, wv, small, stage, out, small_out):
    me = net.me
    mine = fsdp_of(me)
    staged = []
    rows = pl.ds(pl.multiple_of(me["yl"] * 32, 32), 32)
    for core in range(2):
        h = me["z"] * 2 + core
        place = stage.at[core]
        for src, n, lane in ((wq, 256, 0), (wk, 128, 256), (wv, 128, 384)):
            columns = src.at[rows, pl.ds(pl.multiple_of(h * n, n), n)]
            staged.append(net.local(columns, place.at[:, pl.ds(lane, n)]))
    yield
    for copy in staged:
        net.settle(copy)
    task = by_x_then_y(net, lambda place: stage.at[place["core"]], out)
    next(task)
    kept = net.local(small, small_out.at[mine])
    copies = [net.send(small, small_out.at[mine], **shift) for shift in WEIGHT_PLANE]
    yield
    yield from task
    for copy in copies:
        copy.wait_recv()
    net.settle(kept)


def gather_out_weights(net, src, mid, out):
    me = net.me
    mine = chip_of(me)
    stay = net.local(src.at[mine], mid.at[mine])
    first = [
        net.send(src.at[chip_of(moved(me, shift))], mid.at[mine], **shift) for shift in WEIGHT_CHIPS
    ]
    yield
    for copy in first:
        copy.wait_recv()
    net.settle(stay)
    place = out.at[me["core"], mine]
    kept = net.local(mid.at[head_of(me)], place)
    copies = [
        net.send(mid.at[head_of(moved(me, shift))], place, **shift) for shift in WEIGHT_PLANE
    ]
    yield
    for copy in copies:
        copy.wait_recv()
    net.settle(kept)


def pack_columns(src, stage, lane):
    first = lax.broadcasted_iota(jnp.int32, (64, 256), 1) < 64
    for j in range(8):
        low = 192 * j - 64 * (j % 2)
        a = src[:, low : low + 256].astype(F32)
        b = src[:, 1536 + low : 1536 + low + 256].astype(F32)
        if j % 2:
            a = pltpu.roll(a, 192, 1)
        else:
            b = pltpu.roll(b, 64, 1)
        rest = jnp.where(first, jnp.concatenate([a[:, 128:], a[:, 128:]], axis=1), b)
        stage[j, :, lane : lane + 128] = a[:, :128].astype(BF)
        stage[j, :, lane + 128 : lane + 384] = rest.astype(BF)


def gather_ff_weights(net, down, stage, out, down_out):
    me = net.me
    rows = pl.ds(pl.multiple_of(me["yl"] * 32, 32), 32)
    task = by_x_then_y(net, lambda place: stage.at[tp_of(place), rows], out)
    next(task)
    kept = net.local(down, down_out.at[me["yh"]])
    copy = net.send(down, down_out.at[me["yh"]], yh=1, yl=1)
    yield
    yield from task
    copy.wait_recv()
    net.settle(kept)


def chunk_of(place):
    return chip_of(place) * 2 + place["yl"]


def scatter_samples(net, pick, out):
    me = net.me
    mine = chunk_of(me)
    kept = net.local(pick(me), out.at[mine])
    copies = [net.send(pick(moved(me, shift)), out.at[mine], **shift) for shift in SAMPLE_SHIFTS]
    yield
    for copy in copies:
        copy.wait_recv()
    net.settle(kept)


def reduce_ff(net, g, d, rhg, rhd, rg, rd, tg, td, zg, zd, gsum, dsum):
    me = net.me
    ring = ({"y": 1}, {"y": -1})
    some = [pl.ds(0, 2), pl.ds(2, 2)]

    def terms(step, h):
        to = moved(me, {"y": step})
        return g.at[to["yh"], some[h], to["yl"]], d.at[to["yh"], to["yl"], some[h]]

    def send(step, h, dst_g, dst_d, to):
        src_g, src_d = terms(step, h)
        return [net.send(src_g, dst_g, **to), net.send(src_d, dst_d, **to)]

    half = [send(2, h, rhg.at[h], rhd.at[h], ring[h]) for h in range(2)]
    near = send(1, 1, rg.at[0, 1], rd.at[0, 1], ring[0])
    near += send(-1, 0, rg.at[1, 0], rd.at[1, 0], ring[1])
    yield
    for h, step in ((0, 1), (1, -1)):
        for copy in half[h]:
            copy.wait_recv()
        own_g, own_d = terms(step, h)
        for k in range(2):
            add_rows(rhg.at[h, k], [own_g.at[k], rhg.at[h, k]], 64)
            add_rows(rhd.at[h, k], [own_d.at[k], rhd.at[h, k]], 192)
        near.append(net.send(rhg.at[h], rg.at[h, h], **ring[h]))
        near.append(net.send(rhd.at[h], rd.at[h, h], **ring[h]))
    yield
    for copy in near:
        copy.wait_recv()
    for h in range(2):
        own_g, own_d = terms(0, h)
        for k in range(2):
            add_rows(tg.at[2 * h + k], [own_g.at[k], rg.at[0, h, k], rg.at[1, h, k]], 64)
            add_rows(td.at[2 * h + k], [own_d.at[k], rd.at[0, h, k], rd.at[1, h, k]], 192)
    copies = []
    for k in range(3):
        to = moved(me, {"z": k + 1})
        copies.append(net.send(tg.at[to["z"]], zg.at[k], z=k + 1))
        copies.append(net.send(td.at[to["z"]], zd.at[k], z=k + 1))
    yield
    for copy in copies:
        copy.wait_recv()
    add_rows(gsum, [tg.at[me["z"]]] + [zg.at[k] for k in range(3)], 64)
    add_rows(dsum, [td.at[me["z"]]] + [zd.at[k] for k in range(3)], 192)


def reduce_ff_scratch():
    shapes = [(64, 768), (192, 128)]
    out = []
    for lead in ((2, 2), (2, 2, 2), (4,), (3,), ()):
        out += [pltpu.VMEM(lead + s, BF) for s in shapes]
    return out


def exchange(net, src, out, shifts, index):
    me = net.me
    mine = index(me)
    kept = net.local(src.at[mine], out.at[mine])
    copies = [net.send(src.at[index(moved(me, shift))], out.at[mine], **shift) for shift in shifts]
    yield
    for copy in copies:
        copy.wait_recv()
    net.settle(kept)


def unpack_columns(src, lane, out):
    first = lax.broadcasted_iota(jnp.int32, (64, 128), 1) < 64

    def tile(j, k):
        return src[j, :, lane + 128 * k : lane + 128 * k + 128].astype(F32)

    def half(t):
        return pltpu.roll(t, 64, 1)

    for pair in range(4):
        j, n = 2 * pair, 2 * pair + 1
        a = [tile(j, k) for k in range(3)]
        b = [tile(n, k) for k in range(3)]
        low = (
            a[0],
            jnp.where(first, a[1], half(b[0])),
            jnp.where(first, half(b[0]), half(b[1])),
        )
        high = (
            jnp.where(first, half(a[1]), half(a[2])),
            jnp.where(first, half(a[2]), b[1]),
            b[2],
        )
        for base, tiles in ((3 * pair, low), (12 + 3 * pair, high)):
            for k, t in enumerate(tiles):
                out[:, 128 * (base + k) : 128 * (base + k) + 128] = t.astype(BF)


def sum_everywhere(net, own, first, middle, second, total):
    stages = ((own, first, TP_SHIFTS, middle), (middle, second, COPY_SHIFTS, total))
    for src, slots, shifts, dst in stages:
        copies = [net.send(src, slots.at[k], **shift) for k, shift in enumerate(shifts)]
        yield
        for copy in copies:
            copy.wait_recv()
        dst[...] = src[...] + jnp.sum(slots[...], axis=0)


def rope_frequency():
    half = jnp.exp(jnp.arange(0, HEAD // 2, dtype=F32) * (-2.0 * math.log(1000000.0) / HEAD))
    return jnp.concatenate([half, half])[None]


def across_rows(a, b):
    return lax.dot_general(a, b, (((0,), (0,)), ((), ())), preferred_element_type=F32)


def against_cols(a, b):
    return lax.dot_general(a, b, (((1,), (1,)), ((), ())), preferred_element_type=F32)


def forward_dot(a, b):
    return jnp.dot(a, b, preferred_element_type=F32)


EXP2_SCALE = HEAD ** (-0.5) * math.log2(math.e)


def norm_scale(v):
    return lax.rsqrt(jnp.mean(v * v, axis=-1, keepdims=True) + 1e-06)


def visible_tile(lk, lq, sq):
    later = jnp.where(lk < 512, 4096, lk)
    later, lk = jnp.concatenate([later, later], axis=1), jnp.concatenate([lk, lk], axis=1)
    return (lk <= lq) & (later >= sq)


def half_loop(body, part, parts, count):
    lax.fori_loop(part * count // parts, (part + 1) * count // parts, body, 0)


class Front:
    def __init__(self, m, gains, wqkv, wo, xs, tables, saved, part, mixed, vt):
        self.gains, self.wqkv, self.wo, self.xs = gains, wqkv, wo, xs.at[m]
        self.cos, self.sin, self.lk, self.lq, self.sq = (t.at[m] for t in tables)
        self.xn, self.raw, self.q, self.k, self.v, self.mixt, self.rl = (t.at[m] for t in saved)
        self.part, self.mixed, self.vt = part.at[m], mixed, vt

    def project(self, i, carry):
        rows = pl.ds(pl.multiple_of(i * 256, 256), 256)
        x = self.xs[pl.ds(i * 2, 2)].reshape(256, 1024).astype(F32)
        low = (x * norm_scale(x) * self.gains[0:1, :]).astype(BF)
        self.xn[rows, :] = low
        y = forward_dot(low, self.wqkv[...].reshape(1024, 512))
        self.raw[rows, :] = y[:, :384]
        c, s = self.cos[rows, :], self.sin[rows, :]
        for head in range(3):
            u = y[:, head * HEAD : (head + 1) * HEAD]
            lane = HEAD * (head // 2)
            n = u * norm_scale(u) * self.gains[2:3, lane : lane + HEAD]
            turned = (n * c + pltpu.roll(n, HEAD // 2, 1) * s).astype(BF)
            if head < 2:
                self.q[head, rows, :] = turned
            else:
                self.k[rows, :] = turned
        value = y[:, 384:]
        self.v[rows, :] = value.astype(BF)
        self.vt[:, rows] = value.T.astype(BF)
        return carry

    def attend(self, head, i, carry):
        rows = pl.ds(pl.multiple_of(i * 256, 256), 256)
        s = against_cols(self.k[...], self.q[head, rows, :])
        seen = visible_tile(self.lk[...], self.lq[:, rows], self.sq[:, rows])
        e = jnp.where(seen, jnp.exp2(s * EXP2_SCALE), 0.0)
        inv = 1.0 / jnp.sum(e, axis=0, keepdims=True)
        self.rl[head, :, rows] = inv
        m = forward_dot(self.vt[...], e.astype(BF)) * inv
        self.mixt[head * HEAD : (head + 1) * HEAD, rows] = m.astype(BF)
        self.mixed[rows, head * HEAD : (head + 1) * HEAD] = m.T.astype(BF)
        return carry

    def project_out(self, i, carry):
        rows = pl.ds(pl.multiple_of(i * 256, 256), 256)
        y = forward_dot(self.mixed[rows, :], self.wo[...].reshape(256, 1024)).astype(BF)
        self.part[pl.ds(i * 2, 2)] = y.reshape(2, 128, 1024)
        return carry

    def projection(self):
        half_loop(self.project, 0, 1, 4)

    def tile(self, i):
        self.attend(0, i, 0)
        self.attend(1, i, 0)
        self.project_out(i, 0)


def make_tables(m, table, first, frequency, cos, sin, lk):
    row = lax.broadcasted_iota(jnp.int32, (64, HEAD), 0)
    lane = lax.broadcasted_iota(jnp.int32, (64, HEAD), 1)
    for b in range(16):
        rows = slice(64 * b, 64 * b + 64)
        at = table[m, b] * 64 + row
        lk[m, rows, :] = at
        later = jnp.where(at < 512 + first[m, 0], at + (384 - first[m, 0]), at - 128)
        angle = jnp.where(at < 512, at, later).astype(F32) * frequency[...]
        cos[m, rows, :] = jnp.cos(angle)
        turn = jnp.sin(angle)
        sin[m, rows, :] = jnp.where(lane < HEAD // 2, -turn, turn)


def sequence_block(out):
    def block(place, lo, n):
        return out.at[head_of(place), pl.ds(lo, n)]

    return block


def front_first(*refs):
    table, first, frequency = refs[10:13]
    make_tables(0, table, first, frequency, *refs[-3:])


def front_body(
    net,
    tok, cot, small, wq, wk, wv, wo_in, wg, wu, wd, table, first, frequency, lq, sq,
    cos_out, sin_out, lk_out, attended, normed, gains, wqkv_out, wo_out, cots, wgu, wds, mid,
    xn_out, raw_out, q_out, k_out, v_out, mixt_out, rl_out,
    xn, raw, q, k, v, mixt, rl,
    xs, part, mixed, vt, stage, smalls, gu_stage, outbox, inbox, *bufs,
):
    me = net.me
    wqkv, wo, cos, sin, lk = bufs[-5:]
    heads = gather_heads_weights(net, wq, wk, wv, small, stage, wqkv, smalls)
    next(heads)
    swaps = [net.swap(tok.at[m], xs.at[m, ctx_of(me)]) for m in range(2)]
    gather = [
        gather_ring(net, "z", xs.at[m, head_of(me)], sequence_block(xs.at[m]), 128)
        for m in range(2)
    ]
    outs = gather_out_weights(net, wo_in, mid, wo)
    feed = gather_ff_weights(net, wd, gu_stage, wgu, wds)

    def cot_block(place, lo, n):
        return cots.at[:, tp_of(place), pl.ds(lo, n)]

    cots_in = gather_ring(net, "x", cot, cot_block, 128)
    own_cot = net.local(cot, cots.at[:, tp_of(me)])
    next(heads)
    make_tables(1, table, first, frequency, cos, sin, lk)
    for src, dst in ((cos, cos_out), (sin, sin_out), (lk, lk_out)):
        net.local(src, dst)
    swaps[0].wait()
    next(gather[0])
    next(heads)
    next(outs)
    next(cots_in)
    pack_columns(wg, gu_stage, 0)
    pack_columns(wu, gu_stage, 384)
    next(feed)
    next(gather[0])
    swaps[1].wait()
    next(gather[1])
    next(heads)
    next(gather[0])
    drain(gather[0])
    drain(heads)
    next(outs)
    next(feed)
    next(cots_in)
    pairs = [smalls[2 * i].astype(F32) + smalls[2 * i + 1].astype(F32) for i in range(8)]
    both = sum(pairs[1:], pairs[0])
    gains[...] = jnp.zeros_like(gains)
    gains[0:1, :] = jnp.concatenate([p[0:1] for p in pairs], axis=1)
    gains[1:2, :] = jnp.concatenate([p[1:2] for p in pairs], axis=1)
    gains[2:3, : 2 * HEAD] = jnp.concatenate([both[2:3], both[3:4]], axis=1)
    tables = (cos, sin, lk, lq, sq)
    saved = (xn, raw, q, k, v, mixt, rl)
    work = [Front(m, gains, wqkv, wo, xs, tables, saved, part, mixed, vt) for m in range(2)]

    def save(m):
        for src, dst in zip(saved, (xn_out, raw_out, q_out, k_out, v_out, mixt_out, rl_out)):
            net.local(src.at[m], dst.at[m])

    def settle(m):
        x = tok[m].astype(F32) + inbox[m].astype(F32)
        attended[m] = x
        normed[m] = (x * norm_scale(x) * gains[1:2, :]).astype(BF)

    def reduce(m):
        buf = bufs[3 * m : 3 * m + 3]
        yield from reduce_ring_tiles(net, "z", part.at[m], head_of, outbox.at[m], *buf)
        swap = net.swap(outbox.at[m], inbox.at[m])
        yield
        swap.wait()
        settle(m)

    reduces = [reduce(m) for m in range(2)]
    work[0].projection()
    step(gather[1])
    drain(outs)
    for k in TILES:
        work[0].tile((me["z"] + k) % 4)
        next(reduces[0])
        step(gather[1])
        if k == 3:
            step(feed)
    step(cots_in)
    drain(gather[1])
    save(0)
    net.local(wqkv, wqkv_out)
    net.local(wo, wo_out)
    work[1].projection()
    step(reduces[0])
    for at, k in enumerate(TILES):
        work[1].tile((me["z"] + k) % 4)
        next(reduces[1])
        if at == 1:
            drain(reduces[0])
            step(cots_in)
    save(1)
    drain(reduces[1])
    drain(cots_in)
    drain(feed)


class Feed:
    def __init__(self, m, wgu, wd, nm, ct, hid, ggu, out, mid, dg, dd):
        self.m, self.wgu, self.wd = m, wgu, wd
        self.nm, self.ct, self.hid, self.ggu = nm.at[m], ct.at[m], hid.at[m], ggu.at[m]
        self.out, self.mid, self.dg, self.dd = out.at[m], mid.at[m], dg, dd

    def tile(self, i):
        rows = pl.ds(pl.multiple_of(i * 256, 256), 256)
        blocks = pl.ds(i * 2, 2)
        wgu = self.wgu[...].reshape(1024, 768)
        wd = self.wd[...].reshape(384, 1024)
        y = forward_dot(self.nm[blocks].reshape(256, 1024), wgu)
        gate, up = y[:, :384], y[:, 384:]
        gh = against_cols(self.ct[blocks].reshape(256, 1024), wd)
        sig = 1.0 / (1.0 + jnp.exp(-gate))
        silu = gate * sig
        hidden = (silu * up).astype(BF)
        self.hid[rows, :] = hidden
        gg = (gh * up * sig * (1.0 + gate * (1.0 - sig))).astype(BF)
        gu = (gh * silu).astype(BF)
        self.ggu[rows, :384] = gg
        self.ggu[rows, 384:] = gu
        self.mid[blocks] = (
            against_cols(self.ggu[rows, :], wgu).astype(BF).reshape(2, 128, 1024)
        )
        self.out[blocks] = forward_dot(hidden, wd).astype(BF).reshape(2, 128, 1024)

    def in_weights(self):
        def some(i, carry):
            at = pl.ds(pl.multiple_of(i * 128, 128), 128)
            y = across_rows(self.nm[:, :, at].reshape(1024, 128), self.ggu[...])
            self.dg[at, :] = y if self.m == 0 else self.dg[at, :] + y
            return carry

        lax.fori_loop(0, 8, some, 0)

    def down_weights(self):
        def some(i, carry):
            at = pl.ds(pl.multiple_of(i * 128, 128), 128)
            y = across_rows(self.hid[:, at], self.ct[...].reshape(1024, 1024))
            self.dd[at, :] = y if self.m == 0 else self.dd[at, :] + y
            return carry

        lax.fori_loop(0, 3, some, 0)


def feed_body(
    net,
    normed, attended, cot, cots_in, wgu_in, wds_in, gains,
    g_attended, g_attn, gain_sum, dg_low, dd_low, out_part_out,
    nm, hid, ggu, out_part, mid_part, dg, dd, total, cots, wgu, wds, *bufs,
):
    me = net.me
    loads = [net.local(*pair) for pair in ((wgu_in, wgu), (wds_in, wds), (cots_in, cots))]

    def block(m):
        def at(place, lo, n):
            return nm.at[m, tp_of(place), pl.ds(lo, n)]

        return at

    own = [net.local(normed.at[m], nm.at[m, tp_of(me)]) for m in range(2)]
    gather = [gather_ring(net, "x", normed.at[m], block(m), 128) for m in range(2)]
    next(gather[0])
    next(gather[0])
    next(gather[1])
    for copy in own + loads:
        net.settle(copy)
    drain(gather[0])
    work = [Feed(m, wgu, wds, nm, cots, hid, ggu, out_part, mid_part, dg, dd) for m in range(2)]
    gain_sum[...] = jnp.zeros_like(gain_sum)

    def settle(m):
        x, g_mid = attended[m], total[m]
        r = norm_scale(x)
        n = g_mid * gains[1:2, :]
        gain_sum[0:1, :] += jnp.sum(g_mid * x * r, axis=0, keepdims=True)
        y = cot[m].astype(F32) + r * n - x * (r * r * r) * jnp.mean(n * x, axis=-1, keepdims=True)
        g_attended[m] = y
        g_attn[m] = y.astype(BF)

    def reduce(m):
        buf = bufs[3 * m : 3 * m + 3]
        yield from reduce_ring_tiles(net, "x", mid_part.at[m], tp_of, total.at[m], *buf)
        settle(m)

    reduces = [reduce(m) for m in range(2)]
    for k in TILES:
        work[0].tile((me["x"] + k) % 4)
        next(reduces[0])
        step(gather[1])
    net.local(out_part.at[0], out_part_out.at[0])
    drain(gather[1])
    for at, k in enumerate(TILES):
        work[1].tile((me["x"] + k) % 4)
        next(reduces[1])
        if at == 1:
            drain(reduces[0])
    net.local(out_part.at[1], out_part_out.at[1])
    for one in work:
        one.in_weights()
        one.down_weights()
    drain(reduces[1])
    dg_low[...] = dg[...].astype(BF).reshape(2, 4, 2, 64, 768)
    for c in range(8):
        dd_low[:, c % 2, c // 2] = dd[:, 128 * c : 128 * c + 128].astype(BF).reshape(2, 192, 128)


class Back:
    def __init__(self, m, gains, wqkv, wo, g, tables, saved, part, graw, dwqkv, dwo, sums, work):
        self.m, self.gains, self.wqkv, self.wo, self.g = m, gains, wqkv, wo, g.at[m]
        self.cos, self.sin, self.lk, self.lq, self.sq = (t.at[m] for t in tables)
        self.xn, self.raw, self.q, self.k, self.v, self.mixt, self.rl = (t.at[m] for t in saved)
        self.part, self.graw = part.at[m], graw.at[m]
        self.dwqkv, self.dwo, self.sums = dwqkv, dwo, sums
        self.kt, self.dk, self.dv, self.dq = work

    def begin(self):
        self.kt[...] = self.k[...].astype(F32).T.astype(BF)
        self.dk[...] = jnp.zeros_like(self.dk)
        self.dv[...] = jnp.zeros_like(self.dv)

    def attend(self, head, i, carry):
        rows = pl.ds(pl.multiple_of(i * 256, 256), 256)
        at = slice(head * HEAD, (head + 1) * HEAD)
        g = self.g[pl.ds(i * 2, 2)].reshape(256, 1024)
        wo = self.wo[head].reshape(HEAD, 1024)
        gm = against_cols(g, wo).astype(BF)
        gmt = against_cols(wo, g).astype(BF)
        delta = jnp.sum(
            gmt.astype(F32) * self.mixt[at, rows].astype(F32), axis=0, keepdims=True
        )
        qt = self.q[head, rows, :]
        s = against_cols(self.k[...], qt)
        seen = visible_tile(self.lk[...], self.lq[:, rows], self.sq[:, rows])
        p = jnp.where(seen, jnp.exp2(s * EXP2_SCALE), 0.0) * self.rl[head, :, rows]
        dp = forward_dot(self.v[...], gmt)
        ds = (p * (dp - delta)).astype(BF)
        self.dv[...] += forward_dot(p.astype(BF), gm)
        self.dk[...] += forward_dot(ds, qt)
        self.dq[head, rows, :] = forward_dot(self.kt[...], ds).T
        return carry

    def unproject(self, i, carry):
        rows = pl.ds(pl.multiple_of(i * 256, 256), 256)
        c, s = self.cos[rows, :], self.sin[rows, :]
        for head in range(3):
            lane = head // 2
            at = slice(head * HEAD, (head + 1) * HEAD)
            gr = (self.dq[head, rows, :] if head < 2 else self.dk[rows, :]) * HEAD ** (-0.5)
            gu = gr * c - pltpu.roll(gr, HEAD // 2, 1) * s
            u = self.raw[rows, at]
            r = norm_scale(u)
            self.sums[lane : lane + 1, :] += jnp.sum(gu * (u * r), axis=0, keepdims=True)
            n = gu * self.gains[2:3, lane * HEAD : (lane + 1) * HEAD]
            d = r * n - u * (r * r * r) * jnp.mean(n * u, axis=-1, keepdims=True)
            self.graw[rows, at] = d.astype(BF)
        self.graw[rows, 384:] = self.dv[rows, :].astype(BF)
        y = against_cols(self.graw[rows, :], self.wqkv[...].reshape(1024, 512))
        self.part[pl.ds(i * 2, 2)] = y.astype(BF).reshape(2, 128, 1024)
        return carry

    def pieces(self):
        return (
            [self.begin]
            + [
                functools.partial(half_loop, functools.partial(self.attend, head), p, 2, 4)
                for head in range(2)
                for p in range(2)
            ]
            + [functools.partial(half_loop, self.unproject, p, 2, 4) for p in range(2)]
        )

    def out_weights(self):
        def some(i, carry):
            at = pl.ds(pl.multiple_of(i * 256, 256), 256)
            y = forward_dot(self.mixt[...], self.g[:, :, at].reshape(1024, 256))
            self.dwo[:, at] = y if self.m == 0 else self.dwo[:, at] + y
            return carry

        lax.fori_loop(0, 4, some, 0)

    def head_weights(self):
        def some(i, carry):
            at = pl.ds(pl.multiple_of(i * 256, 256), 256)
            y = across_rows(self.xn[:, at], self.graw[...])
            self.dwqkv[at, :] = y if self.m == 0 else self.dwqkv[at, :] + y
            return carry

        lax.fori_loop(0, 4, some, 0)


def back_body(
    net,
    g_own, tok, gain_sum, dg_in, dd_in, out_part_in,
    xn_in, raw_in, q_in, k_in, v_in, mixt_in, rl_in,
    wqkv_in, wo_in_, gains, cos_in, sin_in, lk_in, lq, sq,
    in_sum, out_sum, gain_total,
    gq, gk, gv, gwo, gate, up, gwd,
    xn, raw, q, k, v, mixt, rl,
    g, out_part, part, graw, dwqkv, dwo, kt, dk, dv, dq, outbox, sums,
    qkv_low, wo_low, qkv_in, wo_in, qkv_sum, wo_sum, qkv_all, wo_all, wo_mid, gu_all, gu_out,
    heads_out, outs_out, down_out,
    gain_own, gain_first, gain_middle, gain_second, *bufs,
):
    me = net.me
    ff, bufs = bufs[:10], bufs[10:]
    dg, dd, wqkv, wo, cos, sin, lk = bufs[-7:]
    swaps = [net.swap(g_own.at[m], g.at[m, ctx_of(me)]) for m in range(2)]
    fetched = [net.local(out_part_in.at[0], out_part.at[0])]
    saved = (xn, raw, q, k, v, mixt, rl)
    needed = [
        net.local(src.at[m], dst.at[m])
        for m in range(2)
        for src, dst in zip((xn_in, raw_in, q_in, k_in, v_in, mixt_in, rl_in), saved)
    ]
    fetched.append(net.local(out_part_in.at[1], out_part.at[1]))
    needed += [
        net.local(*pair)
        for pair in (
            (dg_in, dg), (dd_in, dd), (wqkv_in, wqkv), (wo_in_, wo),
            (cos_in, cos), (sin_in, sin), (lk_in, lk),
        )
    ]
    sums[...] = jnp.zeros_like(sums)
    gather = [
        gather_ring(net, "z", g.at[m, head_of(me)], sequence_block(g.at[m]), 128) for m in range(2)
    ]
    outs = [
        reduce_ring(net, "x", out_part.at[m], tp_of, out_sum.at[m], *bufs[3 * m + 6 : 3 * m + 9])
        for m in range(2)
    ]
    gsum, dsum = ff[-2:]

    def feed_gradients():
        yield from reduce_ff(net, dg, dd, *ff)
        kept = [
            net.local(gsum, gu_all.at[ctx_of(me)]),
            net.local(dsum, down_out.at[ctx_of(me)]),
        ]
        spreads = [
            gather_ring(
                net, "z", src, lambda place, lo, n, out=out: out.at[ctx_of(place), pl.ds(lo, n)],
                rows, "yl",
            )
            for src, out, rows in ((gsum, gu_all, 64), (dsum, down_out, 192))
        ]
        for _ in range(4):
            for spread in spreads:
                next(spread)
            yield
        drain(*spreads)
        for copy in kept:
            net.settle(copy)
        yield from exchange(net, gu_all, gu_out, TP_SHIFTS, tp_of)

    feed = feed_gradients()
    swaps[0].wait()
    next(gather[0])
    net.settle(fetched[0])
    next(outs[0])
    next(gather[0])
    swaps[1].wait()
    next(gather[1])
    next(gather[0])
    drain(gather[0])
    for copy in needed:
        net.settle(copy)
    next(feed)
    net.settle(fetched[1])
    tables = (cos, sin, lk, lq, sq)
    work = [
        Back(m, gains, wqkv, wo, g, tables, saved, part, graw, dwqkv, dwo, sums, (kt, dk, dv, dq))
        for m in range(2)
    ]
    for at, piece in enumerate(work[0].pieces()):
        piece()
        step(gather[1])
        if at in (1, 3, 5):
            step(outs[0])
    drain(gather[1])
    def reduce(m):
        yield from reduce_ring(net, "z", part.at[m], head_of, outbox.at[m], *bufs[3 * m : 3 * m + 3])
        swap = net.swap(outbox.at[m], in_sum.at[m])
        yield
        swap.wait()

    reduces = [reduce(m) for m in range(2)]
    next(reduces[0])
    drain(outs[0])
    next(outs[1])
    for at, piece in enumerate(work[1].pieces()):
        piece()
        if at in (1, 3, 5):
            step(reduces[0])
        if at in (2, 4, 6):
            step(outs[1])
        if at in (2, 4, 6):
            step(feed)
    next(reduces[1])
    work[0].head_weights()
    step(reduces[1])
    step(reduces[0])
    work[1].head_weights()
    qkv_low[...] = dwqkv[...].astype(BF).reshape(16, 64, 512)
    scattered = [
        scatter_samples(net, lambda place: qkv_low.at[chunk_of(place)], qkv_in),
        scatter_samples(net, lambda place: wo_low.at[place["yl"], chip_of(place)], wo_in),
    ]
    next(scattered[0])
    step(reduces[1])
    step(feed)
    work[0].out_weights()
    step(reduces[1])
    work[1].out_weights()
    low = dwo[...].astype(BF)
    for half in range(2):
        wo_low[:, :, half * 16 : half * 16 + 16, :] = low[:, half * 512 : half * 512 + 512].reshape(
            2, 8, 16, 512
        )
    next(scattered[1])
    drain(*reduces)
    drain(outs[1])
    step(feed)
    row = jnp.zeros((1, 1024), F32)
    for m in range(2):
        x = tok[m].astype(F32)
        row = row + jnp.sum(in_sum[m].astype(F32) * x * norm_scale(x), axis=0, keepdims=True)
    for k in range(8):
        at = slice(k * 128, k * 128 + 128)
        gain_own[k : k + 1, :] = row[:, at]
        gain_own[8 + k : 9 + k, :] = gain_sum[0:1, at]
    gain_own[16:24, :] = sums[...]
    gain = sum_everywhere(net, gain_own, gain_first, gain_middle, gain_second, gain_total)
    next(gain)
    drain(*scattered)
    qkv_sum[...] = jnp.sum(qkv_in[...].astype(F32), axis=0).astype(BF)
    wo_sum[...] = jnp.sum(wo_in[...].astype(F32), axis=0).astype(BF)
    kept = [
        net.local(qkv_sum, qkv_all.at[head_of(me)]),
        net.local(wo_sum, wo_all.at[head_of(me)]),
    ]
    spreads = [
        gather_ring(net, "z", src, sequence_block(out), rows)
        for src, out, rows in ((qkv_sum, qkv_all, 64), (wo_sum, wo_all, 32))
    ]
    for task in spreads:
        next(task)
    step(feed)
    next(gain)
    drain(*spreads)
    for copy in kept:
        net.settle(copy)
    heads_back = net.swap(qkv_all, heads_out)
    drain(exchange(net, wo_all, wo_mid, CHIP_SHIFTS, chip_of))
    outs_back = net.swap(wo_mid, outs_out)
    drain(gain)
    heads_back.wait()
    for h in range(8):
        gq[:, 256 * h : 256 * h + 256] = heads_out[h, :, :256]
        gk[:, 128 * h : 128 * h + 128] = heads_out[h, :, 256:384]
        gv[:, 128 * h : 128 * h + 128] = heads_out[h, :, 384:]
    drain(feed)
    for c in range(8):
        gwd[:, 128 * c : 128 * c + 128] = down_out[c]
    for k, dst in enumerate((gate, up)):
        unpack_columns(gu_out, 384 * k, dst)
    outs_back.wait()
    for i in range(8):
        for half in range(2):
            rows = slice(16 * half, 16 * half + 16)
            gwo[16 * i : 16 * i + 16, 512 * half : 512 * half + 512] = outs_out[i, rows, :]


def token_places(block_table, first, seq):
    blocks = block_table.shape[1]
    block = seq // blocks
    logical = (
        jnp.repeat(block_table, block, axis=1) * block + jnp.arange(seq, dtype=jnp.int32) % block
    )
    prompt = seq // 2
    segment = jnp.where(logical < prompt, 0, jnp.where(logical < prompt + first, 1, 2))
    return logical, segment


def per_device(
    tokens,
    cotangent,
    block_table,
    segment_ids,
    positions,
    gain_attn,
    w_query,
    key_projection,
    value_projection,
    query_norm_gain,
    key_norm_gain,
    w_out,
    gain_ffn,
    w_gate,
    w_up,
    w_down,
):
    ctx = lax.axis_index("ctx")
    mbs, width = tokens.shape[0], tokens.shape[-1]
    tok = tokens[:, 0]

    f = lax.axis_index("fsdp")
    here = (jnp.arange(16) == f)[:, None]

    def placed(gain):
        return jnp.where(here, gain[None], jnp.zeros((), BF)).reshape(-1)

    zero = jnp.zeros((64,), BF)
    odd = f % 2 == 1

    def halved(gain):
        return jnp.concatenate([jnp.where(odd, zero, gain), jnp.where(odd, gain, zero)])

    small = jnp.concatenate(
        [
            halved(gain_attn),
            halved(gain_ffn),
            placed(query_norm_gain),
            placed(key_norm_gain),
            jnp.zeros((12 * HEAD,), BF),
        ]
    ).reshape(16, HEAD)
    count = jnp.sum((segment_ids[:, 0] == 1).astype(jnp.int32), axis=1, keepdims=True)
    other = lax.ppermute(count, "fsdp", [(i, i ^ 1) for i in range(16)])
    first = jnp.where(ctx % 2 == f % 2, count, other)
    logical, seg = token_places(block_table, first, 1024)
    start = jnp.where(seg == 2, 512 + first, 0)
    lq, sq = logical[:, None, :], start[:, None, :]
    frequency = rope_frequency()

    vm = pltpu.VMEM
    saves = [
        ((2, 1024, width), BF),
        ((2, 1024, 384), F32),
        ((2, 2, 1024, HEAD), BF),
        ((2, 1024, HEAD), BF),
        ((2, 1024, HEAD), BF),
        ((2, 256, 1024), BF),
        ((2, 2, 1, 1024), F32),
    ]
    sequence = vm((2, 8, 128, width), BF)
    shared = [
        vm((2, 8, 2, 32, 512), BF),
        vm((2, 8, 16, width), BF),
        vm((2, 1024, HEAD), F32),
        vm((2, 1024, HEAD), F32),
        vm((2, 1024, HEAD), jnp.int32),
    ]
    cos, sin, lk, attended, normed, gain_rows, wqkv, wo, cots, wgu, wds, _, *saved = comm_call(
        front_body,
        RING_Z + RING_X + RING_Y + WEIGHT_PLANE,
        [
            ((2, 1024, HEAD), F32),
            ((2, 1024, HEAD), F32),
            ((2, 1024, HEAD), jnp.int32),
            ((2, 128, width), F32),
            ((2, 128, width), BF),
            ((8, width), F32),
            ((2, 8, 2, 32, 512), BF),
            ((2, 8, 16, width), BF),
            ((2, 8, 128, width), BF),
            ((2, 8, 2, 32, 768), BF),
            ((2, 192, width), BF),
            ((8, 16, width), BF),
        ]
        + saves,
        [vm(shape, kind) for shape, kind in saves]
        + [sequence, sequence, vm((1024, 256), BF), vm((HEAD, 1024), BF)]
        + [vm((2, 32, 512), BF), vm((16, 16, HEAD), BF), vm((8, 64, 768), BF)]
        + [vm((2, 128, width), BF), vm((2, 128, width), BF)]
        + reduce_ring_scratch(width) * 2
        + shared,
        0,
        [True] + [False] * 6 + [True] * 2 + [False] + [None] * 2 + [True] * 3,
        [False] * 3 + [True] * 3 + [False] * 13,
        160,
        64,
        front_first,
    )(
        tok, cotangent[:, 0], small, w_query, key_projection, value_projection,
        w_out.reshape(8, 16, width), w_gate, w_up, w_down, block_table, first, frequency, lq, sq,
    )
    g_attended, g_attn, gain_sum, dg, dd, out_part = comm_call(
        feed_body,
        RING_X,
        [
            ((2, 128, width), F32),
            ((2, 128, width), BF),
            ((8, width), F32),
            ((2, 4, 2, 64, 768), BF),
            ((2, 2, 4, 192, 128), BF),
            ((2, 8, 128, width), BF),
        ],
        [sequence, vm((2, 1024, 384), BF), vm((2, 1024, 768), BF), sequence, sequence]
        + [vm((1024, 768), F32), vm((384, width), F32), vm((2, 128, width), F32)]
        + [sequence, vm((2, 8, 2, 32, 768), BF), vm((2, 192, width), BF)]
        + reduce_ring_scratch(width) * 2,
        1,
        [True] * 3 + [False] * 3 + [True],
        [True] * 5 + [False],
        64,
        12,
    )(normed, attended, cotangent[:, 0], cots, wgu, wds, gain_rows)
    in_sum, out_sum, gain_total, *weights = comm_call(
        back_body,
        RING_Z + RING_X + RING_Y + [{"yl": 1}] + SAMPLE_SHIFTS + CHIP_SHIFTS + TP_SHIFTS + COPY_SHIFTS,
        [
            ((2, 128, width), BF),
            ((2, 128, width), F32),
            ((24, HEAD), F32),
            ((64, 2048), BF),
            ((64, 1024), BF),
            ((64, 1024), BF),
            ((128, width), BF),
            ((64, 3072), BF),
            ((64, 3072), BF),
            ((192, width), BF),
        ],
        [vm(shape, kind) for shape, kind in saves]
        + [sequence, sequence, sequence, vm((2, 1024, 512), BF)]
        + [vm((1024, 512), F32), vm((256, 1024), F32), vm((HEAD, 1024), BF)]
        + [vm((1024, HEAD), F32), vm((1024, HEAD), F32), vm((2, 1024, HEAD), F32)]
        + [vm((2, 128, width), BF), vm((8, HEAD), F32)]
        + [vm((16, 64, 512), BF), vm((2, 8, 32, 512), BF)]
        + [vm((16, 64, 512), BF), vm((16, 32, 512), BF)]
        + [vm((64, 512), BF), vm((32, 512), BF)]
        + [vm((8, 64, 512), BF), vm((8, 32, 512), BF), vm((8, 32, 512), BF), vm((8, 64, 768), BF)]
        + [vm((8, 64, 768), BF), vm((8, 64, 512), BF), vm((8, 32, 512), BF), vm((8, 192, 128), BF)]
        + [vm((24, HEAD), F32), vm((7, 24, HEAD), F32), vm((24, HEAD), F32), vm((15, 24, HEAD), F32)]
        + reduce_ff_scratch()
        + reduce_ring_scratch(width) * 4
        + [vm((2, 4, 2, 64, 768), BF), vm((2, 2, 4, 192, 128), BF)]
        + shared,
        2,
        [True] * 3 + [False] * 12 + [True] + [False] * 3 + [True] * 2,
        [True] * 10,
        224,
        56,
    )(g_attn, tok, gain_sum, dg, dd, out_part, *saved, wqkv, wo, gain_rows, cos, sin, lk, lq, sq)
    output = (attended + out_sum).astype(BF)
    g_in = in_sum.astype(F32)
    x_own = tok.astype(F32)
    r1 = norm_scale(x_own)
    n1 = g_in * gain_rows[0]
    grad_tokens = (
        g_attended
        + r1 * n1
        - x_own * (r1 * r1 * r1) * jnp.mean(n1 * x_own, axis=-1, keepdims=True)
    )
    grad_w_query, grad_w_key, grad_w_value, grad_w_out, grad_w_gate, grad_w_up, grad_w_down = (
        w.astype(F32) for w in weights
    )

    def mine(rows, n):
        return lax.dynamic_slice_in_dim(rows.reshape(-1), f * n, n)

    gains = [
        mine(gain_total[0:8], 64),
        mine(gain_total[8:16], 64),
        mine(gain_total[16], 8),
        mine(gain_total[17], 8),
    ]
    return (
        output.reshape(2, 1, 128, width),
        grad_tokens.reshape(2, 1, 128, width),
        gains[0],
        grad_w_query,
        grad_w_key,
        grad_w_value,
        gains[2],
        gains[3],
        grad_w_out,
        gains[1],
        grad_w_gate,
        grad_w_up,
        grad_w_down,
    )


def solution(mesh):
    placed = (
        P(None, "fsdp", "ctx", None),
        P(None, "fsdp", "ctx", None),
        P(),
        P(None, "fsdp", None),
        P(None, "fsdp", "ctx"),
        P("fsdp"),
        P("fsdp", None),
        P("fsdp", None),
        P("fsdp", None),
        P("fsdp"),
        P("fsdp"),
        P("fsdp", None),
        P("fsdp"),
        P("fsdp", None),
        P("fsdp", None),
        P("fsdp", None),
    )
    return jax.shard_map(
        per_device,
        mesh=mesh,
        in_specs=placed,
        out_specs=(
            P(None, "fsdp", "ctx", None),
            P(None, "fsdp", "ctx", None),
            P("fsdp"),
            P("fsdp", None),
            P("fsdp", None),
            P("fsdp", None),
            P("fsdp"),
            P("fsdp"),
            P("fsdp", None),
            P("fsdp"),
            P("fsdp", None),
            P("fsdp", None),
            P("fsdp", None),
        ),
        check_vma=False,
    )
```
